512 devices in a mesh: tile: 256 (over x_lo, y, z, core), cores: 2 (over x_hi).
Axes of the slice: x: 4 (x_hi: 2, x_lo: 2; x = x_hi * 2 + x_lo), y: 4, z: 16, core: 2. Of those that a mesh axis runs over, the one named last changes fastest.
Arguments:
- state: float32 [256, 256, 256], P('tile', 'cores'), may hold values from -6 to 6
- increment: float32 [256, 256, 256], P('tile', 'cores'), may hold values from -4 to 4
- diffusivity: float32 [256, 256, 256], P('tile', 'cores'), may hold values from 0.03 to 0.24
- land_sea: int32 [256, 256], P('tile', 'cores'), may hold values 0 or 1
- w_in: float32 [1024, 256], P('tile'), may hold values from -0.375 to 0.375
- w_mid: bfloat16 [1024, 1024], P('tile'), may hold values from -0.2625 to 0.2625
- w_out: float32 [1024, 256], P('tile'), may hold values from -0.1875 to 0.1875
- obs_col: int32 [32768], P(('tile', 'cores')), may hold values from 0 to 127
- obs_lev: int32 [32768], P(('tile', 'cores')), may hold values from 0 to 255
- obs_val: float32 [32768], P(('tile', 'cores')), may hold values from -6 to 6
- obs_prec: float32 [32768], P(('tile', 'cores')), may hold values from 0.5 to 6
Outputs:
- adjoint: float32 [256, 256, 256], P('tile', 'cores')
- w_in_new: float32 [1024, 256], P('tile')
- w_out_new: float32 [1024, 256], P('tile')
The draws below stay inside these ranges and needn't reach their ends.
All inputs are finite; a program needn't handle non-finite values. No bound on the sum of `land_sea` on one device may be relied on, other than what follows from the above.
Results may differ from the reference program's by a relative error of at most 0.015.
Values may be sent and summed in bfloat16 or wider, within the bound.
No kernel may reach another device: no remote copies, remote signals or barrier semaphores. Data moves between devices by JAX's collectives and lax.ppermute only.
A program may use at most 64 MiB of HBM per device.

```python
import math
import jax
import jax.numpy as jnp
from jax import lax

F = 256
H = 1024
LAT_DEV = 1
LON_DEV = 128
NOBS = 64
NLAT = 256
NLON = 256
OBS_TOTAL = 32768
N_CORES = 2


def draw_w_mid(key, part):
    key = jax.random.fold_in(key, 11)
    key_base, key_spread = jax.random.split(key)
    rising = 0.5 + jnp.arange(H, dtype=jnp.float32)[:, None] / H
    spread = jax.random.uniform(key_spread, (H, 1), jnp.float32, 0.7, 1.4)
    base = jnp.clip(jax.random.normal(key_base, (H, H), jnp.float32), -4.0, 4.0)
    return (base * rising * spread * H ** (-0.5)).astype(jnp.bfloat16)


def draw_obs_prec(key, part):
    key = jax.random.fold_in(key, 23)
    rising = 1.0 + 2.0 * jnp.arange(OBS_TOTAL, dtype=jnp.float32) / OBS_TOTAL
    base = jnp.exp(jax.random.uniform(key, (OBS_TOTAL,), jnp.float32, -0.6931472, 0.6931472))
    return base * rising


def touch_ends(result, rng, smallest, high):
    longest = result.shape.index(max(result.shape))
    spots = []
    for shift in (0, 1):
        where = [jax.random.randint(jax.random.fold_in(rng, axis), (), 0, length) for axis, length in enumerate(result.shape)]
        where[longest] = (where[longest] + shift) % result.shape[longest]
        spots.append(tuple(where))
    return result.at[spots[0]].set(smallest).at[spots[1]].set(high)


def levels(rng, dims, cuts, low, largest):
    level, own = 1.0, jax.random.fold_in(rng, 6)
    for dim, parts in cuts:
        heights = jnp.exp(jax.random.uniform(jax.random.fold_in(own, dim), (parts,), jnp.float32, low / len(cuts), largest / len(cuts)))
        level = level * jnp.repeat(heights, dims[dim] // parts).reshape([-1 if axis == dim else 1 for axis in range(len(dims))])
    return level


def scatter_about(stream_key, extent, scale, limit, cuts=(), kind=jnp.bfloat16):
    array = scale * jax.random.normal(stream_key, extent, jnp.float32)
    if cuts:
        array = array * levels(stream_key, extent, cuts, -0.22, 0.18)
    return jnp.clip(array, -limit, limit).astype(kind)


def setup_inputs(seed: int = 0) -> dict:
    streams_of = jax.random.split(jax.random.key(seed), 12)
    return {
        "state": scatter_about(streams_of[0], (NLAT, NLON, F), 1.0, 6.0, ((0, 256), (1, 2)), jnp.float32),
        "increment": scatter_about(streams_of[1], (NLAT, NLON, F), 0.5, 4.0, ((0, 256), (1, 2)), jnp.float32),
        "diffusivity": jnp.clip(jnp.exp(math.log(0.24) - 2.0794415 * jax.random.uniform(streams_of[2], (NLAT, NLON, F), jnp.float32) ** levels(streams_of[2], (NLAT, NLON, F), ((0, 256), (1, 2)), -0.2, 0.2)), 0.03, 0.24),
        "land_sea": touch_ends((jax.random.randint(streams_of[3], (NLAT, NLON), 0, 10) < 3).astype(jnp.int32), jax.random.fold_in(streams_of[3], 1), 0, 1),
        "w_in": scatter_about(streams_of[4], (H, F), F ** -0.5, 0.375, ((0, 256),), jnp.float32),
        "w_mid": draw_w_mid(jax.random.fold_in(streams_of[11], 71), 0),
        "w_out": scatter_about(streams_of[6], (H, F), H ** -0.5, 0.1875, ((0, 256),), jnp.float32),
        "obs_col": touch_ends(jax.random.randint(streams_of[7], (OBS_TOTAL,), 0, LAT_DEV * LON_DEV), jax.random.fold_in(streams_of[7], 1), 0, (LAT_DEV * LON_DEV) - 1).astype(jnp.int32),
        "obs_lev": touch_ends(jax.random.randint(streams_of[8], (OBS_TOTAL,), 0, F), jax.random.fold_in(streams_of[8], 1), 0, F - 1).astype(jnp.int32),
        "obs_val": scatter_about(streams_of[9], (OBS_TOTAL,), 1.0, 6.0, ((0, 512),), jnp.float32),
        "obs_prec": draw_obs_prec(jax.random.fold_in(streams_of[11], 71), 0),
    }


LEARN_RATE = 0.02
EPSILON = 1e-06
CONTRACT_LAST = (((1,), (1,)), ((), ()))
CONTRACT_FIRST = (((0,), (0,)), ((), ()))

def laplace(values):
    north_rows = jnp.concatenate([values[1:], jnp.zeros_like(values[:1])], axis=0)
    south_rows = jnp.concatenate([jnp.zeros_like(values[:1]), values[:-1]], axis=0)
    east_cols = jnp.roll(values, -1, axis=1)
    west_cols = jnp.roll(values, 1, axis=1)
    return north_rows + south_rows + east_cols + west_cols - 4.0 * values

def column_net(states, w_in_b, w_mid, w_out_b):
    states_b = states.astype(jnp.bfloat16)
    hidden_one = jnp.tanh(lax.dot_general(states_b, w_in_b, CONTRACT_LAST, preferred_element_type=jnp.float32)).astype(jnp.bfloat16)
    hidden_two = jnp.tanh(jnp.dot(hidden_one, w_mid, preferred_element_type=jnp.float32)).astype(jnp.bfloat16)
    output = jnp.dot(hidden_two, w_out_b, preferred_element_type=jnp.float32)
    return (states_b, hidden_one, hidden_two, output)

def reference(state, increment, diffusivity, land_sea, w_in, w_mid, w_out, obs_col, obs_lev, obs_val, obs_prec):
    cell_count = NLAT * NLON
    w_in_b = w_in.astype(jnp.bfloat16)
    w_out_b = w_out.astype(jnp.bfloat16)
    gating = (0.5 + land_sea.astype(jnp.float32)).reshape(cell_count, 1)
    current = state
    increment_now = increment
    trajectory = [state]
    for section_index in range(2):
        states_b, hidden_one, hidden_two, output = column_net(current.reshape(cell_count, F), w_in_b, w_mid, w_out_b)
        slope_one = 1.0 - jnp.square(hidden_one.astype(jnp.float32))
        slope_two = 1.0 - jnp.square(hidden_two.astype(jnp.float32))
        tangent_b = increment_now.reshape(cell_count, F).astype(jnp.bfloat16)
        tangent_one = (slope_one * lax.dot_general(tangent_b, w_in_b, CONTRACT_LAST, preferred_element_type=jnp.float32)).astype(jnp.bfloat16)
        tangent_two = (slope_two * jnp.dot(tangent_one, w_mid, preferred_element_type=jnp.float32)).astype(jnp.bfloat16)
        tangent_out = jnp.dot(tangent_two, w_out_b, preferred_element_type=jnp.float32)
        current_next = current + diffusivity * laplace(current) + (gating * output).reshape(state.shape)
        increment_now = increment_now + diffusivity * laplace(increment_now) + (gating * tangent_out).reshape(state.shape)
        current = current_next
        trajectory.append(current)
    obs_order = jnp.arange(OBS_TOTAL, dtype=jnp.int32)
    device = obs_order // NOBS
    lat_index = device // N_CORES * LAT_DEV + obs_col // LON_DEV
    lon_index = device % N_CORES * LON_DEV + obs_col % LON_DEV
    final_state = current + increment_now
    modelled = final_state[lat_index, lon_index, obs_lev]
    weighted = obs_prec * (modelled - obs_val)
    adjoint = jnp.zeros_like(state).at[lat_index, lon_index, obs_lev].add(weighted)
    grad_in = jnp.zeros((H, F), jnp.float32)
    grad_out = jnp.zeros((H, F), jnp.float32)
    for section_index in (1, 0):
        states_b, hidden_one, hidden_two, output = column_net(trajectory[section_index].reshape(cell_count, F), w_in_b, w_mid, w_out_b)
        slope_one = 1.0 - jnp.square(hidden_one.astype(jnp.float32))
        slope_two = 1.0 - jnp.square(hidden_two.astype(jnp.float32))
        source = (gating * adjoint.reshape(cell_count, F)).astype(jnp.bfloat16)
        back_two = (slope_two * lax.dot_general(source, w_out_b, CONTRACT_LAST, preferred_element_type=jnp.float32)).astype(jnp.bfloat16)
        back_one = (slope_one * lax.dot_general(back_two, w_mid, CONTRACT_LAST, preferred_element_type=jnp.float32)).astype(jnp.bfloat16)
        grad_out = grad_out + lax.dot_general(hidden_two, source, CONTRACT_FIRST, preferred_element_type=jnp.float32)
        grad_in = grad_in + lax.dot_general(back_one, states_b, CONTRACT_FIRST, preferred_element_type=jnp.float32)
        adjoint = adjoint + laplace(diffusivity * adjoint) + jnp.dot(back_one, w_in_b, preferred_element_type=jnp.float32).reshape(state.shape)
    square_sum = jnp.sum(grad_in * grad_in) + jnp.sum(grad_out * grad_out)
    scale = LEARN_RATE / jnp.sqrt(square_sum / (2.0 * H * F) + EPSILON)
    return (adjoint, w_in - scale * grad_in, w_out - scale * grad_out)
```

```python
import jax
import jax.numpy as jnp
from jax import lax
from jax.sharding import Mesh
from jax.sharding import PartitionSpec as P

LEARN_RATE = 0.02
EPSILON = 1e-06
CONTRACT_LAST = (((1,), (1,)), ((), ()))
CONTRACT_FIRST = (((0,), (0,)), ((), ()))
FINE_AXES = ("x_lo", "y", "z", "core", "x_hi")
FINE_SIZES = (2, 4, 16, 2, 2)
TILE = ("x_lo", "y", "z", "core")


def spread(block, axis):
    count = lax.axis_size(axis)
    return lax.all_to_all(jnp.broadcast_to(block[None], (count,) + block.shape), axis, 0, 0)


def gather_weights(w_in, w_mid, w_out):
    rows = jnp.concatenate(
        [w_in.astype(jnp.bfloat16), w_mid, w_out.astype(jnp.bfloat16)], axis=1
    )
    rows = lax.all_gather(rows, "core", axis=0, tiled=True)
    width = rows.shape[1] // 2
    half = lax.dynamic_slice_in_dim(rows, lax.axis_index("core") * width, width, 1)
    half = spread(half, "z").reshape(-1, width)
    half = spread(half, ("x_lo", "y")).reshape(-1, width)
    both = spread(half, "core")
    features = w_in.shape[1]
    w_in_all = both[0, :, :features]
    w_mid_all = jnp.concatenate([both[0, :, features:], both[1, :, :-features]], axis=1)
    return w_in_all, w_mid_all, both[1, :, -features:]


def halo(field):
    count = 1
    for axis in TILE:
        count *= lax.axis_size(axis)
    pairs = []
    for row in range(1, count - 1, 2):
        pairs += [(row, row + 1), (row + 1, row)]
    far = lax.ppermute(field, TILE, pairs)
    edges = jnp.concatenate([field[:, :1], field[:, -1:]], axis=1)
    edges = lax.ppermute(edges, "x_hi", [(0, 1), (1, 0)])
    near = lax.ppermute(field, "core", [(0, 1), (1, 0)])
    east = jnp.concatenate([field[:, 1:], edges[:, :1]], axis=1)
    west = jnp.concatenate([edges[:, 1:], field[:, :-1]], axis=1)
    return far + near + east + west


def reduce_gradients(grad_in, grad_out):
    rows, features = grad_in.shape
    part = features // 2
    grads = jnp.stack([grad_in, grad_out]).reshape(2, rows, 2, part)
    me = lax.axis_index("core")
    mine = lax.dynamic_index_in_dim(grads, me, 2, keepdims=False)
    other = lax.dynamic_index_in_dim(grads, 1 - me, 2, keepdims=False)
    got = lax.ppermute(other.astype(jnp.bfloat16), "core", [(0, 1), (1, 0)])
    total = mine + got.astype(jnp.float32)
    peers = lax.axis_size(("x_hi", "x_lo", "y"))
    total = total.reshape(peers, rows * 2 // peers, part).astype(jnp.bfloat16)
    total = lax.all_to_all(total, ("x_hi", "x_lo", "y"), 0, 0)
    total = jnp.sum(total.astype(jnp.float32), axis=0)
    depth = lax.axis_size("z")
    total = total.reshape(depth, 1, -1, part)
    total = jnp.broadcast_to(total, (depth, 2) + total.shape[2:])
    total = lax.all_to_all(
        total.reshape((2 * depth,) + total.shape[2:]), ("z", "x_hi"), 0, 0
    ).reshape(total.shape)
    total = jnp.sum(total, axis=0)
    both = lax.all_gather(total, "core", axis=2, tiled=True)
    square = jnp.broadcast_to(jnp.sum(both * both), (1, 128))
    square = jnp.sum(spread(square, "z"), axis=0)
    square = jnp.sum(spread(square, ("x_lo", "y")), axis=0)[0, 0]
    shard = both.shape[1] // 2
    own = lax.dynamic_slice_in_dim(both, me * shard, shard, 1)
    return own[0], own[1], square


def local(
    state, increment, diffusivity, land_sea, w_in, w_mid, w_out, obs_col, obs_lev, obs_val, obs_prec
):
    _, cells, features = state.shape
    current, increment_now, diffusivity = state[0], increment[0], diffusivity[0]
    pair_sum = halo(jnp.stack([current, increment_now]))
    w_in_b, w_mid_all, w_out_b = gather_weights(w_in, w_mid, w_out)
    hidden_units = w_in_b.shape[0]
    gating = (0.5 + land_sea.astype(jnp.float32)).reshape(cells, 1)
    saved = []

    def network(current, increment_now):
        states_b = current.astype(jnp.bfloat16)
        stacked = jnp.concatenate([states_b, increment_now.astype(jnp.bfloat16)])
        one = lax.dot_general(stacked, w_in_b, CONTRACT_LAST, preferred_element_type=jnp.float32)
        hidden_one = jnp.tanh(one[:cells]).astype(jnp.bfloat16)
        slope_one = 1.0 - jnp.square(hidden_one.astype(jnp.float32))
        tangent_one = (slope_one * one[cells:]).astype(jnp.bfloat16)
        two = jnp.dot(
            jnp.concatenate([hidden_one, tangent_one]),
            w_mid_all,
            preferred_element_type=jnp.float32,
        )
        hidden_two = jnp.tanh(two[:cells]).astype(jnp.bfloat16)
        slope_two = 1.0 - jnp.square(hidden_two.astype(jnp.float32))
        tangent_two = (slope_two * two[cells:]).astype(jnp.bfloat16)
        out = jnp.dot(
            jnp.concatenate([hidden_two, tangent_two]),
            w_out_b,
            preferred_element_type=jnp.float32,
        )
        saved.append((states_b, hidden_two, slope_one, slope_two))
        return gating * out[:cells], gating * out[cells:]

    tend, tangent = network(current, increment_now)
    current = current + diffusivity * (pair_sum[0] - 4.0 * current) + tend
    increment_now = increment_now + diffusivity * (pair_sum[1] - 4.0 * increment_now) + tangent
    final = current + increment_now
    final_sum = halo(final[None])[0]
    tend, tangent = network(current, increment_now)
    final = final + diffusivity * (final_sum - 4.0 * final) + (tend + tangent)

    cell_ids = jnp.arange(cells, dtype=jnp.int32)
    level_ids = jnp.arange(features, dtype=jnp.int32)
    pick_cell = (obs_col[:, None] == cell_ids[None, :]).astype(jnp.float32)
    pick_level = (obs_lev[:, None] == level_ids[None, :]).astype(jnp.float32)
    modelled = jnp.sum(
        jnp.dot(pick_cell, final, precision=lax.Precision.HIGHEST) * pick_level, axis=1
    )
    weighted = obs_prec * (modelled - obs_val)
    adjoint = lax.dot_general(
        pick_cell, weighted[:, None] * pick_level, CONTRACT_FIRST, precision=lax.Precision.HIGHEST
    )
    grad_in = jnp.zeros((hidden_units, features), jnp.float32)
    grad_out = jnp.zeros((hidden_units, features), jnp.float32)
    for section_index in (1, 0):
        states_b, hidden_two, slope_one, slope_two = saved[section_index]
        spreading = diffusivity * adjoint
        spread_sum = halo(spreading[None])[0]
        source = (gating * adjoint).astype(jnp.bfloat16)
        back_two = (
            slope_two
            * lax.dot_general(source, w_out_b, CONTRACT_LAST, preferred_element_type=jnp.float32)
        ).astype(jnp.bfloat16)
        back_one = (
            slope_one
            * lax.dot_general(
                back_two, w_mid_all, CONTRACT_LAST, preferred_element_type=jnp.float32
            )
        ).astype(jnp.bfloat16)
        grad_out = grad_out + lax.dot_general(
            hidden_two, source, CONTRACT_FIRST, preferred_element_type=jnp.float32
        )
        grad_in = grad_in + lax.dot_general(
            back_one, states_b, CONTRACT_FIRST, preferred_element_type=jnp.float32
        )
        adjoint = (
            adjoint
            + (spread_sum - 4.0 * spreading)
            + jnp.dot(back_one, w_in_b, preferred_element_type=jnp.float32)
        )
    share_in, share_out, square_sum = reduce_gradients(grad_in, grad_out)
    scale = LEARN_RATE / jnp.sqrt(square_sum / (2.0 * hidden_units * features) + EPSILON)
    return (adjoint[None], w_in - scale * share_in, w_out - scale * share_out)


def solution(mesh):
    fine = Mesh(mesh.devices.reshape(FINE_SIZES), FINE_AXES)
    everywhere = TILE + ("x_hi",)
    return jax.shard_map(
        local,
        mesh=fine,
        in_specs=(
            P(TILE, "x_hi", None),
            P(TILE, "x_hi", None),
            P(TILE, "x_hi", None),
            P(TILE, "x_hi"),
            P(TILE, None),
            P(TILE, None),
            P(TILE, None),
            P(everywhere),
            P(everywhere),
            P(everywhere),
            P(everywhere),
        ),
        out_specs=(P(TILE, "x_hi", None), P(TILE, None), P(TILE, None)),
        check_vma=False,
    )
```

```python
import jax
import jax.numpy as jnp
from jax import lax
from jax.experimental import pallas as pl
from jax.experimental.pallas import tpu as pltpu
from jax.sharding import Mesh
from jax.sharding import PartitionSpec as P

LEARN_RATE = 0.02
EPSILON = 1e-06
CONTRACT_LAST = (((1,), (1,)), ((), ()))
CONTRACT_FIRST = (((0,), (0,)), ((), ()))
FINE_AXES = ("x_lo", "y", "z", "core", "x_hi")
FINE_SIZES = (2, 4, 16, 2, 2)
TILE = ("x_lo", "y", "z", "core")


def spread(block, axis):
    count = lax.axis_size(axis)
    return lax.all_to_all(jnp.broadcast_to(block[None], (count,) + block.shape), axis, 0, 0)


def gather_weights(w_in, w_mid, w_out):
    rows = jnp.concatenate(
        [w_in.astype(jnp.bfloat16), w_mid, w_out.astype(jnp.bfloat16)], axis=1
    )
    rows = lax.all_gather(rows, "core", axis=0, tiled=True)
    width = rows.shape[1] // 2
    half = lax.dynamic_slice_in_dim(rows, lax.axis_index("core") * width, width, 1)
    half = spread(half, "z").reshape(-1, width)
    half = spread(half, ("x_lo", "y")).reshape(-1, width)
    both = spread(half, "core")
    features = w_in.shape[1]
    w_in_all = both[0, :, :features]
    w_mid_all = jnp.concatenate([both[0, :, features:], both[1, :, :-features]], axis=1)
    return both, w_in_all, w_mid_all, both[1, :, -features:]


def halo(field):
    count = 1
    for axis in TILE:
        count *= lax.axis_size(axis)
    pairs = []
    for row in range(1, count - 1, 2):
        pairs += [(row, row + 1), (row + 1, row)]
    far = lax.ppermute(field, TILE, pairs)
    edges = jnp.concatenate([field[:, :1], field[:, -1:]], axis=1)
    edges = lax.ppermute(edges, "x_hi", [(0, 1), (1, 0)])
    near = lax.ppermute(field, "core", [(0, 1), (1, 0)])
    east = jnp.concatenate([field[:, 1:], edges[:, :1]], axis=1)
    west = jnp.concatenate([edges[:, 1:], field[:, :-1]], axis=1)
    return far + near + east + west


def adjoint_layers(source, hidden_one, hidden_two, weights):
    features = source.shape[1]
    depth = weights.shape[2] - features
    slope_two = 1.0 - jnp.square(hidden_two.astype(jnp.float32))
    back_two = lax.dot_general(
        source, weights[1, :, depth:], CONTRACT_LAST, preferred_element_type=jnp.float32
    )
    back_two = (slope_two * back_two).astype(jnp.bfloat16)
    back_one = lax.dot_general(
        back_two[:, :depth],
        weights[0, :, features:],
        CONTRACT_LAST,
        preferred_element_type=jnp.float32,
    ) + lax.dot_general(
        back_two[:, depth:],
        weights[1, :, :depth],
        CONTRACT_LAST,
        preferred_element_type=jnp.float32,
    )
    slope_one = 1.0 - jnp.square(hidden_one.astype(jnp.float32))
    return (slope_one * back_one).astype(jnp.bfloat16)


def last_step_kernel(adjoint, gating, hidden_one, hidden_two, weights, source_out, one_out, back):
    source = (gating[...] * adjoint[...]).astype(jnp.bfloat16)
    source_out[...] = source
    back_one = adjoint_layers(source, hidden_one[...], hidden_two[...], weights)
    one_out[...] = back_one
    back[...] = jnp.dot(
        back_one, weights[0, :, : source.shape[1]], preferred_element_type=jnp.float32
    )


def first_step_kernel(
    adjoint,
    gating,
    hidden_one,
    hidden_two,
    states,
    source_late,
    one_late,
    hidden_late,
    states_late,
    weights,
    one_out,
    grads,
):
    source = (gating[...] * adjoint[...]).astype(jnp.bfloat16)
    back_one = adjoint_layers(source, hidden_one[...], hidden_two[...], weights)
    one_out[...] = back_one
    pairs = (
        (one_late[...], back_one, states_late[...], states[...]),
        (hidden_late[...], hidden_two[...], source_late[...], source),
    )
    _, blocks, halves, rows, columns = grads.shape
    for which, (left_late, left, right_late, right) in enumerate(pairs):
        total = lax.dot_general(
            jnp.concatenate([left_late, left]),
            jnp.concatenate([right_late, right]),
            CONTRACT_FIRST,
            preferred_element_type=jnp.float32,
        ).astype(jnp.bfloat16)
        for block in range(blocks):
            for half in range(halves):
                grads[which, block, half] = total[
                    block * rows : (block + 1) * rows, half * columns : (half + 1) * columns
                ]


def on_chip(kernel, outs, operands, flops):
    size = sum(array.size * array.dtype.itemsize for array in list(operands) + list(outs))
    return pl.pallas_call(
        kernel,
        out_shape=outs,
        in_specs=[pl.BlockSpec(memory_space=pltpu.VMEM)] * len(operands),
        out_specs=[pl.BlockSpec(memory_space=pltpu.VMEM)] * len(outs),
        compiler_params=pltpu.CompilerParams(vmem_limit_bytes=24 * 1024 * 1024),
        cost_estimate=pl.CostEstimate(flops=flops, bytes_accessed=size, transcendentals=0),
    )(*operands)


def reduce_gradients(grads):
    kinds, blocks, halves, rows, columns = grads.shape
    around = ("x_hi", "x_lo", "y", "core")
    grads = grads.reshape(kinds * blocks * halves, rows, columns)
    grads = lax.all_to_all(grads, around, 0, 0)
    grads = jnp.sum(grads.astype(jnp.float32), axis=0).astype(jnp.bfloat16)
    grads = jnp.sum(spread(grads, "z").astype(jnp.float32), axis=0)
    square = jnp.broadcast_to(jnp.sum(grads * grads), (8, columns))
    depth = rows // lax.axis_size("z")
    own = lax.dynamic_slice_in_dim(grads, lax.axis_index("z") * depth, depth, 0)
    parts = spread(jnp.concatenate([own, square]), around)
    square = jnp.sum(parts[:, depth, 0])
    parts = parts.reshape(kinds, blocks, halves, depth + 8, columns)
    block = lax.axis_index(("x_lo", "y"))
    parts = lax.dynamic_index_in_dim(parts, block, 1, keepdims=False)
    shard = depth // halves
    parts = lax.dynamic_slice_in_dim(parts, lax.axis_index("core") * shard, shard, 2)
    parts = jnp.concatenate([parts[:, 0], parts[:, 1]], axis=2)
    return parts[0], parts[1], square


def local(
    state, increment, diffusivity, land_sea, w_in, w_mid, w_out, obs_col, obs_lev, obs_val, obs_prec
):
    _, cells, features = state.shape
    current, increment_now, diffusivity = state[0], increment[0], diffusivity[0]
    pair_sum = halo(jnp.stack([current, increment_now]))
    weights, w_in_b, w_mid_all, w_out_b = gather_weights(w_in, w_mid, w_out)
    hidden_units = w_in_b.shape[0]
    gating = (0.5 + land_sea.astype(jnp.float32)).reshape(cells, 1)
    saved = []

    def network(current, increment_now):
        states_b = current.astype(jnp.bfloat16)
        stacked = jnp.concatenate([states_b, increment_now.astype(jnp.bfloat16)])
        one = lax.dot_general(stacked, w_in_b, CONTRACT_LAST, preferred_element_type=jnp.float32)
        hidden_one = jnp.tanh(one[:cells]).astype(jnp.bfloat16)
        slope_one = 1.0 - jnp.square(hidden_one.astype(jnp.float32))
        tangent_one = (slope_one * one[cells:]).astype(jnp.bfloat16)
        two = jnp.dot(
            jnp.concatenate([hidden_one, tangent_one]),
            w_mid_all,
            preferred_element_type=jnp.float32,
        )
        hidden_two = jnp.tanh(two[:cells]).astype(jnp.bfloat16)
        slope_two = 1.0 - jnp.square(hidden_two.astype(jnp.float32))
        tangent_two = (slope_two * two[cells:]).astype(jnp.bfloat16)
        out = jnp.dot(
            jnp.concatenate([hidden_two, tangent_two]),
            w_out_b,
            preferred_element_type=jnp.float32,
        )
        saved.append((states_b, hidden_one, hidden_two))
        return gating * out[:cells], gating * out[cells:]

    tend, tangent = network(current, increment_now)
    current = current + diffusivity * (pair_sum[0] - 4.0 * current) + tend
    increment_now = increment_now + diffusivity * (pair_sum[1] - 4.0 * increment_now) + tangent
    final = current + increment_now
    final_sum = halo(final[None])[0]
    tend, tangent = network(current, increment_now)
    final = final + diffusivity * (final_sum - 4.0 * final) + (tend + tangent)

    cell_ids = jnp.arange(cells, dtype=jnp.int32)
    level_ids = jnp.arange(features, dtype=jnp.int32)
    pick_cell = (obs_col[:, None] == cell_ids[None, :]).astype(jnp.float32)
    pick_level = (obs_lev[:, None] == level_ids[None, :]).astype(jnp.float32)
    modelled = jnp.sum(
        jnp.dot(pick_cell, final, precision=lax.Precision.HIGHEST) * pick_level, axis=1
    )
    weighted = obs_prec * (modelled - obs_val)
    adjoint = lax.dot_general(
        pick_cell, weighted[:, None] * pick_level, CONTRACT_FIRST, precision=lax.Precision.HIGHEST
    )
    states_late, one_late, two_late = saved[1]
    states_b, hidden_one, hidden_two = saved[0]
    spreading = diffusivity * adjoint
    spread_sum = halo(spreading[None])[0]
    wide = jax.ShapeDtypeStruct((cells, hidden_units), jnp.bfloat16)
    narrow = jax.ShapeDtypeStruct((cells, features), jnp.float32)
    layer = 2 * cells * hidden_units
    source_late, back_late, back_sum = on_chip(
        last_step_kernel,
        (jax.ShapeDtypeStruct((cells, features), jnp.bfloat16), wide, narrow),
        (adjoint, gating, one_late, two_late, weights),
        layer * (2 * features + hidden_units),
    )
    adjoint = adjoint + (spread_sum - 4.0 * spreading) + back_sum
    blocks = lax.axis_size(("x_lo", "y"))
    halves = lax.axis_size("core")
    back_first, grads = on_chip(
        first_step_kernel,
        (
            wide,
            jax.ShapeDtypeStruct(
                (2, blocks, halves, hidden_units // blocks, features // halves), jnp.bfloat16
            ),
        ),
        (
            adjoint,
            gating,
            hidden_one,
            hidden_two,
            states_b,
            source_late,
            back_late,
            two_late,
            states_late,
            weights,
        ),
        layer * (5 * features + hidden_units),
    )
    share_in, share_out, square_sum = reduce_gradients(grads)
    spreading = diffusivity * adjoint
    adjoint = (
        adjoint
        + (halo(spreading[None])[0] - 4.0 * spreading)
        + jnp.dot(back_first, w_in_b, preferred_element_type=jnp.float32)
    )
    scale = LEARN_RATE / jnp.sqrt(square_sum / (2.0 * hidden_units * features) + EPSILON)
    return (adjoint[None], w_in - scale * share_in, w_out - scale * share_out)


def solution(mesh):
    fine = Mesh(mesh.devices.reshape(FINE_SIZES), FINE_AXES)
    everywhere = TILE + ("x_hi",)
    return jax.shard_map(
        local,
        mesh=fine,
        in_specs=(
            P(TILE, "x_hi", None),
            P(TILE, "x_hi", None),
            P(TILE, "x_hi", None),
            P(TILE, "x_hi"),
            P(TILE, None),
            P(TILE, None),
            P(TILE, None),
            P(everywhere),
            P(everywhere),
            P(everywhere),
            P(everywhere),
        ),
        out_specs=(P(TILE, "x_hi", None), P(TILE, None), P(TILE, None)),
        check_vma=False,
    )
```

```python
import functools

import jax
import jax.numpy as jnp
from jax import lax
from jax.experimental import pallas as pl
from jax.experimental.pallas import tpu as pltpu
from jax.sharding import Mesh
from jax.sharding import PartitionSpec as P

LEARN_RATE = 0.02
EPSILON = 1e-06
CONTRACT_LAST = (((1,), (1,)), ((), ()))
CONTRACT_FIRST = (((0,), (0,)), ((), ()))
FINE_AXES = ("x_lo", "y", "z_hi", "z_lo", "core", "x_hi")
FINE_SIZES = (2, 4, 4, 4, 2, 2)
Z = ("z_hi", "z_lo")
TILE = ("x_lo", "y", "z_hi", "z_lo", "core")
AROUND = ("x_hi", "x_lo", "y", "core")


def spread(block, axis):
    count = lax.axis_size(axis)
    return lax.all_to_all(jnp.broadcast_to(block[None], (count,) + block.shape), axis, 0, 0)


def gather_weights(w_in, w_mid, w_out):
    columns = 2 * w_in.shape[1] + w_mid.shape[1]
    (rows,) = on_chip(
        pack_kernel,
        (jax.ShapeDtypeStruct((w_in.shape[0], columns), jnp.bfloat16),),
        (w_in, w_mid, w_out),
        0,
    )
    rows = lax.all_gather(rows, "core", axis=0, tiled=True)
    width = rows.shape[1] // 2
    half = lax.dynamic_slice_in_dim(rows, lax.axis_index("core") * width, width, 1)
    half = spread(half, Z).reshape(-1, width)
    half = spread(half, ("x_lo", "y")).reshape(-1, width)
    both = spread(half, "core")
    features = w_in.shape[1]
    w_in_all = both[0, :, :features]
    w_mid_all = jnp.concatenate([both[0, :, features:], both[1, :, :-features]], axis=1)
    return both, w_in_all, w_mid_all, both[1, :, -features:]


def halo(field):
    count = 1
    for axis in TILE:
        count *= lax.axis_size(axis)
    pairs = []
    for row in range(1, count - 1, 2):
        pairs += [(row, row + 1), (row + 1, row)]
    far = lax.ppermute(field, TILE, pairs)
    edges = jnp.concatenate([field[:, :1], field[:, -1:]], axis=1)
    edges = lax.ppermute(edges, "x_hi", [(0, 1), (1, 0)])
    near = lax.ppermute(field, "core", [(0, 1), (1, 0)])
    east = jnp.concatenate([field[:, 1:], edges[:, :1]], axis=1)
    west = jnp.concatenate([edges[:, 1:], field[:, :-1]], axis=1)
    return far + near + east + west


def adjoint_layers(source, hidden_one, hidden_two, weights):
    features = source.shape[1]
    depth = weights.shape[2] - features
    slope_two = 1.0 - jnp.square(hidden_two.astype(jnp.float32))
    back_two = lax.dot_general(
        source, weights[1, :, depth:], CONTRACT_LAST, preferred_element_type=jnp.float32
    )
    back_two = (slope_two * back_two).astype(jnp.bfloat16)
    back_one = lax.dot_general(
        back_two[:, :depth],
        weights[0, :, features:],
        CONTRACT_LAST,
        preferred_element_type=jnp.float32,
    ) + lax.dot_general(
        back_two[:, depth:],
        weights[1, :, :depth],
        CONTRACT_LAST,
        preferred_element_type=jnp.float32,
    )
    slope_one = 1.0 - jnp.square(hidden_one.astype(jnp.float32))
    return (slope_one * back_one).astype(jnp.bfloat16)


def last_step_kernel(adjoint, gating, hidden_one, hidden_two, weights, source_out, one_out, back):
    source = (gating[...] * adjoint[...]).astype(jnp.bfloat16)
    source_out[...] = source
    back_one = adjoint_layers(source, hidden_one[...], hidden_two[...], weights)
    one_out[...] = back_one
    back[...] = jnp.dot(
        back_one, weights[0, :, : source.shape[1]], preferred_element_type=jnp.float32
    )


def first_step_kernel(
    adjoint,
    gating,
    hidden_one,
    hidden_two,
    states,
    source_late,
    one_late,
    hidden_late,
    states_late,
    weights,
    one_out,
    grads,
):
    source = (gating[...] * adjoint[...]).astype(jnp.bfloat16)
    back_one = adjoint_layers(source, hidden_one[...], hidden_two[...], weights)
    one_out[...] = back_one
    pairs = (
        (one_late[...], back_one, states_late[...], states[...]),
        (hidden_late[...], hidden_two[...], source_late[...], source),
    )
    _, blocks, halves, rows, columns = grads.shape
    for which, (left_late, left, right_late, right) in enumerate(pairs):
        total = lax.dot_general(
            jnp.concatenate([left_late, left]),
            jnp.concatenate([right_late, right]),
            CONTRACT_FIRST,
            preferred_element_type=jnp.float32,
        ).astype(jnp.bfloat16)
        for block in range(blocks):
            for half in range(halves):
                grads[which, block, half] = total[
                    block * rows : (block + 1) * rows, half * columns : (half + 1) * columns
                ]


def on_chip(kernel, outs, operands, flops, scratch=(), scalars=0):
    size = sum(array.size * array.dtype.itemsize for array in list(operands) + list(outs))
    places = [pltpu.SMEM] * scalars + [pltpu.VMEM] * (len(operands) - scalars)
    return pl.pallas_call(
        kernel,
        out_shape=outs,
        in_specs=[pl.BlockSpec(memory_space=place) for place in places],
        out_specs=[pl.BlockSpec(memory_space=pltpu.VMEM)] * len(outs),
        scratch_shapes=scratch,
        compiler_params=pltpu.CompilerParams(vmem_limit_bytes=24 * 1024 * 1024),
        cost_estimate=pl.CostEstimate(flops=flops, bytes_accessed=size, transcendentals=0),
    )(*operands)


def pack_kernel(w_in, w_mid, w_out, rows):
    features = w_in.shape[1]
    rows[:, :features] = w_in[...].astype(jnp.bfloat16)
    rows[:, features:-features] = w_mid[...]
    rows[:, -features:] = w_out[...].astype(jnp.bfloat16)


def sum_and_spread_kernel(parts, copies):
    total = jnp.sum(parts[...].astype(jnp.float32), axis=0).astype(jnp.bfloat16)
    copies[...] = jnp.broadcast_to(total[None], copies.shape)


def sum_and_square_kernel(place, parts, copies, total):
    total[...] = jnp.sum(parts[...].astype(jnp.float32), axis=0)
    depth = copies.shape[1] // 2
    own = total[pl.ds(pl.multiple_of(place[0] * depth, depth), depth), :]
    squares = jnp.sum(total[...] * total[...], axis=0, keepdims=True)
    both = jnp.concatenate([own, jnp.broadcast_to(squares, own.shape)])
    copies[...] = jnp.broadcast_to(both[None], copies.shape)


def update_kernel(blocks, count, place, parts, w_in, w_out, new_in, new_out):
    depth = parts.shape[1] // 2
    shard = w_in.shape[0]
    squares = jnp.sum(parts[:, depth, :], axis=0, keepdims=True)
    square_sum = jnp.sum(squares, axis=1, keepdims=True)
    scale = LEARN_RATE / jnp.sqrt(square_sum / count + EPSILON)
    for which, (old, new) in enumerate(((w_in, new_in), (w_out, new_out))):
        sides = []
        for half in range(2):
            rows = parts[(which * blocks + place[0]) * 2 + half, :depth, :]
            sides.append(jnp.where(place[1] == 0, rows[:shard], rows[shard:]))
        new[...] = old[...] - scale * jnp.concatenate(sides, axis=1)


def updated(grads, w_in, w_out):
    kinds, blocks, halves, rows, columns = grads.shape
    peers = kinds * blocks * halves
    grads = lax.all_to_all(grads.reshape(peers, rows, columns), AROUND, 0, 0)
    for axis in ("z_lo", "z_hi"):
        count = lax.axis_size(axis)
        (copies,) = on_chip(
            sum_and_spread_kernel,
            (jax.ShapeDtypeStruct((count, rows, columns), jnp.bfloat16),),
            (grads,),
            grads.size,
        )
        grads = lax.all_to_all(copies, axis, 0, 0)
    depth = rows // lax.axis_size(Z)
    (copies,) = on_chip(
        sum_and_square_kernel,
        (jax.ShapeDtypeStruct((peers, 2 * depth, columns), jnp.float32),),
        (lax.axis_index(Z)[None], grads),
        grads.size,
        scratch=(pltpu.VMEM((rows, columns), jnp.float32),),
        scalars=1,
    )
    parts = lax.all_to_all(copies, AROUND, 0, 0)
    place = jnp.stack([lax.axis_index(("x_lo", "y")), lax.axis_index("core")])
    shape = jax.ShapeDtypeStruct(w_in.shape, jnp.float32)
    return on_chip(
        functools.partial(update_kernel, blocks, float(peers * rows * columns)),
        (shape, shape),
        (place, parts, w_in, w_out),
        parts.size,
        scalars=1,
    )


def local(
    state, increment, diffusivity, land_sea, w_in, w_mid, w_out, obs_col, obs_lev, obs_val, obs_prec
):
    _, cells, features = state.shape
    current, increment_now, diffusivity = state[0], increment[0], diffusivity[0]
    pair_sum = halo(jnp.stack([current, increment_now]))
    weights, w_in_b, w_mid_all, w_out_b = gather_weights(w_in, w_mid, w_out)
    hidden_units = w_in_b.shape[0]
    gating = (0.5 + land_sea.astype(jnp.float32)).reshape(cells, 1)
    saved = []

    def network(current, increment_now):
        states_b = current.astype(jnp.bfloat16)
        stacked = jnp.concatenate([states_b, increment_now.astype(jnp.bfloat16)])
        one = lax.dot_general(stacked, w_in_b, CONTRACT_LAST, preferred_element_type=jnp.float32)
        hidden_one = jnp.tanh(one[:cells]).astype(jnp.bfloat16)
        slope_one = 1.0 - jnp.square(hidden_one.astype(jnp.float32))
        tangent_one = (slope_one * one[cells:]).astype(jnp.bfloat16)
        two = jnp.dot(
            jnp.concatenate([hidden_one, tangent_one]),
            w_mid_all,
            preferred_element_type=jnp.float32,
        )
        hidden_two = jnp.tanh(two[:cells]).astype(jnp.bfloat16)
        slope_two = 1.0 - jnp.square(hidden_two.astype(jnp.float32))
        tangent_two = (slope_two * two[cells:]).astype(jnp.bfloat16)
        out = jnp.dot(
            jnp.concatenate([hidden_two, tangent_two]),
            w_out_b,
            preferred_element_type=jnp.float32,
        )
        saved.append((states_b, hidden_one, hidden_two))
        return gating * out[:cells], gating * out[cells:]

    tend, tangent = network(current, increment_now)
    current = current + diffusivity * (pair_sum[0] - 4.0 * current) + tend
    increment_now = increment_now + diffusivity * (pair_sum[1] - 4.0 * increment_now) + tangent
    final = current + increment_now
    final_sum = halo(final[None])[0]
    tend, tangent = network(current, increment_now)
    final = final + diffusivity * (final_sum - 4.0 * final) + (tend + tangent)

    cell_ids = jnp.arange(cells, dtype=jnp.int32)
    level_ids = jnp.arange(features, dtype=jnp.int32)
    pick_cell = (obs_col[:, None] == cell_ids[None, :]).astype(jnp.float32)
    pick_level = (obs_lev[:, None] == level_ids[None, :]).astype(jnp.float32)
    modelled = jnp.sum(
        jnp.dot(pick_cell, final, precision=lax.Precision.HIGHEST) * pick_level, axis=1
    )
    weighted = obs_prec * (modelled - obs_val)
    adjoint = lax.dot_general(
        pick_cell, weighted[:, None] * pick_level, CONTRACT_FIRST, precision=lax.Precision.HIGHEST
    )
    states_late, one_late, two_late = saved[1]
    states_b, hidden_one, hidden_two = saved[0]
    spreading = diffusivity * adjoint
    spread_sum = halo(spreading[None])[0]
    wide = jax.ShapeDtypeStruct((cells, hidden_units), jnp.bfloat16)
    narrow = jax.ShapeDtypeStruct((cells, features), jnp.float32)
    layer = 2 * cells * hidden_units
    source_late, back_late, back_sum = on_chip(
        last_step_kernel,
        (jax.ShapeDtypeStruct((cells, features), jnp.bfloat16), wide, narrow),
        (adjoint, gating, one_late, two_late, weights),
        layer * (2 * features + hidden_units),
    )
    adjoint = adjoint + (spread_sum - 4.0 * spreading) + back_sum
    blocks = lax.axis_size(("x_lo", "y"))
    halves = lax.axis_size("core")
    back_first, grads = on_chip(
        first_step_kernel,
        (
            wide,
            jax.ShapeDtypeStruct(
                (2, blocks, halves, hidden_units // blocks, features // halves), jnp.bfloat16
            ),
        ),
        (
            adjoint,
            gating,
            hidden_one,
            hidden_two,
            states_b,
            source_late,
            back_late,
            two_late,
            states_late,
            weights,
        ),
        layer * (5 * features + hidden_units),
    )
    w_in_new, w_out_new = updated(grads, w_in, w_out)
    spreading = diffusivity * adjoint
    adjoint = (
        adjoint
        + (halo(spreading[None])[0] - 4.0 * spreading)
        + jnp.dot(back_first, w_in_b, preferred_element_type=jnp.float32)
    )
    return adjoint[None], w_in_new, w_out_new


def solution(mesh):
    fine = Mesh(mesh.devices.reshape(FINE_SIZES), FINE_AXES)
    everywhere = TILE + ("x_hi",)
    return jax.shard_map(
        local,
        mesh=fine,
        in_specs=(
            P(TILE, "x_hi", None),
            P(TILE, "x_hi", None),
            P(TILE, "x_hi", None),
            P(TILE, "x_hi"),
            P(TILE, None),
            P(TILE, None),
            P(TILE, None),
            P(everywhere),
            P(everywhere),
            P(everywhere),
            P(everywhere),
        ),
        out_specs=(P(TILE, "x_hi", None), P(TILE, None), P(TILE, None)),
        check_vma=False,
    )
```

```python
import functools

import jax
import jax.numpy as jnp
from jax import lax
from jax.experimental import pallas as pl
from jax.experimental.pallas import tpu as pltpu
from jax.sharding import Mesh
from jax.sharding import PartitionSpec as P

LEARN_RATE = 0.02
EPSILON = 1e-06
CONTRACT_LAST = (((1,), (1,)), ((), ()))
CONTRACT_FIRST = (((0,), (0,)), ((), ()))
FINE_AXES = ("x_lo", "y", "z_hi", "z_lo", "core", "x_hi")
FINE_SIZES = (2, 4, 4, 4, 2, 2)
Z = ("z_hi", "z_lo")
TILE = ("x_lo", "y", "z_hi", "z_lo", "core")
AROUND = ("x_hi", "x_lo", "y", "core")
REACH = 3


def spread(block, axis):
    count = lax.axis_size(axis)
    return lax.all_to_all(jnp.broadcast_to(block[None], (count,) + block.shape), axis, 0, 0)


def gather_weights(w_in, w_mid, w_out):
    columns = 2 * w_in.shape[1] + w_mid.shape[1]
    (rows,) = on_chip(
        pack_kernel,
        (jax.ShapeDtypeStruct((w_in.shape[0], columns), jnp.bfloat16),),
        (w_in, w_mid, w_out),
        0,
    )
    rows = lax.all_gather(rows, "core", axis=0, tiled=True)
    width = rows.shape[1] // 2
    half = lax.dynamic_slice_in_dim(rows, lax.axis_index("core") * width, width, 1)
    half = spread(half, Z).reshape(-1, width)
    half = spread(half, ("x_lo", "y")).reshape(-1, width)
    return spread(half, "core")


def swapped(array, axis):
    return lax.ppermute(array, axis, [(0, 1), (1, 0)])


def swapped_between_chips(array):
    pairs = []
    for row in range(1, lax.axis_size(TILE) - 1, 2):
        pairs += [(row, row + 1), (row + 1, row)]
    return lax.ppermute(array, TILE, pairs)


def neighbour_sum(field):
    far = swapped_between_chips(field)
    edges = swapped(jnp.concatenate([field[:1], field[-1:]]), "x_hi")
    near = swapped(field, "core")
    east = jnp.concatenate([field[1:], edges[:1]])
    west = jnp.concatenate([edges[1:], field[:-1]])
    return far + near + east + west


def adjoint_layers(source, hidden_one, hidden_two, weights):
    features = source.shape[1]
    depth = weights.shape[2] - features
    slope_two = 1.0 - jnp.square(hidden_two.astype(jnp.float32))
    back_two = lax.dot_general(
        source, weights[1, :, depth:], CONTRACT_LAST, preferred_element_type=jnp.float32
    )
    back_two = (slope_two * back_two).astype(jnp.bfloat16)
    back_one = lax.dot_general(
        back_two[:, :depth],
        weights[0, :, features:],
        CONTRACT_LAST,
        preferred_element_type=jnp.float32,
    ) + lax.dot_general(
        back_two[:, depth:],
        weights[1, :, :depth],
        CONTRACT_LAST,
        preferred_element_type=jnp.float32,
    )
    slope_one = 1.0 - jnp.square(hidden_one.astype(jnp.float32))
    return (slope_one * back_one).astype(jnp.bfloat16)


def last_step_kernel(source, hidden_one, hidden_two, weights, one_out, back):
    features = source.shape[1]
    back_one = adjoint_layers(source[...], hidden_one[...], hidden_two[...], weights)
    one_out[...] = back_one
    back[...] = jnp.dot(back_one, weights[0, :, :features], preferred_element_type=jnp.float32)


def first_step_kernel(
    partial,
    near,
    far,
    back,
    gating,
    diffusivity,
    hidden_one,
    hidden_two,
    states,
    source_late,
    one_late,
    hidden_late,
    states_late,
    weights,
    adjoint_out,
    spreading_out,
    one_out,
    grads,
):
    adjoint = partial[...] + (near[...] + far[...]) + back[...]
    adjoint_out[...] = adjoint
    spreading_out[...] = diffusivity[...] * adjoint
    source = (gating[...] * adjoint).astype(jnp.bfloat16)
    back_one = adjoint_layers(source, hidden_one[...], hidden_two[...], weights)
    one_out[...] = back_one
    pairs = (
        (one_late[...], back_one, states_late[...], states[...]),
        (hidden_late[...], hidden_two[...], source_late[...], source),
    )
    _, blocks, halves, rows, columns = grads.shape
    for which, (left_late, left, right_late, right) in enumerate(pairs):
        total = lax.dot_general(
            jnp.concatenate([left_late, left]),
            jnp.concatenate([right_late, right]),
            CONTRACT_FIRST,
            preferred_element_type=jnp.float32,
        ).astype(jnp.bfloat16)
        for block in range(blocks):
            for half in range(halves):
                grads[which, block, half] = total[
                    block * rows : (block + 1) * rows, half * columns : (half + 1) * columns
                ]


def edge_kernel(state, increment, diffusivity, land_sea, col, lev, val, prec, edges):
    edges[...] = jnp.zeros_like(edges)
    cells = state.shape[1]
    for which, field in enumerate((state, increment, diffusivity)):
        start = 2 * REACH * which
        edges[start : start + REACH] = field[0, :REACH]
        edges[start + REACH : start + 2 * REACH] = field[0, cells - REACH :]
    edges[18:19, :cells] = 0.5 + land_sea[...].astype(jnp.float32)
    count = col.shape[1]
    for row, numbers in enumerate((col, lev, val, prec)):
        edges[19 + row : 20 + row, :count] = numbers[...].astype(jnp.float32)


def widen_kernel(state, increment, diffusivity, land_sea, edges, wide):
    cells = state.shape[1]
    length = cells + 8
    for which, field in enumerate((state, increment, diffusivity)):
        base, start = length * which, 2 * REACH * which
        wide[base : base + cells] = field[0]
        wide[base + cells : base + length] = jnp.zeros((8, field.shape[2]), jnp.float32)
        wide[base + cells : base + cells + REACH] = edges[start : start + REACH]
        wide[base + length - REACH : base + length] = edges[start + REACH : start + 2 * REACH]
    own = 0.5 + land_sea[...].astype(jnp.float32)
    other = jnp.broadcast_to(edges[18:19, :cells], (8, cells))
    lane = lax.broadcasted_iota(jnp.int32, (8, cells), 1)
    other = jnp.where(lane < REACH, other, pltpu.roll(other, 8, 1))
    wide[3 * length :, :cells] = jnp.broadcast_to(own, (8, cells))
    wide[3 * length :, cells:] = other


def forward_kernel(
    own,
    near,
    far,
    beyond,
    edges,
    col,
    lev,
    val,
    prec,
    weights,
    first_one,
    first_two,
    first_states,
    last_one,
    last_two,
    last_states,
    source,
    gating_out,
    spreading_out,
    partial,
):
    cells, features = first_states.shape
    depth = weights.shape[2] - features
    length = cells + 8
    counted = (length, own.shape[1])
    diagonal = lax.broadcasted_iota(jnp.int32, counted, 0) == lax.broadcasted_iota(
        jnp.int32, counted, 1
    )

    def row(ref, which):
        return ref[which * length : (which + 1) * length, :]

    def gating(ref):
        return jnp.sum(
            jnp.where(diagonal, ref[3 * length : 3 * length + 1, :], 0.0), axis=1, keepdims=True
        )

    def laplace(field, lat):
        return (
            lat + pltpu.roll(field, 1, 0) + pltpu.roll(field, length - 1, 0) - 4.0 * field
        )

    def activate(both):
        hidden = jnp.tanh(both[:length]).astype(jnp.bfloat16).astype(jnp.float32)
        tangent = (1.0 - hidden * hidden) * both[length:]
        return jnp.concatenate([hidden, tangent]).astype(jnp.bfloat16)

    def network(states, tangents, saved=None):
        stacked = jnp.concatenate([states, tangents]).astype(jnp.bfloat16)
        one = activate(
            lax.dot_general(
                stacked,
                weights[0, :, :features],
                CONTRACT_LAST,
                preferred_element_type=jnp.float32,
            )
        )
        low = activate(jnp.dot(one, weights[0, :, features:], preferred_element_type=jnp.float32))
        high = activate(jnp.dot(one, weights[1, :, :depth], preferred_element_type=jnp.float32))
        if saved is not None:
            saved[0][...] = one[:cells]
            saved[1][:, :depth] = low[:cells]
            saved[1][:, depth:] = high[:cells]
            saved[2][...] = stacked[:cells]
        out = jnp.dot(
            low, weights[1, :depth, depth:], preferred_element_type=jnp.float32
        ) + jnp.dot(high, weights[1, depth:, depth:], preferred_element_type=jnp.float32)
        return out[:length], out[length:]

    gate, diffuse = gating(own), row(own, 2)
    states, tangents = row(own, 0), row(own, 1)
    tend, tangent = network(states, tangents, (first_one, first_two, first_states))
    state_one = states + diffuse * laplace(states, row(near, 0) + row(far, 0)) + gate * tend
    increment_one = (
        tangents + diffuse * laplace(tangents, row(near, 1) + row(far, 1)) + gate * tangent
    )
    middle = states + tangents
    lat = jnp.zeros_like(middle)
    for ref, outer, start in ((near, beyond, 0), (far, far, 3 * length + 8)):
        states, tangents = row(ref, 0), row(ref, 1)
        both = states + tangents
        outside = outer[start : start + length, :] + outer[start + length : start + 2 * length, :]
        tend, tangent = network(states, tangents)
        lat = lat + (
            both
            + row(ref, 2) * laplace(both, middle + outside)
            + gating(ref) * (tend + tangent)
        )
    tend, tangent = network(state_one, increment_one, (last_one, last_two, last_states))
    final = state_one + increment_one
    final = final + diffuse * laplace(final, lat) + gate * (tend + tangent)

    count = col.shape[1]
    columns = edges[19:20, :count]
    columns = jnp.where(
        columns == 0.0, float(cells), jnp.where(columns == cells - 1.0, length - 1.0, -1.0)
    )
    columns = jnp.concatenate([col[...].astype(jnp.float32), columns], axis=1)
    chosen = [lev, val, prec]
    chosen = [
        jnp.concatenate([here[...].astype(jnp.float32), edges[20 + i : 21 + i, :count]], axis=1)
        for i, here in enumerate(chosen)
    ]
    cell_ids = lax.broadcasted_iota(jnp.int32, (length, 2 * count), 0).astype(jnp.float32)
    level_ids = lax.broadcasted_iota(jnp.int32, (features, 2 * count), 0).astype(jnp.float32)
    pick_cell = (cell_ids == columns).astype(jnp.float32)
    pick_level = (level_ids == chosen[0]).astype(jnp.float32)
    at_level = jnp.dot(
        final, pick_level, precision=lax.Precision.HIGHEST, preferred_element_type=jnp.float32
    )
    modelled = jnp.sum(pick_cell * at_level, axis=0, keepdims=True)
    weighted = chosen[2] * (modelled - chosen[1])
    adjoint = lax.dot_general(
        pick_cell * weighted,
        pick_level,
        CONTRACT_LAST,
        precision=lax.Precision.HIGHEST,
        preferred_element_type=jnp.float32,
    )
    spreading = diffuse * adjoint
    spreading_out[...] = spreading[:cells]
    partial[...] = (adjoint + laplace(spreading, jnp.zeros_like(spreading)))[:cells]
    source[...] = (gate * adjoint)[:cells].astype(jnp.bfloat16)
    gating_out[...] = gate[:cells]


def on_chip(kernel, outs, operands, flops, scratch=(), scalars=0):
    size = sum(array.size * array.dtype.itemsize for array in list(operands) + list(outs))
    places = [pltpu.SMEM] * scalars + [pltpu.VMEM] * (len(operands) - scalars)
    return pl.pallas_call(
        kernel,
        out_shape=outs,
        in_specs=[pl.BlockSpec(memory_space=place) for place in places],
        out_specs=[pl.BlockSpec(memory_space=pltpu.VMEM)] * len(outs),
        scratch_shapes=scratch,
        compiler_params=pltpu.CompilerParams(vmem_limit_bytes=24 * 1024 * 1024),
        cost_estimate=pl.CostEstimate(flops=flops, bytes_accessed=size, transcendentals=0),
    )(*operands)


def pack_kernel(w_in, w_mid, w_out, rows):
    features = w_in.shape[1]
    rows[:, :features] = w_in[...].astype(jnp.bfloat16)
    rows[:, features:-features] = w_mid[...]
    rows[:, -features:] = w_out[...].astype(jnp.bfloat16)


def sum_and_spread_kernel(parts, copies):
    total = jnp.sum(parts[...].astype(jnp.float32), axis=0).astype(jnp.bfloat16)
    copies[...] = jnp.broadcast_to(total[None], copies.shape)


def sum_and_square_kernel(place, parts, copies, total):
    total[...] = jnp.sum(parts[...].astype(jnp.float32), axis=0)
    depth = copies.shape[1] // 2
    own = total[pl.ds(pl.multiple_of(place[0] * depth, depth), depth), :]
    squares = jnp.sum(total[...] * total[...], axis=0, keepdims=True)
    both = jnp.concatenate([own, jnp.broadcast_to(squares, own.shape)])
    copies[...] = jnp.broadcast_to(both[None], copies.shape)


def update_kernel(blocks, count, place, parts, w_in, w_out, new_in, new_out):
    depth = parts.shape[1] // 2
    shard = w_in.shape[0]
    squares = jnp.sum(parts[:, depth, :], axis=0, keepdims=True)
    square_sum = jnp.sum(squares, axis=1, keepdims=True)
    scale = LEARN_RATE / jnp.sqrt(square_sum / count + EPSILON)
    for which, (old, new) in enumerate(((w_in, new_in), (w_out, new_out))):
        sides = []
        for half in range(2):
            rows = parts[(which * blocks + place[0]) * 2 + half, :depth, :]
            sides.append(jnp.where(place[1] == 0, rows[:shard], rows[shard:]))
        new[...] = old[...] - scale * jnp.concatenate(sides, axis=1)


def updated(grads, w_in, w_out):
    kinds, blocks, halves, rows, columns = grads.shape
    peers = kinds * blocks * halves
    grads = lax.all_to_all(grads.reshape(peers, rows, columns), AROUND, 0, 0)
    for axis in ("z_lo", "z_hi"):
        count = lax.axis_size(axis)
        (copies,) = on_chip(
            sum_and_spread_kernel,
            (jax.ShapeDtypeStruct((count, rows, columns), jnp.bfloat16),),
            (grads,),
            grads.size,
        )
        grads = lax.all_to_all(copies, axis, 0, 0)
    depth = rows // lax.axis_size(Z)
    (copies,) = on_chip(
        sum_and_square_kernel,
        (jax.ShapeDtypeStruct((peers, 2 * depth, columns), jnp.float32),),
        (lax.axis_index(Z)[None], grads),
        grads.size,
        scratch=(pltpu.VMEM((rows, columns), jnp.float32),),
        scalars=1,
    )
    parts = lax.all_to_all(copies, AROUND, 0, 0)
    place = jnp.stack([lax.axis_index(("x_lo", "y")), lax.axis_index("core")])
    shape = jax.ShapeDtypeStruct(w_in.shape, jnp.float32)
    return on_chip(
        functools.partial(update_kernel, blocks, float(peers * rows * columns)),
        (shape, shape),
        (place, parts, w_in, w_out),
        parts.size,
        scalars=1,
    )


def local(
    state, increment, diffusivity, land_sea, w_in, w_mid, w_out, obs_col, obs_lev, obs_val, obs_prec
):
    _, cells, features = state.shape
    length = cells + 8
    fields = (state, increment, diffusivity, land_sea)
    observed = [numbers[None] for numbers in (obs_col, obs_lev, obs_val, obs_prec)]

    def outs(*shapes):
        return tuple(jax.ShapeDtypeStruct(shape, kind) for shape, kind in shapes)

    (edges,) = on_chip(
        edge_kernel, outs(((24, features), jnp.float32)), fields + tuple(observed), 0
    )
    edges = swapped(edges, "x_hi")
    (own,) = on_chip(
        widen_kernel, outs(((3 * length + 8, features), jnp.float32)), fields + (edges,), 0
    )
    near = swapped(own, "core")
    far = swapped_between_chips(jnp.concatenate([own, near[: 2 * length]]))
    beyond = swapped(far[: 2 * length], "core")

    weights = gather_weights(w_in, w_mid, w_out)
    hidden_units = weights.shape[1]
    layer = 2 * cells * hidden_units
    wide = ((cells, hidden_units), jnp.bfloat16)
    narrow_b = ((cells, features), jnp.bfloat16)
    narrow = ((cells, features), jnp.float32)
    (
        hidden_one,
        hidden_two,
        states_b,
        late_one,
        late_two,
        states_late,
        source_late,
        gating,
        spreading,
        partial,
    ) = on_chip(
        forward_kernel,
        outs(
            wide, wide, narrow_b, wide, wide, narrow_b, narrow_b, ((cells, 1), jnp.float32),
            narrow, narrow,
        ),
        (own, near, far, beyond, edges, *observed, weights),
        8 * layer * (2 * features + hidden_units),
    )
    near = swapped(spreading, "core")
    far = swapped_between_chips(spreading)
    back_late, back_sum = on_chip(
        last_step_kernel,
        outs(wide, narrow),
        (source_late, late_one, late_two, weights),
        layer * (2 * features + hidden_units),
    )
    blocks = lax.axis_size(("x_lo", "y"))
    halves = lax.axis_size("core")
    adjoint, spreading, back_first, grads = on_chip(
        first_step_kernel,
        outs(
            narrow,
            narrow,
            wide,
            ((2, blocks, halves, hidden_units // blocks, features // halves), jnp.bfloat16),
        ),
        (
            partial,
            near,
            far,
            back_sum,
            gating,
            diffusivity[0],
            hidden_one,
            hidden_two,
            states_b,
            source_late,
            back_late,
            late_two,
            states_late,
            weights,
        ),
        layer * (5 * features + hidden_units),
    )
    w_in_new, w_out_new = updated(grads, w_in, w_out)
    adjoint = (
        adjoint
        + (neighbour_sum(spreading) - 4.0 * spreading)
        + jnp.dot(back_first, weights[0, :, :features], preferred_element_type=jnp.float32)
    )
    return adjoint[None], w_in_new, w_out_new


def solution(mesh):
    fine = Mesh(mesh.devices.reshape(FINE_SIZES), FINE_AXES)
    everywhere = TILE + ("x_hi",)
    return jax.shard_map(
        local,
        mesh=fine,
        in_specs=(
            P(TILE, "x_hi", None),
            P(TILE, "x_hi", None),
            P(TILE, "x_hi", None),
            P(TILE, "x_hi"),
            P(TILE, None),
            P(TILE, None),
            P(TILE, None),
            P(everywhere),
            P(everywhere),
            P(everywhere),
            P(everywhere),
        ),
        out_specs=(P(TILE, "x_hi", None), P(TILE, None), P(TILE, None)),
        check_vma=False,
    )
```

```python
import functools

import jax
import jax.numpy as jnp
from jax import lax
from jax.experimental import pallas as pl
from jax.experimental.pallas import tpu as pltpu
from jax.sharding import Mesh
from jax.sharding import PartitionSpec as P

LEARN_RATE = 0.02
EPSILON = 1e-06
CONTRACT_LAST = (((1,), (1,)), ((), ()))
CONTRACT_FIRST = (((0,), (0,)), ((), ()))
FINE_AXES = ("x_lo", "y", "z_hi", "z_lo", "core", "x_hi")
FINE_SIZES = (2, 4, 4, 4, 2, 2)
Z = ("z_hi", "z_lo")
TILE = ("x_lo", "y", "z_hi", "z_lo", "core")
AROUND = ("x_hi", "x_lo", "y", "core")
REACH = 3
BLOCK = 144


def spread(block, axis):
    count = lax.axis_size(axis)
    return lax.all_to_all(jnp.broadcast_to(block[None], (count,) + block.shape), axis, 0, 0)


def gather_weights(w_in, w_mid, w_out):
    columns = 2 * w_in.shape[1] + w_mid.shape[1]
    (rows,) = on_chip(
        pack_kernel,
        (jax.ShapeDtypeStruct((w_in.shape[0], columns), jnp.bfloat16),),
        (w_in, w_mid, w_out),
        0,
        fetched=3,
    )
    rows = lax.all_gather(rows, "core", axis=0, tiled=True)
    width = rows.shape[1] // 2
    half = lax.dynamic_slice_in_dim(rows, lax.axis_index("core") * width, width, 1)
    half = spread(half, Z).reshape(-1, width)
    half = spread(half, ("x_lo", "y")).reshape(-1, width)
    return half


def swapped(array, axis):
    return lax.ppermute(array, axis, [(0, 1), (1, 0)])


def swapped_between_chips(array):
    pairs = []
    for row in range(1, lax.axis_size(TILE) - 1, 2):
        pairs += [(row, row + 1), (row + 1, row)]
    return lax.ppermute(array, TILE, pairs)


def swapped_three_apart(array):
    count = lax.axis_size(TILE)
    pairs = [(row, row + 3) for row in range(1, count - 3, 2)]
    return lax.ppermute(array, TILE, pairs + [(after, row) for row, after in pairs])


def neighbour_sum(field):
    far = swapped_between_chips(field)
    edges = swapped(jnp.concatenate([field[:1], field[-1:]]), "x_hi")
    near = swapped(field, "core")
    east = jnp.concatenate([field[1:], edges[:1]])
    west = jnp.concatenate([edges[1:], field[:-1]])
    return far + near + east + west


def adjoint_layers(source, hidden_one, hidden_two, weights):
    features = source.shape[1]
    depth = weights.shape[2] - features
    slope_two = 1.0 - jnp.square(hidden_two.astype(jnp.float32))
    back_two = lax.dot_general(
        source, weights[1, :, depth:], CONTRACT_LAST, preferred_element_type=jnp.float32
    )
    back_two = (slope_two * back_two).astype(jnp.bfloat16)
    back_one = lax.dot_general(
        back_two[:, :depth],
        weights[0, :, features:],
        CONTRACT_LAST,
        preferred_element_type=jnp.float32,
    ) + lax.dot_general(
        back_two[:, depth:],
        weights[1, :, :depth],
        CONTRACT_LAST,
        preferred_element_type=jnp.float32,
    )
    slope_one = 1.0 - jnp.square(hidden_one.astype(jnp.float32))
    return (slope_one * back_one).astype(jnp.bfloat16)


def edge_kernel(state, increment, diffusivity, land_sea, col, lev, val, prec, edges, outer):
    edges[...] = jnp.zeros_like(edges)
    cells = state.shape[1]
    for which, field in enumerate((state, increment, diffusivity)):
        start = 2 * REACH * which
        edges[start : start + REACH] = field[0, :REACH]
        edges[start + REACH : start + 2 * REACH] = field[0, cells - REACH :]
    edges[18:19, :cells] = 0.5 + land_sea[...].astype(jnp.float32)
    count = col.shape[1]
    for row, numbers in enumerate((col, lev, val, prec)):
        edges[19 + row : 20 + row, :count] = numbers[...].astype(jnp.float32)
    outer[...] = (state[0] + increment[0]).astype(jnp.bfloat16)


def ring_gating(mine, other):
    cells = mine.shape[1]
    lane = lax.broadcasted_iota(jnp.int32, (8, cells), 1)
    mine, other = (jnp.broadcast_to(row, (8, cells)) for row in (mine, other))
    other = jnp.where(lane < REACH, other, pltpu.roll(other, 8, 1))
    return jnp.concatenate([mine, other], axis=1)


def ring_field(field, edges, which):
    start = 2 * REACH * which
    return jnp.concatenate(
        [
            field,
            edges[start : start + REACH],
            jnp.zeros((8 - 2 * REACH, field.shape[1]), jnp.float32),
            edges[start + REACH : start + 2 * REACH],
        ]
    )


def pack_row_kernel(state, increment, diffusivity, mine, other, pack):
    cells, features = state.shape[1:]
    for which, field in enumerate((state, increment, diffusivity)):
        ring = ring_field(field[0], other, which)
        ring = jnp.concatenate([ring, jnp.zeros((8, features), jnp.float32)])
        pack[BLOCK * which : BLOCK * (which + 1)] = ring.astype(jnp.bfloat16)
    gating = ring_gating(mine[18:19, :cells], other[18:19, :cells])[:1]
    numbers = mine[21:23, :]
    coarse = numbers.astype(jnp.bfloat16).astype(jnp.float32)
    fine = numbers - coarse
    rest = [gating, mine[19:21, :], coarse, fine, jnp.zeros((16 - 7, features), jnp.float32)]
    pack[3 * BLOCK :] = jnp.concatenate(rest).astype(jnp.bfloat16)


def whole_kernel(
    observations,
    state,
    increment,
    diffusivity,
    mine,
    other,
    near,
    far,
    beyond,
    outer,
    settled_out,
    spreading_out,
    grads,
    weights,
):
    cells, features = state.shape[1:]
    depth = weights.shape[2] - features
    length = cells + 8
    pack = 3 * BLOCK + 16
    square = (length, 2 * cells)
    diagonal = lax.broadcasted_iota(jnp.int32, square, 0) == lax.broadcasted_iota(
        jnp.int32, square, 1
    )

    def column(row):
        return jnp.sum(jnp.where(diagonal, row, 0.0), axis=1, keepdims=True)

    def laplace(field, lat):
        return lat + pltpu.roll(field, 1, 0) + pltpu.roll(field, length - 1, 0) - 4.0 * field

    def unpack(ref, start):
        fields = [
            ref[start + BLOCK * i : start + BLOCK * (i + 1), :].astype(jnp.float32)[:length]
            for i in range(3)
        ]
        rest = ref[start + 3 * BLOCK : start + pack, :].astype(jnp.float32)
        return fields + [column(rest[:1])], rest

    def activate(both):
        hidden = jnp.tanh(both[:length]).astype(jnp.bfloat16).astype(jnp.float32)
        tangent = (1.0 - hidden * hidden) * both[length:]
        return jnp.concatenate([hidden, tangent]).astype(jnp.bfloat16)

    def network(states, tangents):
        stacked = jnp.concatenate([states, tangents]).astype(jnp.bfloat16)
        one = activate(
            lax.dot_general(
                stacked,
                weights[0, :, :features],
                CONTRACT_LAST,
                preferred_element_type=jnp.float32,
            )
        )
        low = activate(jnp.dot(one, weights[0, :, features:], preferred_element_type=jnp.float32))
        high = activate(jnp.dot(one, weights[1, :, :depth], preferred_element_type=jnp.float32))
        out = jnp.dot(
            low, weights[1, :depth, depth:], preferred_element_type=jnp.float32
        ) + jnp.dot(high, weights[1, depth:, depth:], preferred_element_type=jnp.float32)
        saved = (one[:cells], jnp.concatenate([low[:cells], high[:cells]], axis=1), stacked[:cells])
        return out[:length], out[length:], saved

    def observed(final, columns, levels, values, precisions):
        count = columns.shape[1]
        cell_ids = lax.broadcasted_iota(jnp.int32, (length, count), 0).astype(jnp.float32)
        level_ids = lax.broadcasted_iota(jnp.int32, (features, count), 0).astype(jnp.float32)
        pick_cell = (cell_ids == columns).astype(jnp.float32)
        pick_level = (level_ids == levels).astype(jnp.float32)
        at_level = jnp.dot(
            final, pick_level, precision=lax.Precision.HIGHEST, preferred_element_type=jnp.float32
        )
        modelled = jnp.sum(pick_cell * at_level, axis=0, keepdims=True)
        return lax.dot_general(
            pick_cell * (precisions * (modelled - values)),
            pick_level,
            CONTRACT_LAST,
            precision=lax.Precision.HIGHEST,
            preferred_element_type=jnp.float32,
        )

    own = [ring_field(ref[0], other, i) for i, ref in enumerate((state, increment, diffusivity))]
    gate = column(ring_gating(mine[18:19, :cells], other[18:19, :cells])[:1])
    own.append(gate)
    beside, beside_rest = zip(unpack(near, 0), unpack(far, 0))
    second = [unpack(beyond, 0)[0], unpack(far, pack)[0]]
    third = [unpack(beyond, pack)[0]]
    third = [
        third[0][0] + third[0][1],
        jnp.concatenate(
            [outer[...].astype(jnp.float32), jnp.zeros((length - cells, features), jnp.float32)]
        ),
    ]

    def advance(row, lats):
        states, tangents, diffuse, gated = row
        tend, tangent, saved = network(states, tangents)
        return (
            states + diffuse * laplace(states, lats[0]) + gated * tend,
            tangents + diffuse * laplace(tangents, lats[1]) + gated * tangent,
            saved,
        )

    def advance_sum(row, middle, lat):
        tend, tangent, saved = network(row[0], row[1])
        return middle + row[2] * laplace(middle, lat) + row[3] * (tend + tangent), saved

    state_one, increment_one, first = advance(
        own, [beside[0][i] + beside[1][i] for i in range(2)]
    )
    middle_one = state_one + increment_one
    beside_one, beside_middle, second_middle = [], [], []
    for row, next_row, last in zip(beside, second, third):
        one = advance(row, [own[i] + next_row[i] for i in range(2)])[:2]
        beside_one.append(one)
        beside_middle.append(one[0] + one[1])
        next_sum = next_row[0] + next_row[1]
        second_middle.append(
            advance_sum(next_row, next_sum, row[0] + row[1] + last)[0]
        )
    final, late = advance_sum(
        [state_one, increment_one, own[2], gate],
        middle_one,
        beside_middle[0] + beside_middle[1],
    )

    count = observations
    columns = other[19:20, :count]
    columns = jnp.where(
        columns == 0.0, float(cells), jnp.where(columns == cells - 1.0, length - 1.0, -1.0)
    )
    columns = jnp.concatenate([mine[19:20, :count], columns], axis=1)
    chosen = [
        jnp.concatenate([mine[i : i + 1, :count], other[i : i + 1, :count]], axis=1)
        for i in (20, 21, 22)
    ]
    adjoint = observed(final, columns, *chosen)
    around = jnp.zeros_like(adjoint)
    for row, one, middle, next_middle, rest in zip(
        beside, beside_one, beside_middle, second_middle, beside_rest
    ):
        total = advance_sum(
            [one[0], one[1], row[2], row[3]], middle, middle_one + next_middle
        )[0]
        around = around + row[2] * observed(
            total,
            rest[1:2, :cells],
            rest[2:3, :cells],
            rest[3:4, :cells] + rest[5:6, :cells],
            rest[4:5, :cells] + rest[6:7, :cells],
        )
    spreading = own[2] * adjoint
    adjoint_one = (adjoint + laplace(spreading, around))[:cells]
    gate = gate[:cells]
    source_late = (gate * adjoint[:cells]).astype(jnp.bfloat16)
    back_late = adjoint_layers(source_late, late[0], late[1], weights)
    adjoint_one = adjoint_one + jnp.dot(
        back_late, weights[0, :, :features], preferred_element_type=jnp.float32
    )
    spreading = own[2][:cells] * adjoint_one
    spreading_out[...] = spreading
    source = (gate * adjoint_one).astype(jnp.bfloat16)
    back_one = adjoint_layers(source, first[0], first[1], weights)
    settled_out[...] = (
        adjoint_one
        - 4.0 * spreading
        + jnp.dot(back_one, weights[0, :, :features], preferred_element_type=jnp.float32)
    )
    pairs = (
        (back_late, back_one, late[2], first[2]),
        (late[1], first[1], source_late, source),
    )
    _, blocks, halves, rows, width = grads.shape
    for which, (left_late, left, right_late, right) in enumerate(pairs):
        total = lax.dot_general(
            jnp.concatenate([left_late, left]),
            jnp.concatenate([right_late, right]),
            CONTRACT_FIRST,
            preferred_element_type=jnp.float32,
        ).astype(jnp.bfloat16)
        for block in range(blocks):
            for half in range(halves):
                grads[which, block, half] = total[
                    block * rows : (block + 1) * rows, half * width : (half + 1) * width
                ]


def on_chip(kernel, outs, operands, flops, scratch=(), scalars=0, fetched=0, place=None):
    size = sum(array.size * array.dtype.itemsize for array in list(operands) + list(outs))
    count = len(operands) - scalars
    by_kernel = fetched > 0
    places = [pltpu.SMEM] * scalars + [pl.ANY if by_kernel else pltpu.VMEM] * count
    body = kernel
    if by_kernel:
        copies = tuple(
            pltpu.VMEM(array.shape, array.dtype)
            for array in operands[scalars : scalars + fetched]
        )
        scratch = copies + (pltpu.SemaphoreType.DMA((count,)),) + tuple(scratch)

        def body(*refs):
            numbers, sources, refs = refs[:scalars], refs[scalars : scalars + count], refs[scalars + count :]
            results, refs = refs[: len(outs)], refs[len(outs) :]
            held, done, rest = refs[:fetched], refs[fetched], refs[fetched + 1 :]
            targets = list(held)
            if place is not None:
                targets += place(numbers, rest)
            moves = [
                pltpu.make_async_copy(source, target, done.at[i])
                for i, (source, target) in enumerate(zip(sources, targets))
            ]
            for move in moves:
                move.start()
            for move in moves:
                move.wait()
            kernel(*held, *results, *rest)

    return pl.pallas_call(
        body,
        out_shape=outs,
        in_specs=[pl.BlockSpec(memory_space=place_) for place_ in places],
        out_specs=[pl.BlockSpec(memory_space=pltpu.VMEM)] * len(outs),
        scratch_shapes=scratch,
        compiler_params=pltpu.CompilerParams(vmem_limit_bytes=32 * 1024 * 1024),
        cost_estimate=pl.CostEstimate(flops=flops, bytes_accessed=size, transcendentals=0),
    )(*operands)


def pack_kernel(w_in, w_mid, w_out, rows):
    features = w_in.shape[1]
    rows[:, :features] = w_in[...].astype(jnp.bfloat16)
    rows[:, features:-features] = w_mid[...]
    rows[:, -features:] = w_out[...].astype(jnp.bfloat16)


def sum_and_spread_kernel(parts, copies):
    total = jnp.sum(parts[...].astype(jnp.float32), axis=0).astype(jnp.bfloat16)
    copies[...] = jnp.broadcast_to(total[None], copies.shape)


def sum_and_square_kernel(place, parts, copies, total):
    total[...] = jnp.sum(parts[...].astype(jnp.float32), axis=0)
    depth = copies.shape[1] // 2
    own = total[pl.ds(pl.multiple_of(place[0] * depth, depth), depth), :]
    squares = jnp.sum(total[...] * total[...], axis=0, keepdims=True)
    both = jnp.concatenate([own, jnp.broadcast_to(squares, own.shape)])
    copies[...] = jnp.broadcast_to(both[None], copies.shape)


def update_kernel(blocks, count, place, parts, w_in, w_out, new_in, new_out):
    depth = parts.shape[1] // 2
    shard = w_in.shape[0]
    squares = jnp.sum(parts[:, depth, :], axis=0, keepdims=True)
    square_sum = jnp.sum(squares, axis=1, keepdims=True)
    scale = LEARN_RATE / jnp.sqrt(square_sum / count + EPSILON)
    for which, (old, new) in enumerate(((w_in, new_in), (w_out, new_out))):
        sides = []
        for half in range(2):
            rows = parts[(which * blocks + place[0]) * 2 + half, :depth, :]
            sides.append(jnp.where(place[1] == 0, rows[:shard], rows[shard:]))
        new[...] = old[...] - scale * jnp.concatenate(sides, axis=1)


def updated(grads, w_in, w_out):
    kinds, blocks, halves, rows, columns = grads.shape
    peers = kinds * blocks * halves
    grads = lax.all_to_all(grads.reshape(peers, rows, columns), AROUND, 0, 0)
    for axis in ("z_lo", "z_hi"):
        count = lax.axis_size(axis)
        (copies,) = on_chip(
            sum_and_spread_kernel,
            (jax.ShapeDtypeStruct((count, rows, columns), jnp.bfloat16),),
            (grads,),
            grads.size,
        )
        grads = lax.all_to_all(copies, axis, 0, 0)
    depth = rows // lax.axis_size(Z)
    (copies,) = on_chip(
        sum_and_square_kernel,
        (jax.ShapeDtypeStruct((peers, 2 * depth, columns), jnp.float32),),
        (lax.axis_index(Z)[None], grads),
        grads.size,
        scratch=(pltpu.VMEM((rows, columns), jnp.float32),),
        scalars=1,
    )
    parts = lax.all_to_all(copies, AROUND, 0, 0)
    place = jnp.stack([lax.axis_index(("x_lo", "y")), lax.axis_index("core")])
    shape = jax.ShapeDtypeStruct(w_in.shape, jnp.float32)
    return on_chip(
        functools.partial(update_kernel, blocks, float(peers * rows * columns)),
        (shape, shape),
        (place, parts, w_in, w_out),
        parts.size,
        scalars=1,
    )


def local(
    state, increment, diffusivity, land_sea, w_in, w_mid, w_out, obs_col, obs_lev, obs_val, obs_prec
):
    _, cells, features = state.shape
    length = cells + 8
    fields = (state, increment, diffusivity, land_sea)
    observed = [numbers[None] for numbers in (obs_col, obs_lev, obs_val, obs_prec)]

    def outs(*shapes):
        return tuple(jax.ShapeDtypeStruct(shape, kind) for shape, kind in shapes)

    mine, outer = on_chip(
        edge_kernel,
        outs(((24, features), jnp.float32), ((cells, features), jnp.bfloat16)),
        fields + tuple(observed),
        0,
        fetched=8,
    )
    outer = swapped_three_apart(outer)
    other = swapped(mine, "x_hi")
    (own,) = on_chip(
        pack_row_kernel,
        outs(((3 * BLOCK + 16, features), jnp.bfloat16)),
        fields[:3] + (mine, other),
        0,
        fetched=5,
    )
    near = swapped(own, "core")
    far = swapped_between_chips(jnp.concatenate([own, near]))
    beyond = swapped(far, "core")

    half = gather_weights(w_in, w_mid, w_out)
    hidden_units, width = half.shape
    blocks = lax.axis_size(("x_lo", "y"))
    halves = lax.axis_size("core")
    narrow = ((cells, features), jnp.float32)
    settled, spreading, grads = on_chip(
        functools.partial(whole_kernel, obs_col.shape[0]),
        outs(
            narrow,
            narrow,
            ((2, blocks, halves, hidden_units // blocks, features // halves), jnp.bfloat16),
        ),
        (lax.axis_index("core")[None], *fields[:3], mine, other, near, far, beyond, outer)
        + (half, swapped(half, "core")),
        40 * cells * hidden_units * (2 * features + hidden_units),
        scratch=(pltpu.VMEM((2, hidden_units, width), jnp.bfloat16),),
        scalars=1,
        fetched=9,
        place=lambda numbers, rest: [
            rest[0].at[numbers[0][0]],
            rest[0].at[1 - numbers[0][0]],
        ],
    )
    w_in_new, w_out_new = updated(grads, w_in, w_out)
    adjoint = settled + neighbour_sum(spreading)
    return adjoint[None], w_in_new, w_out_new


def solution(mesh):
    fine = Mesh(mesh.devices.reshape(FINE_SIZES), FINE_AXES)
    everywhere = TILE + ("x_hi",)
    return jax.shard_map(
        local,
        mesh=fine,
        in_specs=(
            P(TILE, "x_hi", None),
            P(TILE, "x_hi", None),
            P(TILE, "x_hi", None),
            P(TILE, "x_hi"),
            P(TILE, None),
            P(TILE, None),
            P(TILE, None),
            P(everywhere),
            P(everywhere),
            P(everywhere),
            P(everywhere),
        ),
        out_specs=(P(TILE, "x_hi", None), P(TILE, None), P(TILE, None)),
        check_vma=False,
    )
```

```python
import functools

import jax
import jax.numpy as jnp
from jax import lax
from jax.experimental import pallas as pl
from jax.experimental.pallas import tpu as pltpu
from jax.sharding import Mesh
from jax.sharding import PartitionSpec as P

LEARN_RATE = 0.02
EPSILON = 1e-06
CONTRACT_LAST = (((1,), (1,)), ((), ()))
CONTRACT_FIRST = (((0,), (0,)), ((), ()))
FINE_AXES = ("x_lo", "y", "z_hi", "z_lo", "core", "x_hi")
FINE_SIZES = (2, 4, 4, 4, 2, 2)
Z = ("z_hi", "z_lo")
TILE = ("x_lo", "y", "z_hi", "z_lo", "core")
AROUND = ("x_hi", "x_lo", "y", "core")
REACH = 3
BLOCK = 144


def spread(block, axis):
    count = lax.axis_size(axis)
    return lax.all_to_all(jnp.broadcast_to(block[None], (count,) + block.shape), axis, 0, 0)


def chip_rows(w_in, w_mid, w_out):
    columns = 2 * w_in.shape[1] + w_mid.shape[1]
    (rows,) = on_chip(
        pack_kernel,
        (jax.ShapeDtypeStruct((w_in.shape[0], columns), jnp.bfloat16),),
        (w_in, w_mid, w_out),
        0,
        fetched=3,
        room=56,
    )
    rows = lax.all_gather(rows, "core", axis=0, tiled=True)
    width = columns // 2
    return lax.dynamic_slice_in_dim(rows, lax.axis_index("core") * width, width, 1)


def swapped(array, axis):
    return lax.ppermute(array, axis, [(0, 1), (1, 0)])


def swapped_between_chips(array):
    pairs = []
    for row in range(1, lax.axis_size(TILE) - 1, 2):
        pairs += [(row, row + 1), (row + 1, row)]
    return lax.ppermute(array, TILE, pairs)


def swapped_three_apart(array):
    count = lax.axis_size(TILE)
    pairs = [(row, row + 3) for row in range(1, count - 3, 2)]
    return lax.ppermute(array, TILE, pairs + [(after, row) for row, after in pairs])


def neighbour_sum(field):
    far = swapped_between_chips(field)
    edges = swapped(jnp.concatenate([field[:1], field[-1:]]), "x_hi")
    near = swapped(field, "core")
    east = jnp.concatenate([field[1:], edges[:1]])
    west = jnp.concatenate([edges[1:], field[:-1]])
    return far + near + east + west


def adjoint_layers(source, hidden_one, hidden_two, weights):
    features = source.shape[1]
    depth = weights.shape[2] - features
    slope_two = 1.0 - jnp.square(hidden_two.astype(jnp.float32))
    back_two = lax.dot_general(
        source, weights[1, :, depth:], CONTRACT_LAST, preferred_element_type=jnp.float32
    )
    back_two = (slope_two * back_two).astype(jnp.bfloat16)
    back_one = lax.dot_general(
        back_two[:, :depth],
        weights[0, :, features:],
        CONTRACT_LAST,
        preferred_element_type=jnp.float32,
    ) + lax.dot_general(
        back_two[:, depth:],
        weights[1, :, :depth],
        CONTRACT_LAST,
        preferred_element_type=jnp.float32,
    )
    slope_one = 1.0 - jnp.square(hidden_one.astype(jnp.float32))
    return (slope_one * back_one).astype(jnp.bfloat16)


def edge_kernel(state, increment, diffusivity, land_sea, col, lev, val, prec, edges, outer):
    edges[...] = jnp.zeros_like(edges)
    cells = state.shape[1]
    for which, field in enumerate((state, increment, diffusivity)):
        start = 2 * REACH * which
        edges[start : start + REACH] = field[0, :REACH]
        edges[start + REACH : start + 2 * REACH] = field[0, cells - REACH :]
    edges[18:19, :cells] = 0.5 + land_sea[...].astype(jnp.float32)
    count = col.shape[1]
    for row, numbers in enumerate((col, lev, val, prec)):
        edges[19 + row : 20 + row, :count] = numbers[...].astype(jnp.float32)
    outer[...] = (state[0] + increment[0]).astype(jnp.bfloat16)


def ring_gating(mine, other):
    cells = mine.shape[1]
    lane = lax.broadcasted_iota(jnp.int32, (8, cells), 1)
    mine, other = (jnp.broadcast_to(row, (8, cells)) for row in (mine, other))
    other = jnp.where(lane < REACH, other, pltpu.roll(other, 8, 1))
    return jnp.concatenate([mine, other], axis=1)


def ring_field(field, edges, which):
    start = 2 * REACH * which
    return jnp.concatenate(
        [
            field,
            edges[start : start + REACH],
            jnp.zeros((8 - 2 * REACH, field.shape[1]), jnp.float32),
            edges[start + REACH : start + 2 * REACH],
        ]
    )


def pack_row_kernel(state, increment, diffusivity, mine, other, pack):
    cells, features = state.shape[1:]
    for which, field in enumerate((state, increment, diffusivity)):
        ring = ring_field(field[0], other, which)
        ring = jnp.concatenate([ring, jnp.zeros((8, features), jnp.float32)])
        pack[BLOCK * which : BLOCK * (which + 1)] = ring.astype(jnp.bfloat16)
    gating = ring_gating(mine[18:19, :cells], other[18:19, :cells])[:1]
    numbers = mine[21:23, :]
    coarse = numbers.astype(jnp.bfloat16).astype(jnp.float32)
    fine = numbers - coarse
    rest = [gating, mine[19:21, :], coarse, fine, jnp.zeros((16 - 7, features), jnp.float32)]
    pack[3 * BLOCK :] = jnp.concatenate(rest).astype(jnp.bfloat16)


def whole_kernel(
    observations,
    state,
    increment,
    diffusivity,
    mine,
    other,
    near,
    far,
    beyond,
    outer,
    settled_out,
    spreading_out,
    grads,
    weights,
):
    cells, features = state.shape[1:]
    depth = weights.shape[2] - features
    length = cells + 8
    pack = 3 * BLOCK + 16
    square = (length, 2 * cells)
    diagonal = lax.broadcasted_iota(jnp.int32, square, 0) == lax.broadcasted_iota(
        jnp.int32, square, 1
    )

    def column(row):
        return jnp.sum(jnp.where(diagonal, row, 0.0), axis=1, keepdims=True)

    def laplace(field, lat):
        return lat + pltpu.roll(field, 1, 0) + pltpu.roll(field, length - 1, 0) - 4.0 * field

    def unpack(ref, start):
        fields = [
            ref[start + BLOCK * i : start + BLOCK * (i + 1), :].astype(jnp.float32)[:length]
            for i in range(3)
        ]
        rest = ref[start + 3 * BLOCK : start + pack, :].astype(jnp.float32)
        return fields + [column(rest[:1])], rest

    def activate(both):
        hidden = jnp.tanh(both[:length]).astype(jnp.bfloat16).astype(jnp.float32)
        tangent = (1.0 - hidden * hidden) * both[length:]
        return jnp.concatenate([hidden, tangent]).astype(jnp.bfloat16)

    def network(states, tangents):
        stacked = jnp.concatenate([states, tangents]).astype(jnp.bfloat16)
        one = activate(
            lax.dot_general(
                stacked,
                weights[0, :, :features],
                CONTRACT_LAST,
                preferred_element_type=jnp.float32,
            )
        )
        low = activate(jnp.dot(one, weights[0, :, features:], preferred_element_type=jnp.float32))
        high = activate(jnp.dot(one, weights[1, :, :depth], preferred_element_type=jnp.float32))
        out = jnp.dot(
            low, weights[1, :depth, depth:], preferred_element_type=jnp.float32
        ) + jnp.dot(high, weights[1, depth:, depth:], preferred_element_type=jnp.float32)
        saved = (one[:cells], jnp.concatenate([low[:cells], high[:cells]], axis=1), stacked[:cells])
        return out[:length], out[length:], saved

    def observed(final, columns, levels, values, precisions):
        count = columns.shape[1]
        cell_ids = lax.broadcasted_iota(jnp.int32, (length, count), 0).astype(jnp.float32)
        level_ids = lax.broadcasted_iota(jnp.int32, (features, count), 0).astype(jnp.float32)
        pick_cell = (cell_ids == columns).astype(jnp.float32)
        pick_level = (level_ids == levels).astype(jnp.float32)
        at_level = jnp.dot(
            final, pick_level, precision=lax.Precision.HIGHEST, preferred_element_type=jnp.float32
        )
        modelled = jnp.sum(pick_cell * at_level, axis=0, keepdims=True)
        return lax.dot_general(
            pick_cell * (precisions * (modelled - values)),
            pick_level,
            CONTRACT_LAST,
            precision=lax.Precision.HIGHEST,
            preferred_element_type=jnp.float32,
        )

    own = [ring_field(ref[0], other, i) for i, ref in enumerate((state, increment, diffusivity))]
    gate = column(ring_gating(mine[18:19, :cells], other[18:19, :cells])[:1])
    own.append(gate)
    beside, beside_rest = zip(unpack(near, 0), unpack(far, 0))
    second = [unpack(beyond, 0)[0], unpack(far, pack)[0]]
    third = [unpack(beyond, pack)[0]]
    third = [
        third[0][0] + third[0][1],
        jnp.concatenate(
            [outer[...].astype(jnp.float32), jnp.zeros((length - cells, features), jnp.float32)]
        ),
    ]

    def advance(row, lats):
        states, tangents, diffuse, gated = row
        tend, tangent, saved = network(states, tangents)
        return (
            states + diffuse * laplace(states, lats[0]) + gated * tend,
            tangents + diffuse * laplace(tangents, lats[1]) + gated * tangent,
            saved,
        )

    def advance_sum(row, middle, lat):
        tend, tangent, saved = network(row[0], row[1])
        return middle + row[2] * laplace(middle, lat) + row[3] * (tend + tangent), saved

    state_one, increment_one, first = advance(
        own, [beside[0][i] + beside[1][i] for i in range(2)]
    )
    middle_one = state_one + increment_one
    beside_one, beside_middle, second_middle = [], [], []
    for row, next_row, last in zip(beside, second, third):
        one = advance(row, [own[i] + next_row[i] for i in range(2)])[:2]
        beside_one.append(one)
        beside_middle.append(one[0] + one[1])
        next_sum = next_row[0] + next_row[1]
        second_middle.append(
            advance_sum(next_row, next_sum, row[0] + row[1] + last)[0]
        )
    final, late = advance_sum(
        [state_one, increment_one, own[2], gate],
        middle_one,
        beside_middle[0] + beside_middle[1],
    )

    count = observations
    columns = other[19:20, :count]
    columns = jnp.where(
        columns == 0.0, float(cells), jnp.where(columns == cells - 1.0, length - 1.0, -1.0)
    )
    columns = jnp.concatenate([mine[19:20, :count], columns], axis=1)
    chosen = [
        jnp.concatenate([mine[i : i + 1, :count], other[i : i + 1, :count]], axis=1)
        for i in (20, 21, 22)
    ]
    adjoint = observed(final, columns, *chosen)
    around = jnp.zeros_like(adjoint)
    for row, one, middle, next_middle, rest in zip(
        beside, beside_one, beside_middle, second_middle, beside_rest
    ):
        total = advance_sum(
            [one[0], one[1], row[2], row[3]], middle, middle_one + next_middle
        )[0]
        around = around + row[2] * observed(
            total,
            rest[1:2, :cells],
            rest[2:3, :cells],
            rest[3:4, :cells] + rest[5:6, :cells],
            rest[4:5, :cells] + rest[6:7, :cells],
        )
    spreading = own[2] * adjoint
    adjoint_one = (adjoint + laplace(spreading, around))[:cells]
    gate = gate[:cells]
    source_late = (gate * adjoint[:cells]).astype(jnp.bfloat16)
    back_late = adjoint_layers(source_late, late[0], late[1], weights)
    adjoint_one = adjoint_one + jnp.dot(
        back_late, weights[0, :, :features], preferred_element_type=jnp.float32
    )
    spreading = own[2][:cells] * adjoint_one
    spreading_out[...] = spreading
    source = (gate * adjoint_one).astype(jnp.bfloat16)
    back_one = adjoint_layers(source, first[0], first[1], weights)
    settled_out[...] = (
        adjoint_one
        - 4.0 * spreading
        + jnp.dot(back_one, weights[0, :, :features], preferred_element_type=jnp.float32)
    )
    pairs = (
        (back_late, back_one, late[2], first[2]),
        (late[1], first[1], source_late, source),
    )
    _, blocks, halves, rows, width = grads.shape
    for which, (left_late, left, right_late, right) in enumerate(pairs):
        total = lax.dot_general(
            jnp.concatenate([left_late, left]),
            jnp.concatenate([right_late, right]),
            CONTRACT_FIRST,
            preferred_element_type=jnp.float32,
        ).astype(jnp.bfloat16)
        for block in range(blocks):
            for half in range(halves):
                grads[which, block, half] = total[
                    block * rows : (block + 1) * rows, half * width : (half + 1) * width
                ]


def on_chip(kernel, outs, operands, flops, scratch=(), scalars=0, fetched=0, place=None, room=32):
    size = sum(array.size * array.dtype.itemsize for array in list(operands) + list(outs))
    count = len(operands) - scalars
    by_kernel = fetched > 0
    places = [pltpu.SMEM] * scalars + [pl.ANY if by_kernel else pltpu.VMEM] * count
    body = kernel
    if by_kernel:
        copies = tuple(
            pltpu.VMEM(array.shape, array.dtype)
            for array in operands[scalars : scalars + fetched]
        )
        scratch = copies + (pltpu.SemaphoreType.DMA((count,)),) + tuple(scratch)

        def body(*refs):
            numbers, sources, refs = refs[:scalars], refs[scalars : scalars + count], refs[scalars + count :]
            results, refs = refs[: len(outs)], refs[len(outs) :]
            held, done, rest = refs[:fetched], refs[fetched], refs[fetched + 1 :]
            targets = list(held)
            if place is not None:
                targets += place(numbers, rest)
            moves = [
                pltpu.make_async_copy(source, target, done.at[i])
                for i, (source, target) in enumerate(zip(sources, targets))
            ]
            for move in moves:
                move.start()
            for move in moves:
                move.wait()
            kernel(*held, *results, *rest)

    return pl.pallas_call(
        body,
        out_shape=outs,
        in_specs=[pl.BlockSpec(memory_space=place_) for place_ in places],
        out_specs=[pl.BlockSpec(memory_space=pltpu.VMEM)] * len(outs),
        scratch_shapes=scratch,
        compiler_params=pltpu.CompilerParams(vmem_limit_bytes=room * 1024 * 1024),
        cost_estimate=pl.CostEstimate(flops=flops, bytes_accessed=size, transcendentals=0),
    )(*operands)


def pack_kernel(w_in, w_mid, w_out, rows):
    features = w_in.shape[1]
    rows[:, :features] = w_in[...].astype(jnp.bfloat16)
    rows[:, features:-features] = w_mid[...]
    rows[:, -features:] = w_out[...].astype(jnp.bfloat16)


def sum_and_spread_kernel(parts, copies):
    total = jnp.sum(parts[...].astype(jnp.float32), axis=0).astype(jnp.bfloat16)
    copies[...] = jnp.broadcast_to(total[None], copies.shape)


def sum_and_square_kernel(place, parts, copies, total):
    total[...] = jnp.sum(parts[...].astype(jnp.float32), axis=0)
    depth = copies.shape[1] // 2
    own = total[pl.ds(pl.multiple_of(place[0] * depth, depth), depth), :]
    squares = jnp.sum(total[...] * total[...], axis=0, keepdims=True)
    both = jnp.concatenate([own, jnp.broadcast_to(squares, own.shape)])
    copies[...] = jnp.broadcast_to(both[None], copies.shape)


def update_kernel(blocks, count, place, parts, w_in, w_out, new_in, new_out):
    depth = parts.shape[1] // 2
    shard = w_in.shape[0]
    squares = jnp.sum(parts[:, depth, :], axis=0, keepdims=True)
    square_sum = jnp.sum(squares, axis=1, keepdims=True)
    scale = LEARN_RATE / jnp.sqrt(square_sum / count + EPSILON)
    for which, (old, new) in enumerate(((w_in, new_in), (w_out, new_out))):
        sides = []
        for half in range(2):
            rows = parts[(which * blocks + place[0]) * 2 + half, :depth, :]
            sides.append(jnp.where(place[1] == 0, rows[:shard], rows[shard:]))
        new[...] = old[...] - scale * jnp.concatenate(sides, axis=1)


def updated(grads, w_in, w_out):
    kinds, blocks, halves, rows, columns = grads.shape
    peers = kinds * blocks * halves
    grads = lax.all_to_all(grads.reshape(peers, rows, columns), AROUND, 0, 0)
    for axis in ("z_lo", "z_hi"):
        count = lax.axis_size(axis)
        (copies,) = on_chip(
            sum_and_spread_kernel,
            (jax.ShapeDtypeStruct((count, rows, columns), jnp.bfloat16),),
            (grads,),
            grads.size,
        )
        grads = lax.all_to_all(copies, axis, 0, 0)
    depth = rows // lax.axis_size(Z)
    (copies,) = on_chip(
        sum_and_square_kernel,
        (jax.ShapeDtypeStruct((peers, 2 * depth, columns), jnp.float32),),
        (lax.axis_index(Z)[None], grads),
        grads.size,
        scratch=(pltpu.VMEM((rows, columns), jnp.float32),),
        scalars=1,
    )
    parts = lax.all_to_all(copies, AROUND, 0, 0)
    place = jnp.stack([lax.axis_index(("x_lo", "y")), lax.axis_index("core")])
    shape = jax.ShapeDtypeStruct(w_in.shape, jnp.float32)
    return on_chip(
        functools.partial(update_kernel, blocks, float(peers * rows * columns)),
        (shape, shape),
        (place, parts, w_in, w_out),
        parts.size,
        scalars=1,
    )


def local(
    state, increment, diffusivity, land_sea, w_in, w_mid, w_out, obs_col, obs_lev, obs_val, obs_prec
):
    _, cells, features = state.shape
    length = cells + 8
    observed = [numbers[None] for numbers in (obs_col, obs_lev, obs_val, obs_prec)]

    def outs(*shapes):
        return tuple(jax.ShapeDtypeStruct(shape, kind) for shape, kind in shapes)

    half = chip_rows(w_in, w_mid, w_out)
    width = half.shape[1]
    half, land_sea = lax.optimization_barrier((half, land_sea))
    fields = (state, increment, diffusivity, land_sea)
    mine, outer = on_chip(
        edge_kernel,
        outs(((24, features), jnp.float32), ((cells, features), jnp.bfloat16)),
        fields + tuple(observed),
        0,
        fetched=8,
        room=56,
    )
    half = spread(half, Z).reshape(-1, width)
    other = swapped(mine, "x_hi")
    outer = swapped_three_apart(outer)
    (own,) = on_chip(
        pack_row_kernel,
        outs(((3 * BLOCK + 16, features), jnp.bfloat16)),
        fields[:3] + (mine, other),
        0,
        fetched=5,
        room=56,
    )
    near = swapped(own, "core")
    half, near, outer = lax.optimization_barrier((half, near, outer))
    half = spread(half, ("x_lo", "y")).reshape(-1, width)
    far = swapped_between_chips(jnp.concatenate([own, near]))
    beyond = swapped(far, "core")
    half, far, beyond = lax.optimization_barrier((half, far, beyond))
    hidden_units, width = half.shape
    blocks = lax.axis_size(("x_lo", "y"))
    halves = lax.axis_size("core")
    narrow = ((cells, features), jnp.float32)
    settled, spreading, grads = on_chip(
        functools.partial(whole_kernel, obs_col.shape[0]),
        outs(
            narrow,
            narrow,
            ((2, blocks, halves, hidden_units // blocks, features // halves), jnp.bfloat16),
        ),
        (lax.axis_index("core")[None], *fields[:3], mine, other, near, far, beyond, outer)
        + (half, swapped(half, "core")),
        40 * cells * hidden_units * (2 * features + hidden_units),
        scratch=(pltpu.VMEM((2, hidden_units, width), jnp.bfloat16),),
        scalars=1,
        fetched=9,
        place=lambda numbers, rest: [
            rest[0].at[numbers[0][0]],
            rest[0].at[1 - numbers[0][0]],
        ],
    )
    w_in_new, w_out_new = updated(grads, w_in, w_out)
    adjoint = settled + neighbour_sum(spreading)
    return adjoint[None], w_in_new, w_out_new


def solution(mesh):
    fine = Mesh(mesh.devices.reshape(FINE_SIZES), FINE_AXES)
    everywhere = TILE + ("x_hi",)
    return jax.shard_map(
        local,
        mesh=fine,
        in_specs=(
            P(TILE, "x_hi", None),
            P(TILE, "x_hi", None),
            P(TILE, "x_hi", None),
            P(TILE, "x_hi"),
            P(TILE, None),
            P(TILE, None),
            P(TILE, None),
            P(everywhere),
            P(everywhere),
            P(everywhere),
            P(everywhere),
        ),
        out_specs=(P(TILE, "x_hi", None), P(TILE, None), P(TILE, None)),
        check_vma=False,
    )
```

```python
import functools

import jax
import jax.numpy as jnp
from jax import lax
from jax.experimental import pallas as pl
from jax.experimental.pallas import tpu as pltpu
from jax.sharding import Mesh
from jax.sharding import PartitionSpec as P

LEARN_RATE = 0.02
EPSILON = 1e-06
CONTRACT_LAST = (((1,), (1,)), ((), ()))
CONTRACT_FIRST = (((0,), (0,)), ((), ()))
FINE_AXES = ("x_lo", "y", "z_hi", "z_lo", "core", "x_hi")
FINE_SIZES = (2, 4, 4, 4, 2, 2)
Z = ("z_hi", "z_lo")
TILE = ("x_lo", "y", "z_hi", "z_lo", "core")
AROUND = ("x_hi", "x_lo", "y", "core")
REACH = 3
BLOCK = 144


def spread(block, axis):
    count = lax.axis_size(axis)
    return lax.all_to_all(jnp.broadcast_to(block[None], (count,) + block.shape), axis, 0, 0)


def chip_rows(w_in, w_mid, w_out):
    columns = 2 * w_in.shape[1] + w_mid.shape[1]
    (rows,) = on_chip(
        pack_kernel,
        (jax.ShapeDtypeStruct((w_in.shape[0], columns), jnp.bfloat16),),
        (w_in, w_mid, w_out),
        0,
        fetched=3,
        room=56,
    )
    rows = lax.all_gather(rows, "core", axis=0, tiled=True)
    width = columns // lax.axis_size(("core", "x_hi"))
    return lax.dynamic_slice_in_dim(rows, lax.axis_index(("core", "x_hi")) * width, width, 1)


def swapped(array, axis):
    return lax.ppermute(array, axis, [(0, 1), (1, 0)])


def swapped_between_chips(array):
    pairs = []
    for row in range(1, lax.axis_size(TILE) - 1, 2):
        pairs += [(row, row + 1), (row + 1, row)]
    return lax.ppermute(array, TILE, pairs)


def swapped_three_apart(array):
    count = lax.axis_size(TILE)
    pairs = [(row, row + 3) for row in range(1, count - 3, 2)]
    return lax.ppermute(array, TILE, pairs + [(after, row) for row, after in pairs])


def neighbour_sum(field):
    far = swapped_between_chips(field)
    edges = swapped(jnp.concatenate([field[:1], field[-1:]]), "x_hi")
    near = swapped(field, "core")
    east = jnp.concatenate([field[1:], edges[:1]])
    west = jnp.concatenate([edges[1:], field[:-1]])
    return far + near + east + west


def adjoint_layers(source, hidden_one, hidden_two, weights):
    features = source.shape[1]
    depth = weights.shape[2] - features
    slope_two = 1.0 - jnp.square(hidden_two.astype(jnp.float32))
    back_two = lax.dot_general(
        source, weights[1, :, depth:], CONTRACT_LAST, preferred_element_type=jnp.float32
    )
    back_two = (slope_two * back_two).astype(jnp.bfloat16)
    back_one = lax.dot_general(
        back_two[:, :depth],
        weights[0, :, features:],
        CONTRACT_LAST,
        preferred_element_type=jnp.float32,
    ) + lax.dot_general(
        back_two[:, depth:],
        weights[1, :, :depth],
        CONTRACT_LAST,
        preferred_element_type=jnp.float32,
    )
    slope_one = 1.0 - jnp.square(hidden_one.astype(jnp.float32))
    return (slope_one * back_one).astype(jnp.bfloat16)


def edge_kernel(state, increment, diffusivity, land_sea, col, lev, val, prec, edges, outer):
    edges[...] = jnp.zeros_like(edges)
    cells = state.shape[1]
    for which, field in enumerate((state, increment, diffusivity)):
        start = 2 * REACH * which
        edges[start : start + REACH] = field[0, :REACH]
        edges[start + REACH : start + 2 * REACH] = field[0, cells - REACH :]
    edges[18:19, :cells] = 0.5 + land_sea[...].astype(jnp.float32)
    count = col.shape[1]
    for row, numbers in enumerate((col, lev, val, prec)):
        edges[19 + row : 20 + row, :count] = numbers[...].astype(jnp.float32)
    outer[...] = (state[0] + increment[0]).astype(jnp.bfloat16)


def ring_gating(mine, other):
    cells = mine.shape[1]
    lane = lax.broadcasted_iota(jnp.int32, (8, cells), 1)
    mine, other = (jnp.broadcast_to(row, (8, cells)) for row in (mine, other))
    other = jnp.where(lane < REACH, other, pltpu.roll(other, 8, 1))
    return jnp.concatenate([mine, other], axis=1)


def ring_field(field, edges, which):
    start = 2 * REACH * which
    return jnp.concatenate(
        [
            field,
            edges[start : start + REACH],
            jnp.zeros((8 - 2 * REACH, field.shape[1]), jnp.float32),
            edges[start + REACH : start + 2 * REACH],
        ]
    )


def pack_row_kernel(state, increment, diffusivity, mine, other, pack):
    cells, features = state.shape[1:]
    for which, field in enumerate((state, increment, diffusivity)):
        ring = ring_field(field[0], other, which)
        ring = jnp.concatenate([ring, jnp.zeros((8, features), jnp.float32)])
        pack[BLOCK * which : BLOCK * (which + 1)] = ring.astype(jnp.bfloat16)
    gating = ring_gating(mine[18:19, :cells], other[18:19, :cells])[:1]
    numbers = mine[21:23, :]
    coarse = numbers.astype(jnp.bfloat16).astype(jnp.float32)
    fine = numbers - coarse
    rest = [gating, mine[19:21, :], coarse, fine, jnp.zeros((16 - 7, features), jnp.float32)]
    pack[3 * BLOCK :] = jnp.concatenate(rest).astype(jnp.bfloat16)


def whole_kernel(
    observations,
    state,
    increment,
    diffusivity,
    mine,
    other,
    near,
    far,
    beyond,
    outer,
    settled_out,
    spreading_out,
    grads,
    weights,
):
    cells, features = state.shape[1:]
    depth = weights.shape[2] - features
    length = cells + 8
    pack = 3 * BLOCK + 16
    square = (length, 2 * cells)
    diagonal = lax.broadcasted_iota(jnp.int32, square, 0) == lax.broadcasted_iota(
        jnp.int32, square, 1
    )

    def column(row):
        return jnp.sum(jnp.where(diagonal, row, 0.0), axis=1, keepdims=True)

    def laplace(field, lat):
        return lat + pltpu.roll(field, 1, 0) + pltpu.roll(field, length - 1, 0) - 4.0 * field

    def unpack(ref, start):
        fields = [
            ref[start + BLOCK * i : start + BLOCK * (i + 1), :].astype(jnp.float32)[:length]
            for i in range(3)
        ]
        rest = ref[start + 3 * BLOCK : start + pack, :].astype(jnp.float32)
        return fields + [column(rest[:1])], rest

    def activate(both):
        hidden = jnp.tanh(both[:length]).astype(jnp.bfloat16).astype(jnp.float32)
        tangent = (1.0 - hidden * hidden) * both[length:]
        return jnp.concatenate([hidden, tangent]).astype(jnp.bfloat16)

    def network(states, tangents):
        stacked = jnp.concatenate([states, tangents]).astype(jnp.bfloat16)
        one = activate(
            lax.dot_general(
                stacked,
                weights[0, :, :features],
                CONTRACT_LAST,
                preferred_element_type=jnp.float32,
            )
        )
        low = activate(jnp.dot(one, weights[0, :, features:], preferred_element_type=jnp.float32))
        high = activate(jnp.dot(one, weights[1, :, :depth], preferred_element_type=jnp.float32))
        out = jnp.dot(
            low, weights[1, :depth, depth:], preferred_element_type=jnp.float32
        ) + jnp.dot(high, weights[1, depth:, depth:], preferred_element_type=jnp.float32)
        saved = (one[:cells], jnp.concatenate([low[:cells], high[:cells]], axis=1), stacked[:cells])
        return out[:length], out[length:], saved

    def observed(final, columns, levels, values, precisions):
        count = columns.shape[1]
        cell_ids = lax.broadcasted_iota(jnp.int32, (length, count), 0).astype(jnp.float32)
        level_ids = lax.broadcasted_iota(jnp.int32, (features, count), 0).astype(jnp.float32)
        pick_cell = (cell_ids == columns).astype(jnp.float32)
        pick_level = (level_ids == levels).astype(jnp.float32)
        at_level = jnp.dot(
            final, pick_level, precision=lax.Precision.HIGHEST, preferred_element_type=jnp.float32
        )
        modelled = jnp.sum(pick_cell * at_level, axis=0, keepdims=True)
        return lax.dot_general(
            pick_cell * (precisions * (modelled - values)),
            pick_level,
            CONTRACT_LAST,
            precision=lax.Precision.HIGHEST,
            preferred_element_type=jnp.float32,
        )

    own = [ring_field(ref[0], other, i) for i, ref in enumerate((state, increment, diffusivity))]
    gate = column(ring_gating(mine[18:19, :cells], other[18:19, :cells])[:1])
    own.append(gate)
    beside, beside_rest = zip(unpack(near, 0), unpack(far, 0))
    second = [unpack(beyond, 0)[0], unpack(far, pack)[0]]
    third = [unpack(beyond, pack)[0]]
    third = [
        third[0][0] + third[0][1],
        jnp.concatenate(
            [outer[...].astype(jnp.float32), jnp.zeros((length - cells, features), jnp.float32)]
        ),
    ]

    def advance(row, lats):
        states, tangents, diffuse, gated = row
        tend, tangent, saved = network(states, tangents)
        return (
            states + diffuse * laplace(states, lats[0]) + gated * tend,
            tangents + diffuse * laplace(tangents, lats[1]) + gated * tangent,
            saved,
        )

    def advance_sum(row, middle, lat):
        tend, tangent, saved = network(row[0], row[1])
        return middle + row[2] * laplace(middle, lat) + row[3] * (tend + tangent), saved

    state_one, increment_one, first = advance(
        own, [beside[0][i] + beside[1][i] for i in range(2)]
    )
    middle_one = state_one + increment_one
    beside_one, beside_middle, second_middle = [], [], []
    for row, next_row, last in zip(beside, second, third):
        one = advance(row, [own[i] + next_row[i] for i in range(2)])[:2]
        beside_one.append(one)
        beside_middle.append(one[0] + one[1])
        next_sum = next_row[0] + next_row[1]
        second_middle.append(
            advance_sum(next_row, next_sum, row[0] + row[1] + last)[0]
        )
    final, late = advance_sum(
        [state_one, increment_one, own[2], gate],
        middle_one,
        beside_middle[0] + beside_middle[1],
    )

    count = observations
    columns = other[19:20, :count]
    columns = jnp.where(
        columns == 0.0, float(cells), jnp.where(columns == cells - 1.0, length - 1.0, -1.0)
    )
    columns = jnp.concatenate([mine[19:20, :count], columns], axis=1)
    chosen = [
        jnp.concatenate([mine[i : i + 1, :count], other[i : i + 1, :count]], axis=1)
        for i in (20, 21, 22)
    ]
    adjoint = observed(final, columns, *chosen)
    around = jnp.zeros_like(adjoint)
    for row, one, middle, next_middle, rest in zip(
        beside, beside_one, beside_middle, second_middle, beside_rest
    ):
        total = advance_sum(
            [one[0], one[1], row[2], row[3]], middle, middle_one + next_middle
        )[0]
        around = around + row[2] * observed(
            total,
            rest[1:2, :cells],
            rest[2:3, :cells],
            rest[3:4, :cells] + rest[5:6, :cells],
            rest[4:5, :cells] + rest[6:7, :cells],
        )
    spreading = own[2] * adjoint
    adjoint_one = (adjoint + laplace(spreading, around))[:cells]
    gate = gate[:cells]
    source_late = (gate * adjoint[:cells]).astype(jnp.bfloat16)
    back_late = adjoint_layers(source_late, late[0], late[1], weights)
    adjoint_one = adjoint_one + jnp.dot(
        back_late, weights[0, :, :features], preferred_element_type=jnp.float32
    )
    spreading = own[2][:cells] * adjoint_one
    spreading_out[...] = spreading
    source = (gate * adjoint_one).astype(jnp.bfloat16)
    back_one = adjoint_layers(source, first[0], first[1], weights)
    settled_out[...] = (
        adjoint_one
        - 4.0 * spreading
        + jnp.dot(back_one, weights[0, :, :features], preferred_element_type=jnp.float32)
    )
    pairs = (
        (back_late, back_one, late[2], first[2]),
        (late[1], first[1], source_late, source),
    )
    _, blocks, halves, rows, width = grads.shape
    for which, (left_late, left, right_late, right) in enumerate(pairs):
        total = lax.dot_general(
            jnp.concatenate([left_late, left]),
            jnp.concatenate([right_late, right]),
            CONTRACT_FIRST,
            preferred_element_type=jnp.float32,
        ).astype(jnp.bfloat16)
        for block in range(blocks):
            for half in range(halves):
                grads[which, block, half] = total[
                    block * rows : (block + 1) * rows, half * width : (half + 1) * width
                ]


def on_chip(kernel, outs, operands, flops, scratch=(), scalars=0, fetched=0, place=None, room=32):
    size = sum(array.size * array.dtype.itemsize for array in list(operands) + list(outs))
    count = len(operands) - scalars
    by_kernel = fetched > 0
    places = [pltpu.SMEM] * scalars + [pl.ANY if by_kernel else pltpu.VMEM] * count
    body = kernel
    if by_kernel:
        copies = tuple(
            pltpu.VMEM(array.shape, array.dtype)
            for array in operands[scalars : scalars + fetched]
        )
        scratch = copies + (pltpu.SemaphoreType.DMA((2 * count,)),) + tuple(scratch)

        def body(*refs):
            numbers, sources, refs = refs[:scalars], refs[scalars : scalars + count], refs[scalars + count :]
            results, refs = refs[: len(outs)], refs[len(outs) :]
            held, done, rest = refs[:fetched], refs[fetched], refs[fetched + 1 :]
            pairs = list(zip(sources, held))
            if place is not None:
                for source, targets in zip(sources[fetched:], place(numbers, rest)):
                    pairs += [(source.at[i], target) for i, target in enumerate(targets)]
            moves = [
                pltpu.make_async_copy(source, target, done.at[i])
                for i, (source, target) in enumerate(pairs)
            ]
            for move in moves:
                move.start()
            for move in moves:
                move.wait()
            kernel(*held, *results, *rest)

    return pl.pallas_call(
        body,
        out_shape=outs,
        in_specs=[pl.BlockSpec(memory_space=place_) for place_ in places],
        out_specs=[pl.BlockSpec(memory_space=pltpu.VMEM)] * len(outs),
        scratch_shapes=scratch,
        compiler_params=pltpu.CompilerParams(vmem_limit_bytes=room * 1024 * 1024),
        cost_estimate=pl.CostEstimate(flops=flops, bytes_accessed=size, transcendentals=0),
    )(*operands)


def pack_kernel(w_in, w_mid, w_out, rows):
    features = w_in.shape[1]
    rows[:, :features] = w_in[...].astype(jnp.bfloat16)
    rows[:, features:-features] = w_mid[...]
    rows[:, -features:] = w_out[...].astype(jnp.bfloat16)


def sum_and_spread_kernel(parts, copies):
    total = jnp.sum(parts[...].astype(jnp.float32), axis=0).astype(jnp.bfloat16)
    copies[...] = jnp.broadcast_to(total[None], copies.shape)


def sum_and_square_kernel(place, parts, copies, total):
    total[...] = jnp.sum(parts[...].astype(jnp.float32), axis=0)
    depth = copies.shape[1] // 2
    own = total[pl.ds(pl.multiple_of(place[0] * depth, depth), depth), :]
    squares = jnp.sum(total[...] * total[...], axis=0, keepdims=True)
    terms = []
    for _ in range(3):
        terms.append(squares.astype(jnp.bfloat16).astype(jnp.float32))
        squares = squares - terms[-1]
    rest = jnp.zeros((depth - len(terms), squares.shape[1]), jnp.float32)
    both = jnp.concatenate([own] + terms + [rest]).astype(jnp.bfloat16)
    copies[...] = jnp.broadcast_to(both[None], copies.shape)


def update_kernel(blocks, count, place, parts_ref, w_in, w_out, new_in, new_out):
    depth = parts_ref.shape[1] // 2
    shard = w_in.shape[0]
    parts = parts_ref[...].astype(jnp.float32)
    squares = jnp.sum(parts, axis=0)[depth:]
    square_sum = jnp.sum(jnp.sum(squares, axis=0, keepdims=True), axis=1, keepdims=True)
    scale = LEARN_RATE / jnp.sqrt(square_sum / count + EPSILON)
    for which, (old, new) in enumerate(((w_in, new_in), (w_out, new_out))):
        sides = []
        for half in range(2):
            rows = parts_ref[(which * blocks + place[0]) * 2 + half].astype(jnp.float32)[:depth]
            sides.append(jnp.where(place[1] == 0, rows[:shard], rows[shard:]))
        new[...] = old[...] - scale * jnp.concatenate(sides, axis=1)


def updated(grads, w_in, w_out):
    kinds, blocks, halves, rows, columns = grads.shape
    peers = kinds * blocks * halves
    grads = lax.all_to_all(grads.reshape(peers, rows, columns), AROUND, 0, 0)
    for axis in ("z_lo", "z_hi"):
        count = lax.axis_size(axis)
        (copies,) = on_chip(
            sum_and_spread_kernel,
            (jax.ShapeDtypeStruct((count, rows, columns), jnp.bfloat16),),
            (grads,),
            grads.size,
        )
        grads = lax.all_to_all(copies, axis, 0, 0)
    depth = rows // lax.axis_size(Z)
    (copies,) = on_chip(
        sum_and_square_kernel,
        (jax.ShapeDtypeStruct((peers, 2 * depth, columns), jnp.bfloat16),),
        (lax.axis_index(Z)[None], grads),
        grads.size,
        scratch=(pltpu.VMEM((rows, columns), jnp.float32),),
        scalars=1,
    )
    parts = lax.all_to_all(copies, AROUND, 0, 0)
    place = jnp.stack([lax.axis_index(("x_lo", "y")), lax.axis_index("core")])
    shape = jax.ShapeDtypeStruct(w_in.shape, jnp.float32)
    return on_chip(
        functools.partial(update_kernel, blocks, float(peers * rows * columns)),
        (shape, shape),
        (place, parts, w_in, w_out),
        parts.size,
        scalars=1,
    )


def local(
    state, increment, diffusivity, land_sea, w_in, w_mid, w_out, obs_col, obs_lev, obs_val, obs_prec
):
    _, cells, features = state.shape
    length = cells + 8
    observed = [numbers[None] for numbers in (obs_col, obs_lev, obs_val, obs_prec)]

    def outs(*shapes):
        return tuple(jax.ShapeDtypeStruct(shape, kind) for shape, kind in shapes)

    half = chip_rows(w_in, w_mid, w_out)
    width = half.shape[1]
    half, land_sea = lax.optimization_barrier((half, land_sea))
    fields = (state, increment, diffusivity, land_sea)
    mine, outer = on_chip(
        edge_kernel,
        outs(((24, features), jnp.float32), ((cells, features), jnp.bfloat16)),
        fields + tuple(observed),
        0,
        fetched=8,
        room=56,
    )
    half = spread(half, Z).reshape(-1, width)
    other = swapped(mine, "x_hi")
    outer = swapped_three_apart(outer)
    (own,) = on_chip(
        pack_row_kernel,
        outs(((3 * BLOCK + 16, features), jnp.bfloat16)),
        fields[:3] + (mine, other),
        0,
        fetched=5,
        room=56,
    )
    near = swapped(own, "core")
    half, near = lax.optimization_barrier((half, near))
    half = spread(half, ("x_hi", "x_lo", "y"))
    far = swapped_between_chips(jnp.concatenate([own, near]))
    far, outer = lax.optimization_barrier((far, outer))
    beyond = swapped(far, "core")
    half, far, beyond = lax.optimization_barrier((half, far, beyond))
    pieces = lax.axis_size("x_hi")
    half = half.reshape(pieces, -1, width)
    hidden_units = half.shape[1]
    blocks = lax.axis_size(("x_lo", "y"))
    halves = lax.axis_size("core")
    narrow = ((cells, features), jnp.float32)
    settled, spreading, grads = on_chip(
        functools.partial(whole_kernel, obs_col.shape[0]),
        outs(
            narrow,
            narrow,
            ((2, blocks, halves, hidden_units // blocks, features // halves), jnp.bfloat16),
        ),
        (lax.axis_index("core")[None], *fields[:3], mine, other, near, far, beyond, outer)
        + (half, swapped(half, "core")),
        40 * cells * hidden_units * (2 * features + hidden_units),
        scratch=(pltpu.VMEM((2, hidden_units, pieces * width), jnp.bfloat16),),
        scalars=1,
        fetched=9,
        place=lambda numbers, rest: [
            [rest[0].at[side, :, pl.ds(piece * width, width)] for piece in range(pieces)]
            for side in (numbers[0][0], 1 - numbers[0][0])
        ],
    )
    w_in_new, w_out_new = updated(grads, w_in, w_out)
    adjoint = settled + neighbour_sum(spreading)
    return adjoint[None], w_in_new, w_out_new


def solution(mesh):
    fine = Mesh(mesh.devices.reshape(FINE_SIZES), FINE_AXES)
    everywhere = TILE + ("x_hi",)
    return jax.shard_map(
        local,
        mesh=fine,
        in_specs=(
            P(TILE, "x_hi", None),
            P(TILE, "x_hi", None),
            P(TILE, "x_hi", None),
            P(TILE, "x_hi"),
            P(TILE, None),
            P(TILE, None),
            P(TILE, None),
            P(everywhere),
            P(everywhere),
            P(everywhere),
            P(everywhere),
        ),
        out_specs=(P(TILE, "x_hi", None), P(TILE, None), P(TILE, None)),
        check_vma=False,
    )
```

```python
import functools

import jax
import jax.numpy as jnp
from jax import lax
from jax.experimental import pallas as pl
from jax.experimental.pallas import tpu as pltpu
from jax.sharding import Mesh
from jax.sharding import PartitionSpec as P

LEARN_RATE = 0.02
EPSILON = 1e-06
CONTRACT_LAST = (((1,), (1,)), ((), ()))
CONTRACT_FIRST = (((0,), (0,)), ((), ()))
FINE_AXES = ("x_lo", "y", "z_hi", "z_lo", "core", "x_hi")
FINE_SIZES = (2, 4, 4, 4, 2, 2)
Z = ("z_hi", "z_lo")
TILE = ("x_lo", "y", "z_hi", "z_lo", "core")
AROUND = ("x_hi", "x_lo", "y", "core")
REACH = 3
BLOCK = 144


def spread(block, axis):
    count = lax.axis_size(axis)
    return lax.all_to_all(jnp.broadcast_to(block[None], (count,) + block.shape), axis, 0, 0)


def swapped(array, axis):
    return lax.ppermute(array, axis, [(0, 1), (1, 0)])


def swapped_between_chips(array):
    pairs = []
    for row in range(1, lax.axis_size(TILE) - 1, 2):
        pairs += [(row, row + 1), (row + 1, row)]
    return lax.ppermute(array, TILE, pairs)


def swapped_three_apart(array):
    count = lax.axis_size(TILE)
    pairs = [(row, row + 3) for row in range(1, count - 3, 2)]
    return lax.ppermute(array, TILE, pairs + [(after, row) for row, after in pairs])


def adjoint_layers(source, hidden_one, hidden_two, weights):
    features = source.shape[1]
    depth = weights.shape[2] - features
    slope_two = 1.0 - jnp.square(hidden_two.astype(jnp.float32))
    back_two = lax.dot_general(
        source, weights[1, :, depth:], CONTRACT_LAST, preferred_element_type=jnp.float32
    )
    back_two = (slope_two * back_two).astype(jnp.bfloat16)
    back_one = lax.dot_general(
        back_two[:, :depth],
        weights[0, :, features:],
        CONTRACT_LAST,
        preferred_element_type=jnp.float32,
    ) + lax.dot_general(
        back_two[:, depth:],
        weights[1, :, :depth],
        CONTRACT_LAST,
        preferred_element_type=jnp.float32,
    )
    slope_one = 1.0 - jnp.square(hidden_one.astype(jnp.float32))
    return (slope_one * back_one).astype(jnp.bfloat16)


def first_kernel(
    state,
    increment,
    diffusivity,
    land_sea,
    col,
    lev,
    val,
    prec,
    w_in,
    w_mid,
    w_out,
    rows,
    edges,
    outer,
):
    features = w_in.shape[1]
    rows[:, :features] = w_in[...].astype(jnp.bfloat16)
    rows[:, features:-features] = w_mid[...]
    rows[:, -features:] = w_out[...].astype(jnp.bfloat16)
    edges[...] = jnp.zeros_like(edges)
    cells = state.shape[1]
    for which, field in enumerate((state, increment, diffusivity)):
        start = 2 * REACH * which
        edges[start : start + REACH] = field[0, :REACH]
        edges[start + REACH : start + 2 * REACH] = field[0, cells - REACH :]
    edges[18:19, :cells] = 0.5 + land_sea[...].astype(jnp.float32)
    count = col.shape[1]
    for row, numbers in enumerate((col, lev, val, prec)):
        edges[19 + row : 20 + row, :count] = numbers[...].astype(jnp.float32)
    outer[...] = (state[0] + increment[0]).astype(jnp.bfloat16)


def ring_gating(mine, other):
    cells = mine.shape[1]
    lane = lax.broadcasted_iota(jnp.int32, (8, cells), 1)
    mine, other = (jnp.broadcast_to(row, (8, cells)) for row in (mine, other))
    other = jnp.where(lane < REACH, other, pltpu.roll(other, 8, 1))
    return jnp.concatenate([mine, other], axis=1)


def ring_field(field, edges, which):
    start = 2 * REACH * which
    return jnp.concatenate(
        [
            field,
            edges[start : start + REACH],
            jnp.zeros((8 - 2 * REACH, field.shape[1]), jnp.float32),
            edges[start + REACH : start + 2 * REACH],
        ]
    )


def pack_row_kernel(mine, other, state, increment, diffusivity, pack):
    cells, features = state.shape[1:]
    for which, field in enumerate((state, increment, diffusivity)):
        ring = ring_field(field[0], other, which)
        ring = jnp.concatenate([ring, jnp.zeros((8, features), jnp.float32)])
        pack[BLOCK * which : BLOCK * (which + 1)] = ring.astype(jnp.bfloat16)
    gating = ring_gating(mine[18:19, :cells], other[18:19, :cells])[:1]
    numbers = mine[21:23, :]
    coarse = numbers.astype(jnp.bfloat16).astype(jnp.float32)
    fine = numbers - coarse
    rest = [gating, mine[19:21, :], coarse, fine, jnp.zeros((16 - 7, features), jnp.float32)]
    pack[3 * BLOCK :] = jnp.concatenate(rest).astype(jnp.bfloat16)


def whole_kernel(
    observations,
    state,
    increment,
    diffusivity,
    mine,
    other,
    near,
    far,
    beyond,
    outer,
    settled_out,
    spreading_out,
    ends_out,
    grads,
    weights,
):
    cells, features = state.shape[1:]
    depth = weights.shape[2] - features
    length = cells + 8
    pack = 3 * BLOCK + 16
    square = (length, 2 * cells)
    diagonal = lax.broadcasted_iota(jnp.int32, square, 0) == lax.broadcasted_iota(
        jnp.int32, square, 1
    )

    def column(row):
        return jnp.sum(jnp.where(diagonal, row, 0.0), axis=1, keepdims=True)

    def laplace(field, lat):
        return lat + pltpu.roll(field, 1, 0) + pltpu.roll(field, length - 1, 0) - 4.0 * field

    def unpack(ref, start):
        fields = [
            ref[start + BLOCK * i : start + BLOCK * (i + 1), :].astype(jnp.float32)[:length]
            for i in range(3)
        ]
        rest = ref[start + 3 * BLOCK : start + pack, :].astype(jnp.float32)
        return fields + [column(rest[:1])], rest

    def activate(both):
        hidden = jnp.tanh(both[:length]).astype(jnp.bfloat16).astype(jnp.float32)
        tangent = (1.0 - hidden * hidden) * both[length:]
        return jnp.concatenate([hidden, tangent]).astype(jnp.bfloat16)

    def network(states, tangents):
        stacked = jnp.concatenate([states, tangents]).astype(jnp.bfloat16)
        one = activate(
            lax.dot_general(
                stacked,
                weights[0, :, :features],
                CONTRACT_LAST,
                preferred_element_type=jnp.float32,
            )
        )
        low = activate(jnp.dot(one, weights[0, :, features:], preferred_element_type=jnp.float32))
        high = activate(jnp.dot(one, weights[1, :, :depth], preferred_element_type=jnp.float32))
        out = jnp.dot(
            low, weights[1, :depth, depth:], preferred_element_type=jnp.float32
        ) + jnp.dot(high, weights[1, depth:, depth:], preferred_element_type=jnp.float32)
        saved = (one[:cells], jnp.concatenate([low[:cells], high[:cells]], axis=1), stacked[:cells])
        return out[:length], out[length:], saved

    def observed(final, columns, levels, values, precisions):
        count = columns.shape[1]
        cell_ids = lax.broadcasted_iota(jnp.int32, (length, count), 0).astype(jnp.float32)
        level_ids = lax.broadcasted_iota(jnp.int32, (features, count), 0).astype(jnp.float32)
        pick_cell = (cell_ids == columns).astype(jnp.float32)
        pick_level = (level_ids == levels).astype(jnp.float32)
        at_level = jnp.dot(
            final, pick_level, precision=lax.Precision.HIGHEST, preferred_element_type=jnp.float32
        )
        modelled = jnp.sum(pick_cell * at_level, axis=0, keepdims=True)
        return lax.dot_general(
            pick_cell * (precisions * (modelled - values)),
            pick_level,
            CONTRACT_LAST,
            precision=lax.Precision.HIGHEST,
            preferred_element_type=jnp.float32,
        )

    own = [ring_field(ref[0], other, i) for i, ref in enumerate((state, increment, diffusivity))]
    gate = column(ring_gating(mine[18:19, :cells], other[18:19, :cells])[:1])
    own.append(gate)
    beside, beside_rest = zip(unpack(near, 0), unpack(far, 0))
    second = [unpack(beyond, 0)[0], unpack(far, pack)[0]]
    third = [unpack(beyond, pack)[0]]
    third = [
        third[0][0] + third[0][1],
        jnp.concatenate(
            [outer[...].astype(jnp.float32), jnp.zeros((length - cells, features), jnp.float32)]
        ),
    ]

    def advance(row, lats):
        states, tangents, diffuse, gated = row
        tend, tangent, saved = network(states, tangents)
        return (
            states + diffuse * laplace(states, lats[0]) + gated * tend,
            tangents + diffuse * laplace(tangents, lats[1]) + gated * tangent,
            saved,
        )

    def advance_sum(row, middle, lat):
        tend, tangent, saved = network(row[0], row[1])
        return middle + row[2] * laplace(middle, lat) + row[3] * (tend + tangent), saved

    state_one, increment_one, first = advance(
        own, [beside[0][i] + beside[1][i] for i in range(2)]
    )
    middle_one = state_one + increment_one
    beside_one, beside_middle, second_middle = [], [], []
    for row, next_row, last in zip(beside, second, third):
        one = advance(row, [own[i] + next_row[i] for i in range(2)])[:2]
        beside_one.append(one)
        beside_middle.append(one[0] + one[1])
        next_sum = next_row[0] + next_row[1]
        second_middle.append(
            advance_sum(next_row, next_sum, row[0] + row[1] + last)[0]
        )
    final, late = advance_sum(
        [state_one, increment_one, own[2], gate],
        middle_one,
        beside_middle[0] + beside_middle[1],
    )

    count = observations
    columns = other[19:20, :count]
    columns = jnp.where(
        columns == 0.0, float(cells), jnp.where(columns == cells - 1.0, length - 1.0, -1.0)
    )
    columns = jnp.concatenate([mine[19:20, :count], columns], axis=1)
    chosen = [
        jnp.concatenate([mine[i : i + 1, :count], other[i : i + 1, :count]], axis=1)
        for i in (20, 21, 22)
    ]
    adjoint = observed(final, columns, *chosen)
    around = jnp.zeros_like(adjoint)
    for row, one, middle, next_middle, rest in zip(
        beside, beside_one, beside_middle, second_middle, beside_rest
    ):
        total = advance_sum(
            [one[0], one[1], row[2], row[3]], middle, middle_one + next_middle
        )[0]
        around = around + row[2] * observed(
            total,
            rest[1:2, :cells],
            rest[2:3, :cells],
            rest[3:4, :cells] + rest[5:6, :cells],
            rest[4:5, :cells] + rest[6:7, :cells],
        )
    spreading = own[2] * adjoint
    adjoint_one = (adjoint + laplace(spreading, around))[:cells]
    gate = gate[:cells]
    source_late = (gate * adjoint[:cells]).astype(jnp.bfloat16)
    back_late = adjoint_layers(source_late, late[0], late[1], weights)
    adjoint_one = adjoint_one + jnp.dot(
        back_late, weights[0, :, :features], preferred_element_type=jnp.float32
    )
    spreading = own[2][:cells] * adjoint_one
    spreading_out[...] = spreading
    ends_out[...] = jnp.concatenate([spreading[:1], spreading[cells - 7 :]])
    source = (gate * adjoint_one).astype(jnp.bfloat16)
    back_one = adjoint_layers(source, first[0], first[1], weights)
    settled_out[...] = (
        adjoint_one
        - 4.0 * spreading
        + jnp.dot(back_one, weights[0, :, :features], preferred_element_type=jnp.float32)
    )
    pairs = (
        (back_late, back_one, late[2], first[2]),
        (late[1], first[1], source_late, source),
    )
    _, blocks, halves, rows, width = grads.shape
    for which, (left_late, left, right_late, right) in enumerate(pairs):
        total = lax.dot_general(
            jnp.concatenate([left_late, left]),
            jnp.concatenate([right_late, right]),
            CONTRACT_FIRST,
            preferred_element_type=jnp.float32,
        ).astype(jnp.bfloat16)
        for block in range(blocks):
            for half in range(halves):
                grads[which, block, half] = total[
                    block * rows : (block + 1) * rows, half * width : (half + 1) * width
                ]


def on_chip(kernel, outs, operands, flops, scratch=(), scalars=0, direct=0, fetched=0, place=None, room=32):
    size = sum(array.size * array.dtype.itemsize for array in list(operands) + list(outs))
    by_kernel = fetched > 0
    before = scalars + (direct if by_kernel else len(operands) - scalars)
    count = len(operands) - before
    places = [pltpu.SMEM] * scalars + [pltpu.VMEM] * (before - scalars) + [pl.ANY] * count
    body = kernel
    if by_kernel:
        copies = tuple(
            pltpu.VMEM(array.shape, array.dtype)
            for array in operands[before : before + fetched]
        )
        scratch = copies + (pltpu.SemaphoreType.DMA((count,)),) + tuple(scratch)

        def body(*refs):
            numbers, ready = refs[:scalars], refs[scalars:before]
            sources, refs = refs[before : before + count], refs[before + count :]
            results, refs = refs[: len(outs)], refs[len(outs) :]
            held, done, rest = refs[:fetched], refs[fetched], refs[fetched + 1 :]
            targets = list(held)
            if place is not None:
                targets += place(numbers, rest)
            moves = [
                pltpu.make_async_copy(source, target, done.at[i])
                for i, (source, target) in enumerate(zip(sources, targets))
            ]
            for move in moves:
                move.start()
            for move in moves:
                move.wait()
            kernel(*ready, *held, *results, *rest)

    return pl.pallas_call(
        body,
        out_shape=outs,
        in_specs=[pl.BlockSpec(memory_space=place_) for place_ in places],
        out_specs=[pl.BlockSpec(memory_space=pltpu.VMEM)] * len(outs),
        scratch_shapes=scratch,
        compiler_params=pltpu.CompilerParams(vmem_limit_bytes=room * 1024 * 1024),
        cost_estimate=pl.CostEstimate(flops=flops, bytes_accessed=size, transcendentals=0),
    )(*operands)


def sum_and_spread_kernel(parts, copies):
    total = jnp.sum(parts[...].astype(jnp.float32), axis=0).astype(jnp.bfloat16)
    copies[...] = jnp.broadcast_to(total[None], copies.shape)


def sum_and_square_kernel(place, parts, copies, total):
    total[...] = jnp.sum(parts[...].astype(jnp.float32), axis=0)
    depth = copies.shape[1] // 2
    own = total[pl.ds(pl.multiple_of(place[0] * depth, depth), depth), :]
    squares = jnp.sum(total[...] * total[...], axis=0, keepdims=True)
    terms = []
    for _ in range(3):
        terms.append(squares.astype(jnp.bfloat16).astype(jnp.float32))
        squares = squares - terms[-1]
    rest = jnp.zeros((depth - len(terms), squares.shape[1]), jnp.float32)
    both = jnp.concatenate([own] + terms + [rest]).astype(jnp.bfloat16)
    copies[...] = jnp.broadcast_to(both[None], copies.shape)


def update_kernel(blocks, count, place, parts_ref, w_in, w_out, new_in, new_out):
    depth = parts_ref.shape[1] // 2
    shard = w_in.shape[0]
    parts = parts_ref[...].astype(jnp.float32)
    squares = jnp.sum(parts, axis=0)[depth:]
    square_sum = jnp.sum(jnp.sum(squares, axis=0, keepdims=True), axis=1, keepdims=True)
    scale = LEARN_RATE / jnp.sqrt(square_sum / count + EPSILON)
    for which, (old, new) in enumerate(((w_in, new_in), (w_out, new_out))):
        sides = []
        for half in range(2):
            rows = parts_ref[(which * blocks + place[0]) * 2 + half].astype(jnp.float32)[:depth]
            sides.append(jnp.where(place[1] == 0, rows[:shard], rows[shard:]))
        new[...] = old[...] - scale * jnp.concatenate(sides, axis=1)


def updated(grads, w_in, w_out, arriving):
    kinds, blocks, halves, rows, columns = grads.shape
    peers = kinds * blocks * halves
    grads = lax.all_to_all(grads.reshape(peers, rows, columns), AROUND, 0, 0)
    grads, arriving = lax.optimization_barrier((grads, arriving))
    for axis in ("z_lo", "z_hi"):
        count = lax.axis_size(axis)
        (copies,) = on_chip(
            sum_and_spread_kernel,
            (jax.ShapeDtypeStruct((count, rows, columns), jnp.bfloat16),),
            (grads,),
            grads.size,
        )
        grads = lax.all_to_all(copies, axis, 0, 0)
    depth = rows // lax.axis_size(Z)
    (copies,) = on_chip(
        sum_and_square_kernel,
        (jax.ShapeDtypeStruct((peers, 2 * depth, columns), jnp.bfloat16),),
        (lax.axis_index(Z)[None], grads),
        grads.size,
        scratch=(pltpu.VMEM((rows, columns), jnp.float32),),
        scalars=1,
    )
    parts = lax.all_to_all(copies, AROUND, 0, 0)
    place = jnp.stack([lax.axis_index(("x_lo", "y")), lax.axis_index("core")])
    shape = jax.ShapeDtypeStruct(w_in.shape, jnp.float32)
    new_in, new_out = on_chip(
        functools.partial(update_kernel, blocks, float(peers * rows * columns)),
        (shape, shape),
        (place, parts, w_in, w_out),
        parts.size,
        scalars=1,
    )
    return new_in, new_out, arriving


def local(
    state, increment, diffusivity, land_sea, w_in, w_mid, w_out, obs_col, obs_lev, obs_val, obs_prec
):
    _, cells, features = state.shape
    length = cells + 8
    observed = [numbers[None] for numbers in (obs_col, obs_lev, obs_val, obs_prec)]

    def outs(*shapes):
        return tuple(jax.ShapeDtypeStruct(shape, kind) for shape, kind in shapes)

    columns = 2 * features + w_mid.shape[1]
    width = columns // lax.axis_size("core")
    rows, mine, outer = on_chip(
        first_kernel,
        outs(
            ((w_in.shape[0], columns), jnp.bfloat16),
            ((24, features), jnp.float32),
            ((cells, features), jnp.bfloat16),
        ),
        (state, increment, diffusivity, land_sea, *observed, w_in, w_mid, w_out),
        0,
        fetched=11,
        room=56,
    )
    rows = lax.all_gather(rows, "core", axis=0, tiled=True)
    half = lax.dynamic_slice_in_dim(rows, lax.axis_index("core") * width, width, 1)
    half, mine, outer = lax.optimization_barrier((half, mine, outer))
    half = spread(half, Z).reshape(-1, width)
    other = swapped(mine, "x_hi")
    outer = swapped_three_apart(outer)
    (own,) = on_chip(
        pack_row_kernel,
        outs(((3 * BLOCK + 16, features), jnp.bfloat16)),
        (mine, other, state, increment, diffusivity),
        0,
        direct=2,
        fetched=3,
        room=56,
    )
    near = swapped(own, "core")
    half, near = lax.optimization_barrier((half, near))
    half = spread(half, ("x_lo", "y")).reshape(-1, width)
    far = swapped_between_chips(jnp.concatenate([own, near]))
    far, outer = lax.optimization_barrier((far, outer))
    beyond = swapped(far, "core")
    half, far, beyond = lax.optimization_barrier((half, far, beyond))
    hidden_units = half.shape[0]
    blocks = lax.axis_size(("x_lo", "y"))
    halves = lax.axis_size("core")
    narrow = ((cells, features), jnp.float32)
    settled, spreading, ends, grads = on_chip(
        functools.partial(whole_kernel, obs_col.shape[0]),
        outs(
            narrow,
            narrow,
            ((8, features), jnp.float32),
            ((2, blocks, halves, hidden_units // blocks, features // halves), jnp.bfloat16),
        ),
        (lax.axis_index("core")[None], state, increment, diffusivity, mine, other, near, far, beyond, outer)
        + (half, swapped(half, "core")),
        40 * cells * hidden_units * (2 * features + hidden_units),
        scratch=(pltpu.VMEM((2, hidden_units, width), jnp.bfloat16),),
        scalars=1,
        fetched=9,
        place=lambda numbers, rest: [
            rest[0].at[numbers[0][0]],
            rest[0].at[1 - numbers[0][0]],
        ],
    )
    arriving = (
        swapped_between_chips(spreading),
        swapped(spreading, "core"),
        swapped(ends, "x_hi"),
    )
    w_in_new, w_out_new, (far, near, ends) = updated(grads, w_in, w_out, arriving)
    east = jnp.concatenate([spreading[1:], ends[:1]])
    west = jnp.concatenate([ends[-1:], spreading[:-1]])
    adjoint = settled + (far + near + east + west)
    return adjoint[None], w_in_new, w_out_new


def solution(mesh):
    fine = Mesh(mesh.devices.reshape(FINE_SIZES), FINE_AXES)
    everywhere = TILE + ("x_hi",)
    return jax.shard_map(
        local,
        mesh=fine,
        in_specs=(
            P(TILE, "x_hi", None),
            P(TILE, "x_hi", None),
            P(TILE, "x_hi", None),
            P(TILE, "x_hi"),
            P(TILE, None),
            P(TILE, None),
            P(TILE, None),
            P(everywhere),
            P(everywhere),
            P(everywhere),
            P(everywhere),
        ),
        out_specs=(P(TILE, "x_hi", None), P(TILE, None), P(TILE, None)),
        check_vma=False,
    )
```

```python
import functools

import jax
import jax.numpy as jnp
from jax import lax
from jax.experimental import pallas as pl
from jax.experimental.pallas import tpu as pltpu
from jax.sharding import Mesh
from jax.sharding import PartitionSpec as P

LEARN_RATE = 0.02
EPSILON = 1e-06
CONTRACT_LAST = (((1,), (1,)), ((), ()))
CONTRACT_FIRST = (((0,), (0,)), ((), ()))
FINE_AXES = ("x_lo", "y", "z_hi", "z_lo", "core", "x_hi")
FINE_SIZES = (2, 4, 4, 4, 2, 2)
Z = ("z_hi", "z_lo")
TILE = ("x_lo", "y", "z_hi", "z_lo", "core")
AROUND = ("x_hi", "x_lo", "y", "core")
REACH = 3
BLOCK = 144


def spread(block, axis):
    count = lax.axis_size(axis)
    return lax.all_to_all(jnp.broadcast_to(block[None], (count,) + block.shape), axis, 0, 0)


def swapped(array, axis):
    return lax.ppermute(array, axis, [(0, 1), (1, 0)])


def swapped_between_chips(array):
    pairs = []
    for row in range(1, lax.axis_size(TILE) - 1, 2):
        pairs += [(row, row + 1), (row + 1, row)]
    return lax.ppermute(array, TILE, pairs)


def swapped_three_apart(array):
    count = lax.axis_size(TILE)
    pairs = [(row, row + 3) for row in range(1, count - 3, 2)]
    return lax.ppermute(array, TILE, pairs + [(after, row) for row, after in pairs])


def adjoint_layers(source, hidden_one, hidden_two, weights):
    features = source.shape[1]
    depth = weights.shape[2] - features
    slope_two = 1.0 - jnp.square(hidden_two.astype(jnp.float32))
    back_two = lax.dot_general(
        source, weights[1, :, depth:], CONTRACT_LAST, preferred_element_type=jnp.float32
    )
    back_two = (slope_two * back_two).astype(jnp.bfloat16)
    back_one = lax.dot_general(
        back_two[:, :depth],
        weights[0, :, features:],
        CONTRACT_LAST,
        preferred_element_type=jnp.float32,
    ) + lax.dot_general(
        back_two[:, depth:],
        weights[1, :, :depth],
        CONTRACT_LAST,
        preferred_element_type=jnp.float32,
    )
    slope_one = 1.0 - jnp.square(hidden_one.astype(jnp.float32))
    return (slope_one * back_one).astype(jnp.bfloat16)


def first_kernel(
    state,
    increment,
    diffusivity,
    land_sea,
    col,
    lev,
    val,
    prec,
    w_in,
    w_mid,
    w_out,
    rows,
    edges,
    outer,
):
    features = w_in.shape[1]
    rows[:, :features] = w_in[...].astype(jnp.bfloat16)
    rows[:, features:-features] = w_mid[...]
    rows[:, -features:] = w_out[...].astype(jnp.bfloat16)
    edges[...] = jnp.zeros_like(edges)
    cells = state.shape[1]
    for which, field in enumerate((state, increment, diffusivity)):
        start = 2 * REACH * which
        edges[start : start + REACH] = field[0, :REACH]
        edges[start + REACH : start + 2 * REACH] = field[0, cells - REACH :]
    edges[18:19, :cells] = 0.5 + land_sea[...].astype(jnp.float32)
    count = col.shape[1]
    for row, numbers in enumerate((col, lev, val, prec)):
        edges[19 + row : 20 + row, :count] = numbers[...].astype(jnp.float32)
    outer[...] = (state[0] + increment[0]).astype(jnp.bfloat16)


def ring_gating(mine, other):
    cells = mine.shape[1]
    lane = lax.broadcasted_iota(jnp.int32, (8, cells), 1)
    mine, other = (jnp.broadcast_to(row, (8, cells)) for row in (mine, other))
    other = jnp.where(lane < REACH, other, pltpu.roll(other, 8, 1))
    return jnp.concatenate([mine, other], axis=1)


def ring_field(field, edges, which):
    start = 2 * REACH * which
    return jnp.concatenate(
        [
            field,
            edges[start : start + REACH],
            jnp.zeros((8 - 2 * REACH, field.shape[1]), jnp.float32),
            edges[start + REACH : start + 2 * REACH],
        ]
    )


def pack_fields_kernel(state, increment, diffusivity, pack):
    cells = state.shape[1]
    for which, field in enumerate((state, increment, diffusivity)):
        pack[BLOCK * which : BLOCK * which + cells] = field[0].astype(jnp.bfloat16)


def pack_edges_kernel(fields, mine, other, pack):
    features = fields.shape[1]
    cells = BLOCK - 16
    for which in range(3):
        base, start = BLOCK * which, 2 * REACH * which
        pack[base : base + cells] = fields[base : base + cells]
        edges = [
            other[start : start + REACH],
            jnp.zeros((8 - 2 * REACH, features), jnp.float32),
            other[start + REACH : start + 2 * REACH],
            jnp.zeros((8, features), jnp.float32),
        ]
        pack[base + cells : base + BLOCK] = jnp.concatenate(edges).astype(jnp.bfloat16)
    gating = ring_gating(mine[18:19, :cells], other[18:19, :cells])[:1]
    numbers = mine[21:23, :]
    coarse = numbers.astype(jnp.bfloat16).astype(jnp.float32)
    fine = numbers - coarse
    rest = [gating, mine[19:21, :], coarse, fine, jnp.zeros((16 - 7, features), jnp.float32)]
    pack[3 * BLOCK :] = jnp.concatenate(rest).astype(jnp.bfloat16)


def whole_kernel(
    observations,
    core,
    state,
    increment,
    diffusivity,
    mine,
    other,
    near,
    far,
    beyond,
    outer,
    settled_out,
    spreading_out,
    ends_out,
    kept,
    given,
    weights,
):
    cells, features = state.shape[1:]
    depth = weights.shape[2] - features
    length = cells + 8
    pack = 3 * BLOCK + 16
    square = (length, 2 * cells)
    diagonal = lax.broadcasted_iota(jnp.int32, square, 0) == lax.broadcasted_iota(
        jnp.int32, square, 1
    )

    def column(row):
        return jnp.sum(jnp.where(diagonal, row, 0.0), axis=1, keepdims=True)

    def laplace(field, lat):
        return lat + pltpu.roll(field, 1, 0) + pltpu.roll(field, length - 1, 0) - 4.0 * field

    def unpack(ref, start):
        fields = [
            ref[start + BLOCK * i : start + BLOCK * (i + 1), :].astype(jnp.float32)[:length]
            for i in range(3)
        ]
        rest = ref[start + 3 * BLOCK : start + pack, :].astype(jnp.float32)
        return fields + [column(rest[:1])], rest

    def activate(both):
        middle = both.shape[0] // 2
        hidden = jnp.tanh(both[:middle]).astype(jnp.bfloat16).astype(jnp.float32)
        tangent = (1.0 - hidden * hidden) * both[middle:]
        return jnp.concatenate([hidden, tangent]).astype(jnp.bfloat16)

    def networks(rows):
        stacked = jnp.concatenate([row[0] for row in rows] + [row[1] for row in rows])
        stacked = stacked.astype(jnp.bfloat16)
        one = activate(
            lax.dot_general(
                stacked,
                weights[0, :, :features],
                CONTRACT_LAST,
                preferred_element_type=jnp.float32,
            )
        )
        low = activate(jnp.dot(one, weights[0, :, features:], preferred_element_type=jnp.float32))
        high = activate(jnp.dot(one, weights[1, :, :depth], preferred_element_type=jnp.float32))
        out = jnp.dot(
            low, weights[1, :depth, depth:], preferred_element_type=jnp.float32
        ) + jnp.dot(high, weights[1, depth:, depth:], preferred_element_type=jnp.float32)
        saved = (one[:cells], jnp.concatenate([low[:cells], high[:cells]], axis=1), stacked[:cells])
        outs = [out[i * length : (i + 1) * length] for i in range(2 * len(rows))]
        return list(zip(outs[: len(rows)], outs[len(rows) :])), saved

    def observed(final, columns, levels, values, precisions):
        count = columns.shape[1]
        cell_ids = lax.broadcasted_iota(jnp.int32, (length, count), 0).astype(jnp.float32)
        level_ids = lax.broadcasted_iota(jnp.int32, (features, count), 0).astype(jnp.float32)
        pick_cell = (cell_ids == columns).astype(jnp.float32)
        pick_level = (level_ids == levels).astype(jnp.float32)
        at_level = jnp.dot(
            final, pick_level, precision=lax.Precision.HIGHEST, preferred_element_type=jnp.float32
        )
        modelled = jnp.sum(pick_cell * at_level, axis=0, keepdims=True)
        return lax.dot_general(
            pick_cell * (precisions * (modelled - values)),
            pick_level,
            CONTRACT_LAST,
            precision=lax.Precision.HIGHEST,
            preferred_element_type=jnp.float32,
        )

    own = [ring_field(ref[0], other, i) for i, ref in enumerate((state, increment, diffusivity))]
    gate = column(ring_gating(mine[18:19, :cells], other[18:19, :cells])[:1])
    own.append(gate)
    beside, beside_rest = zip(unpack(near, 0), unpack(far, 0))
    second = [unpack(beyond, 0)[0], unpack(far, pack)[0]]
    third = [unpack(beyond, pack)[0]]
    third = [
        third[0][0] + third[0][1],
        jnp.concatenate(
            [outer[...].astype(jnp.float32), jnp.zeros((length - cells, features), jnp.float32)]
        ),
    ]

    def advance(row, lats, moved):
        states, tangents, diffuse, gated = row
        return (
            states + diffuse * laplace(states, lats[0]) + gated * moved[0],
            tangents + diffuse * laplace(tangents, lats[1]) + gated * moved[1],
        )

    def advance_sum(row, middle, lat, moved):
        return middle + row[2] * laplace(middle, lat) + row[3] * (moved[0] + moved[1])

    groups = ((0,), (1, 2), (3, 4))
    all_rows = [own] + list(beside) + second
    moved = []
    first = None
    for group in groups:
        got, saved = networks([all_rows[i] for i in group])
        moved += got
        first = saved if first is None else first
    state_one, increment_one = advance(
        own, [beside[0][i] + beside[1][i] for i in range(2)], moved[0]
    )
    middle_one = state_one + increment_one
    beside_one, beside_middle, second_middle = [], [], []
    for i, (row, next_row, last) in enumerate(zip(beside, second, third)):
        one = advance(row, [own[j] + next_row[j] for j in range(2)], moved[1 + i])
        beside_one.append(one)
        beside_middle.append(one[0] + one[1])
        next_sum = next_row[0] + next_row[1]
        second_middle.append(advance_sum(next_row, next_sum, row[0] + row[1] + last, moved[3 + i]))
    all_rows = [(state_one, increment_one)] + beside_one
    late, moved = None, []
    for group in ((0,), (1, 2)):
        got, saved = networks([all_rows[i] for i in group])
        moved += got
        late = saved if late is None else late
    final = advance_sum(own, middle_one, beside_middle[0] + beside_middle[1], moved[0])
    count = observations
    columns = other[19:20, :count]
    columns = jnp.where(
        columns == 0.0, float(cells), jnp.where(columns == cells - 1.0, length - 1.0, -1.0)
    )
    columns = jnp.concatenate([mine[19:20, :count], columns], axis=1)
    chosen = [
        jnp.concatenate([mine[i : i + 1, :count], other[i : i + 1, :count]], axis=1)
        for i in (20, 21, 22)
    ]
    adjoint = observed(final, columns, *chosen)
    around = jnp.zeros_like(adjoint)
    for row, middle, next_middle, rest, moves in zip(
        beside, beside_middle, second_middle, beside_rest, moved[1:]
    ):
        total = advance_sum(row, middle, middle_one + next_middle, moves)
        around = around + row[2] * observed(
            total,
            rest[1:2, :cells],
            rest[2:3, :cells],
            rest[3:4, :cells] + rest[5:6, :cells],
            rest[4:5, :cells] + rest[6:7, :cells],
        )
    spreading = own[2] * adjoint
    adjoint_one = (adjoint + laplace(spreading, around))[:cells]
    gate = gate[:cells]
    source_late = (gate * adjoint[:cells]).astype(jnp.bfloat16)
    back_late = adjoint_layers(source_late, late[0], late[1], weights)
    adjoint_one = adjoint_one + jnp.dot(
        back_late, weights[0, :, :features], preferred_element_type=jnp.float32
    )
    spreading = own[2][:cells] * adjoint_one
    spreading_out[...] = spreading
    ends_out[...] = jnp.concatenate([spreading[:1], spreading[cells - 7 :]])
    source = (gate * adjoint_one).astype(jnp.bfloat16)
    back_one = adjoint_layers(source, first[0], first[1], weights)
    settled_out[...] = (
        adjoint_one
        - 4.0 * spreading
        + jnp.dot(back_one, weights[0, :, :features], preferred_element_type=jnp.float32)
    )
    first_core = core[0] == 0
    lefts = [jnp.concatenate([back_late, back_one]), jnp.concatenate([late[1], first[1]])]
    rights = [jnp.concatenate([late[2], first[2]]), jnp.concatenate([source_late, source])]
    halves, blocks, rows, width = kept.shape
    for out, which in ((given, 1), (kept, 0)):
        total = lax.dot_general(
            jnp.where(first_core, lefts[which], lefts[1 - which]),
            jnp.where(first_core, rights[which], rights[1 - which]),
            CONTRACT_FIRST,
            preferred_element_type=jnp.float32,
        ).astype(jnp.bfloat16)
        for half in range(halves):
            for block in range(blocks):
                out[half, block] = total[
                    block * rows : (block + 1) * rows, half * width : (half + 1) * width
                ]


def on_chip(kernel, outs, operands, flops, scratch=(), scalars=0, direct=0, fetched=0, place=None, room=32):
    size = sum(array.size * array.dtype.itemsize for array in list(operands) + list(outs))
    by_kernel = fetched > 0 or place is not None
    before = scalars + (direct if by_kernel else len(operands) - scalars)
    count = len(operands) - before
    places = [pltpu.SMEM] * scalars + [pltpu.VMEM] * (before - scalars) + [pl.ANY] * count
    body = kernel
    if by_kernel:
        copies = tuple(
            pltpu.VMEM(array.shape, array.dtype)
            for array in operands[before : before + fetched]
        )
        scratch = copies + (pltpu.SemaphoreType.DMA((count,)),) + tuple(scratch)

        def body(*refs):
            numbers, ready = refs[:scalars], refs[scalars:before]
            sources, refs = refs[before : before + count], refs[before + count :]
            results, refs = refs[: len(outs)], refs[len(outs) :]
            held, done, rest = refs[:fetched], refs[fetched], refs[fetched + 1 :]
            targets = list(held)
            if place is not None:
                targets += place(numbers, rest)
            moves = [
                pltpu.make_async_copy(source, target, done.at[i])
                for i, (source, target) in enumerate(zip(sources, targets))
            ]
            for move in moves:
                move.start()
            for move in moves:
                move.wait()
            kernel(*numbers, *ready, *held, *results, *rest)

    return pl.pallas_call(
        body,
        out_shape=outs,
        in_specs=[pl.BlockSpec(memory_space=place_) for place_ in places],
        out_specs=[pl.BlockSpec(memory_space=pltpu.VMEM)] * len(outs),
        scratch_shapes=scratch,
        compiler_params=pltpu.CompilerParams(vmem_limit_bytes=room * 1024 * 1024),
        cost_estimate=pl.CostEstimate(flops=flops, bytes_accessed=size, transcendentals=0),
    )(*operands)


def sum_and_spread_kernel(parts, copies):
    total = jnp.sum(parts[...].astype(jnp.float32), axis=0).astype(jnp.bfloat16)
    copies[...] = jnp.broadcast_to(total[None], copies.shape)


def sum_and_square_kernel(place, parts, copies, total):
    total[...] = jnp.sum(parts[...].astype(jnp.float32), axis=0)
    depth = copies.shape[1] // 2
    own = total[pl.ds(pl.multiple_of(place[0] * depth, depth), depth), :]
    squares = jnp.sum(total[...] * total[...], axis=0, keepdims=True)
    terms = []
    for _ in range(3):
        terms.append(squares.astype(jnp.bfloat16).astype(jnp.float32))
        squares = squares - terms[-1]
    rest = jnp.zeros((depth - len(terms), squares.shape[1]), jnp.float32)
    both = jnp.concatenate([own] + terms + [rest]).astype(jnp.bfloat16)
    copies[...] = jnp.broadcast_to(both[None], copies.shape)


def update_kernel(blocks, count, place, parts_ref, w_in, w_out, new_in, new_out):
    depth = parts_ref.shape[1] // 2
    shard = w_in.shape[0]
    parts = parts_ref[...].astype(jnp.float32)
    squares = jnp.sum(parts, axis=0)[depth:]
    square_sum = jnp.sum(jnp.sum(squares, axis=0, keepdims=True), axis=1, keepdims=True)
    scale = LEARN_RATE / jnp.sqrt(square_sum / count + EPSILON)
    for which, (old, new) in enumerate(((w_in, new_in), (w_out, new_out))):
        sides = []
        for half in range(2):
            rows = parts_ref[(half * blocks + place[0]) * 2 + which].astype(jnp.float32)[:depth]
            sides.append(jnp.where(place[1] == 0, rows[:shard], rows[shard:]))
        new[...] = old[...] - scale * jnp.concatenate(sides, axis=1)


def add_kernel(left, right, total):
    total[...] = (left[...].astype(jnp.float32) + right[...].astype(jnp.float32)).astype(
        jnp.bfloat16
    )


def updated(kept, given, w_in, w_out, arriving):
    halves, blocks, rows, columns = kept.shape
    peers = halves * blocks
    (grads,) = on_chip(
        add_kernel,
        (jax.ShapeDtypeStruct((peers, rows, columns), jnp.bfloat16),),
        (kept.reshape(peers, rows, columns), swapped(given, "core").reshape(peers, rows, columns)),
        kept.size,
    )
    grads = lax.all_to_all(grads, AROUND[:-1], 0, 0)
    grads, arriving = lax.optimization_barrier((grads, arriving))
    for axis in ("z_lo", "z_hi"):
        count = lax.axis_size(axis)
        (copies,) = on_chip(
            sum_and_spread_kernel,
            (jax.ShapeDtypeStruct((count, rows, columns), jnp.bfloat16),),
            (grads,),
            grads.size,
        )
        grads = lax.all_to_all(copies, axis, 0, 0)
    peers *= lax.axis_size("core")
    depth = rows // lax.axis_size(Z)
    (copies,) = on_chip(
        sum_and_square_kernel,
        (jax.ShapeDtypeStruct((peers, 2 * depth, columns), jnp.bfloat16),),
        (lax.axis_index(Z)[None], grads),
        grads.size,
        scratch=(pltpu.VMEM((rows, columns), jnp.float32),),
        scalars=1,
    )
    parts = lax.all_to_all(copies, AROUND, 0, 0)
    place = jnp.stack([lax.axis_index(("x_lo", "y")), lax.axis_index("core")])
    shape = jax.ShapeDtypeStruct(w_in.shape, jnp.float32)
    new_in, new_out = on_chip(
        functools.partial(update_kernel, blocks, float(peers * rows * columns)),
        (shape, shape),
        (place, parts, w_in, w_out),
        parts.size,
        scalars=1,
    )
    return new_in, new_out, arriving


def local(
    state, increment, diffusivity, land_sea, w_in, w_mid, w_out, obs_col, obs_lev, obs_val, obs_prec
):
    _, cells, features = state.shape
    length = cells + 8
    observed = [numbers[None] for numbers in (obs_col, obs_lev, obs_val, obs_prec)]

    def outs(*shapes):
        return tuple(jax.ShapeDtypeStruct(shape, kind) for shape, kind in shapes)

    columns = 2 * features + w_mid.shape[1]
    width = columns // lax.axis_size("core")
    rows, mine, outer = on_chip(
        first_kernel,
        outs(
            ((w_in.shape[0], columns), jnp.bfloat16),
            ((24, features), jnp.float32),
            ((cells, features), jnp.bfloat16),
        ),
        (state, increment, diffusivity, land_sea, *observed, w_in, w_mid, w_out),
        0,
        fetched=11,
        room=56,
    )
    rows = lax.all_gather(rows, "core", axis=0, tiled=True)
    half = lax.dynamic_slice_in_dim(rows, lax.axis_index("core") * width, width, 1)
    fields = (state, increment, diffusivity)
    half, mine, outer, fields = lax.optimization_barrier((half, mine, outer, fields))
    half = spread(half, Z).reshape(-1, width)
    other = swapped(mine, "x_hi")
    outer = swapped_three_apart(outer)
    packed = outs(((3 * BLOCK + 16, features), jnp.bfloat16))
    (packs,) = on_chip(pack_fields_kernel, packed, fields, 0, fetched=3)
    (own,) = on_chip(pack_edges_kernel, packed, (packs, mine, other), 0)
    near = swapped(own, "core")
    half, near = lax.optimization_barrier((half, near))
    half = spread(half, ("x_lo", "y")).reshape(-1, width)
    far = swapped_between_chips(jnp.concatenate([own, near]))
    far, outer = lax.optimization_barrier((far, outer))
    beyond = swapped(far, "core")
    half, far, beyond = lax.optimization_barrier((half, far, beyond))
    hidden_units = half.shape[0]
    blocks = lax.axis_size(("x_lo", "y"))
    halves = lax.axis_size("x_hi")
    part = ((halves, blocks, hidden_units // blocks, features // halves), jnp.bfloat16)
    narrow = ((cells, features), jnp.float32)
    settled, spreading, ends, kept, given = on_chip(
        functools.partial(whole_kernel, obs_col.shape[0]),
        outs(
            narrow,
            narrow,
            ((8, features), jnp.float32),
            part,
            part,
        ),
        (lax.axis_index("core")[None], state, increment, diffusivity, mine, other, near, far, beyond, outer)
        + (half, swapped(half, "core")),
        40 * cells * hidden_units * (2 * features + hidden_units),
        scratch=(pltpu.VMEM((2, hidden_units, width), jnp.bfloat16),),
        scalars=1,
        direct=9,
        fetched=0,
        place=lambda numbers, rest: [
            rest[0].at[numbers[0][0]],
            rest[0].at[1 - numbers[0][0]],
        ],
    )
    arriving = (
        swapped_between_chips(spreading),
        swapped(spreading, "core"),
        swapped(ends, "x_hi"),
    )
    w_in_new, w_out_new, (far, near, ends) = updated(kept, given, w_in, w_out, arriving)
    east = jnp.concatenate([spreading[1:], ends[:1]])
    west = jnp.concatenate([ends[-1:], spreading[:-1]])
    adjoint = settled + (far + near + east + west)
    return adjoint[None], w_in_new, w_out_new


def solution(mesh):
    fine = Mesh(mesh.devices.reshape(FINE_SIZES), FINE_AXES)
    everywhere = TILE + ("x_hi",)
    return jax.shard_map(
        local,
        mesh=fine,
        in_specs=(
            P(TILE, "x_hi", None),
            P(TILE, "x_hi", None),
            P(TILE, "x_hi", None),
            P(TILE, "x_hi"),
            P(TILE, None),
            P(TILE, None),
            P(TILE, None),
            P(everywhere),
            P(everywhere),
            P(everywhere),
            P(everywhere),
        ),
        out_specs=(P(TILE, "x_hi", None), P(TILE, None), P(TILE, None)),
        check_vma=False,
    )
```

```python
import functools

import jax
import jax.numpy as jnp
from jax import lax
from jax.experimental import pallas as pl
from jax.experimental.pallas import tpu as pltpu
from jax.sharding import Mesh
from jax.sharding import PartitionSpec as P

LEARN_RATE = 0.02
EPSILON = 1e-06
CONTRACT_LAST = (((1,), (1,)), ((), ()))
CONTRACT_FIRST = (((0,), (0,)), ((), ()))
FINE_AXES = ("x_lo", "y", "z_hi", "z_lo", "core", "x_hi")
FINE_SIZES = (2, 4, 4, 4, 2, 2)
Z = ("z_hi", "z_lo")
TILE = ("x_lo", "y", "z_hi", "z_lo", "core")
AROUND = ("x_hi", "x_lo", "y", "core")
REACH = 3
BLOCK = 144


def spread(block, axis):
    count = lax.axis_size(axis)
    return lax.all_to_all(jnp.broadcast_to(block[None], (count,) + block.shape), axis, 0, 0)


def swapped(array, axis):
    return lax.ppermute(array, axis, [(0, 1), (1, 0)])


def swapped_between_chips(array):
    pairs = []
    for row in range(1, lax.axis_size(TILE) - 1, 2):
        pairs += [(row, row + 1), (row + 1, row)]
    return lax.ppermute(array, TILE, pairs)


def swapped_three_apart(array):
    count = lax.axis_size(TILE)
    pairs = [(row, row + 3) for row in range(1, count - 3, 2)]
    return lax.ppermute(array, TILE, pairs + [(after, row) for row, after in pairs])


def adjoint_layers(source, hidden_one, hidden_two, weights):
    features = source.shape[1]
    depth = weights.shape[2] - features
    slope_two = 1.0 - jnp.square(hidden_two.astype(jnp.float32))
    back_two = lax.dot_general(
        source, weights[1, :, depth:], CONTRACT_LAST, preferred_element_type=jnp.float32
    )
    back_two = (slope_two * back_two).astype(jnp.bfloat16)
    back_one = lax.dot_general(
        back_two[:, :depth],
        weights[0, :, features:],
        CONTRACT_LAST,
        preferred_element_type=jnp.float32,
    ) + lax.dot_general(
        back_two[:, depth:],
        weights[1, :, :depth],
        CONTRACT_LAST,
        preferred_element_type=jnp.float32,
    )
    slope_one = 1.0 - jnp.square(hidden_one.astype(jnp.float32))
    return (slope_one * back_one).astype(jnp.bfloat16)


def first_kernel(
    state,
    increment,
    diffusivity,
    land_sea,
    col,
    lev,
    val,
    prec,
    w_in,
    w_mid,
    w_out,
    rows,
    edges,
    outer,
):
    features = w_in.shape[1]
    rows[:, :features] = w_in[...].astype(jnp.bfloat16)
    rows[:, features:-features] = w_mid[...]
    rows[:, -features:] = w_out[...].astype(jnp.bfloat16)
    edges[...] = jnp.zeros_like(edges)
    cells = state.shape[1]
    for which, field in enumerate((state, increment, diffusivity)):
        start = 2 * REACH * which
        edges[start : start + REACH] = field[0, :REACH]
        edges[start + REACH : start + 2 * REACH] = field[0, cells - REACH :]
    edges[18:19, :cells] = 0.5 + land_sea[...].astype(jnp.float32)
    count = col.shape[1]
    for row, numbers in enumerate((col, lev, val, prec)):
        edges[19 + row : 20 + row, :count] = numbers[...].astype(jnp.float32)
    outer[...] = (state[0] + increment[0]).astype(jnp.bfloat16)


def ring_gating(mine, other):
    cells = mine.shape[1]
    lane = lax.broadcasted_iota(jnp.int32, (8, cells), 1)
    mine, other = (jnp.broadcast_to(row, (8, cells)) for row in (mine, other))
    other = jnp.where(lane < REACH, other, pltpu.roll(other, 8, 1))
    return jnp.concatenate([mine, other], axis=1)


def ring_field(field, edges, which):
    start = 2 * REACH * which
    return jnp.concatenate(
        [
            field,
            edges[start : start + REACH],
            jnp.zeros((8 - 2 * REACH, field.shape[1]), jnp.float32),
            edges[start + REACH : start + 2 * REACH],
        ]
    )


def pack_fields_kernel(state, increment, diffusivity, pack):
    cells = state.shape[1]
    for which, field in enumerate((state, increment, diffusivity)):
        pack[BLOCK * which : BLOCK * which + cells] = field[0].astype(jnp.bfloat16)


def pack_edges_kernel(fields, mine, other, pack):
    features = fields.shape[1]
    cells = BLOCK - 16
    for which in range(3):
        base, start = BLOCK * which, 2 * REACH * which
        pack[base : base + cells] = fields[base : base + cells]
        edges = [
            other[start : start + REACH],
            jnp.zeros((8 - 2 * REACH, features), jnp.float32),
            other[start + REACH : start + 2 * REACH],
            jnp.zeros((8, features), jnp.float32),
        ]
        pack[base + cells : base + BLOCK] = jnp.concatenate(edges).astype(jnp.bfloat16)
    gating = ring_gating(mine[18:19, :cells], other[18:19, :cells])[:1]
    numbers = mine[21:23, :]
    coarse = numbers.astype(jnp.bfloat16).astype(jnp.float32)
    fine = numbers - coarse
    rest = [gating, mine[19:21, :], coarse, fine, jnp.zeros((16 - 7, features), jnp.float32)]
    pack[3 * BLOCK :] = jnp.concatenate(rest).astype(jnp.bfloat16)


def whole_kernel(
    observations,
    core,
    state,
    increment,
    diffusivity,
    mine,
    other,
    near,
    far,
    beyond,
    outer,
    settled_out,
    spreading_out,
    ends_out,
    kept,
    given,
    weights,
):
    cells, features = state.shape[1:]
    depth = weights.shape[2] - features
    length = cells + 8
    pack = 3 * BLOCK + 16
    square = (length, 2 * cells)
    diagonal = lax.broadcasted_iota(jnp.int32, square, 0) == lax.broadcasted_iota(
        jnp.int32, square, 1
    )

    def column(row):
        return jnp.sum(jnp.where(diagonal, row, 0.0), axis=1, keepdims=True)

    def laplace(field, lat):
        return lat + pltpu.roll(field, 1, 0) + pltpu.roll(field, length - 1, 0) - 4.0 * field

    def unpack(ref, start):
        fields = [
            ref[start + BLOCK * i : start + BLOCK * (i + 1), :].astype(jnp.float32)[:length]
            for i in range(3)
        ]
        rest = ref[start + 3 * BLOCK : start + pack, :].astype(jnp.float32)
        return fields + [column(rest[:1])], rest

    def activate(both):
        middle = both.shape[0] // 2
        hidden = jnp.tanh(both[:middle]).astype(jnp.bfloat16).astype(jnp.float32)
        tangent = (1.0 - hidden * hidden) * both[middle:]
        return jnp.concatenate([hidden, tangent]).astype(jnp.bfloat16)

    def networks(rows):
        stacked = jnp.concatenate([row[0] for row in rows] + [row[1] for row in rows])
        stacked = stacked.astype(jnp.bfloat16)
        one = activate(
            lax.dot_general(
                stacked,
                weights[0, :, :features],
                CONTRACT_LAST,
                preferred_element_type=jnp.float32,
            )
        )
        low = activate(jnp.dot(one, weights[0, :, features:], preferred_element_type=jnp.float32))
        high = activate(jnp.dot(one, weights[1, :, :depth], preferred_element_type=jnp.float32))
        out = jnp.dot(
            low, weights[1, :depth, depth:], preferred_element_type=jnp.float32
        ) + jnp.dot(high, weights[1, depth:, depth:], preferred_element_type=jnp.float32)
        saved = (one[:cells], jnp.concatenate([low[:cells], high[:cells]], axis=1), stacked[:cells])
        outs = [out[i * length : (i + 1) * length] for i in range(2 * len(rows))]
        return list(zip(outs[: len(rows)], outs[len(rows) :])), saved

    def observed(final, columns, levels, values, precisions):
        count = columns.shape[1]
        cell_ids = lax.broadcasted_iota(jnp.int32, (length, count), 0).astype(jnp.float32)
        level_ids = lax.broadcasted_iota(jnp.int32, (features, count), 0).astype(jnp.float32)
        pick_cell = (cell_ids == columns).astype(jnp.float32)
        pick_level = (level_ids == levels).astype(jnp.float32)
        at_level = jnp.dot(
            final, pick_level, precision=lax.Precision.HIGHEST, preferred_element_type=jnp.float32
        )
        modelled = jnp.sum(pick_cell * at_level, axis=0, keepdims=True)
        return lax.dot_general(
            pick_cell * (precisions * (modelled - values)),
            pick_level,
            CONTRACT_LAST,
            precision=lax.Precision.HIGHEST,
            preferred_element_type=jnp.float32,
        )

    own = [ring_field(ref[0], other, i) for i, ref in enumerate((state, increment, diffusivity))]
    gate = column(ring_gating(mine[18:19, :cells], other[18:19, :cells])[:1])
    own.append(gate)
    beside, beside_rest = zip(unpack(near, 0), unpack(far, 0))
    second = [unpack(beyond, 0)[0], unpack(far, pack)[0]]
    third = [unpack(beyond, pack)[0]]
    third = [
        third[0][0] + third[0][1],
        jnp.concatenate(
            [outer[...].astype(jnp.float32), jnp.zeros((length - cells, features), jnp.float32)]
        ),
    ]

    def advance(row, lats, moved):
        states, tangents, diffuse, gated = row
        return (
            states + diffuse * laplace(states, lats[0]) + gated * moved[0],
            tangents + diffuse * laplace(tangents, lats[1]) + gated * moved[1],
        )

    def advance_sum(row, middle, lat, moved):
        return middle + row[2] * laplace(middle, lat) + row[3] * (moved[0] + moved[1])

    groups = ((0,), (1, 2), (3, 4))
    all_rows = [own] + list(beside) + second
    moved = []
    first = None
    for group in groups:
        got, saved = networks([all_rows[i] for i in group])
        moved += got
        first = saved if first is None else first
    state_one, increment_one = advance(
        own, [beside[0][i] + beside[1][i] for i in range(2)], moved[0]
    )
    middle_one = state_one + increment_one
    beside_one, beside_middle, second_middle = [], [], []
    for i, (row, next_row, last) in enumerate(zip(beside, second, third)):
        one = advance(row, [own[j] + next_row[j] for j in range(2)], moved[1 + i])
        beside_one.append(one)
        beside_middle.append(one[0] + one[1])
        next_sum = next_row[0] + next_row[1]
        second_middle.append(advance_sum(next_row, next_sum, row[0] + row[1] + last, moved[3 + i]))
    all_rows = [(state_one, increment_one)] + beside_one
    late, moved = None, []
    for group in ((0,), (1, 2)):
        got, saved = networks([all_rows[i] for i in group])
        moved += got
        late = saved if late is None else late
    final = advance_sum(own, middle_one, beside_middle[0] + beside_middle[1], moved[0])
    count = observations
    columns = other[19:20, :count]
    columns = jnp.where(
        columns == 0.0, float(cells), jnp.where(columns == cells - 1.0, length - 1.0, -1.0)
    )
    columns = jnp.concatenate([mine[19:20, :count], columns], axis=1)
    chosen = [
        jnp.concatenate([mine[i : i + 1, :count], other[i : i + 1, :count]], axis=1)
        for i in (20, 21, 22)
    ]
    adjoint = observed(final, columns, *chosen)
    around = jnp.zeros_like(adjoint)
    for row, middle, next_middle, rest, moves in zip(
        beside, beside_middle, second_middle, beside_rest, moved[1:]
    ):
        total = advance_sum(row, middle, middle_one + next_middle, moves)
        around = around + row[2] * observed(
            total,
            rest[1:2, :cells],
            rest[2:3, :cells],
            rest[3:4, :cells] + rest[5:6, :cells],
            rest[4:5, :cells] + rest[6:7, :cells],
        )
    spreading = own[2] * adjoint
    adjoint_one = (adjoint + laplace(spreading, around))[:cells]
    gate = gate[:cells]
    source_late = (gate * adjoint[:cells]).astype(jnp.bfloat16)
    back_late = adjoint_layers(source_late, late[0], late[1], weights)
    adjoint_one = adjoint_one + jnp.dot(
        back_late, weights[0, :, :features], preferred_element_type=jnp.float32
    )
    spreading = own[2][:cells] * adjoint_one
    spreading_out[...] = spreading
    ends_out[...] = jnp.concatenate([spreading[:1], spreading[cells - 7 :]])
    source = (gate * adjoint_one).astype(jnp.bfloat16)
    back_one = adjoint_layers(source, first[0], first[1], weights)
    settled_out[...] = (
        adjoint_one
        - 4.0 * spreading
        + jnp.dot(back_one, weights[0, :, :features], preferred_element_type=jnp.float32)
    )
    first_core = core[0] == 0
    lefts = [jnp.concatenate([back_late, back_one]), jnp.concatenate([late[1], first[1]])]
    rights = [jnp.concatenate([late[2], first[2]]), jnp.concatenate([source_late, source])]
    halves, blocks, rows, width = kept.shape
    for out, which in ((given, 1), (kept, 0)):
        total = lax.dot_general(
            jnp.where(first_core, lefts[which], lefts[1 - which]),
            jnp.where(first_core, rights[which], rights[1 - which]),
            CONTRACT_FIRST,
            preferred_element_type=jnp.float32,
        ).astype(jnp.bfloat16)
        for half in range(halves):
            for block in range(blocks):
                out[half, block] = total[
                    block * rows : (block + 1) * rows, half * width : (half + 1) * width
                ]


def on_chip(kernel, outs, operands, flops, scratch=(), scalars=0, direct=0, fetched=0, place=None, room=32):
    size = sum(array.size * array.dtype.itemsize for array in list(operands) + list(outs))
    by_kernel = fetched > 0 or place is not None
    before = scalars + (direct if by_kernel else len(operands) - scalars)
    count = len(operands) - before
    places = [pltpu.SMEM] * scalars + [pltpu.VMEM] * (before - scalars) + [pl.ANY] * count
    body = kernel
    if by_kernel:
        copies = tuple(
            pltpu.VMEM(array.shape, array.dtype)
            for array in operands[before : before + fetched]
        )
        scratch = copies + (pltpu.SemaphoreType.DMA((count,)),) + tuple(scratch)

        def body(*refs):
            numbers, ready = refs[:scalars], refs[scalars:before]
            sources, refs = refs[before : before + count], refs[before + count :]
            results, refs = refs[: len(outs)], refs[len(outs) :]
            held, done, rest = refs[:fetched], refs[fetched], refs[fetched + 1 :]
            targets = list(held)
            if place is not None:
                targets += place(numbers, rest)
            moves = [
                pltpu.make_async_copy(source, target, done.at[i])
                for i, (source, target) in enumerate(zip(sources, targets))
            ]
            for move in moves:
                move.start()
            for move in moves:
                move.wait()
            kernel(*numbers, *ready, *held, *results, *rest)

    return pl.pallas_call(
        body,
        out_shape=outs,
        in_specs=[pl.BlockSpec(memory_space=place_) for place_ in places],
        out_specs=[pl.BlockSpec(memory_space=pltpu.VMEM)] * len(outs),
        scratch_shapes=scratch,
        compiler_params=pltpu.CompilerParams(vmem_limit_bytes=room * 1024 * 1024),
        cost_estimate=pl.CostEstimate(flops=flops, bytes_accessed=size, transcendentals=0),
    )(*operands)


def sum_and_spread_kernel(parts, copies):
    total = jnp.sum(parts[...].astype(jnp.float32), axis=0).astype(jnp.bfloat16)
    copies[...] = jnp.broadcast_to(total[None], copies.shape)


def sum_and_square_kernel(place, parts, copies, total):
    total[...] = jnp.sum(parts[...].astype(jnp.float32), axis=0)
    depth = copies.shape[1] // 2
    own = total[pl.ds(pl.multiple_of(place[0] * depth, depth), depth), :]
    squares = jnp.sum(total[...] * total[...], axis=0, keepdims=True)
    terms = []
    for _ in range(3):
        terms.append(squares.astype(jnp.bfloat16).astype(jnp.float32))
        squares = squares - terms[-1]
    rest = jnp.zeros((depth - len(terms), squares.shape[1]), jnp.float32)
    both = jnp.concatenate([own] + terms + [rest]).astype(jnp.bfloat16)
    copies[...] = jnp.broadcast_to(both[None], copies.shape)


def update_kernel(blocks, count, place, parts_ref, w_in, w_out, new_in, new_out):
    depth = parts_ref.shape[1] // 2
    shard = w_in.shape[0]
    parts = parts_ref[...].astype(jnp.float32)
    squares = jnp.sum(parts, axis=0)[depth:]
    square_sum = jnp.sum(jnp.sum(squares, axis=0, keepdims=True), axis=1, keepdims=True)
    scale = LEARN_RATE / jnp.sqrt(square_sum / count + EPSILON)
    for which, (old, new) in enumerate(((w_in, new_in), (w_out, new_out))):
        sides = []
        for half in range(2):
            rows = parts_ref[(half * blocks + place[0]) * 2 + which].astype(jnp.float32)[:depth]
            sides.append(jnp.where(place[1] == 0, rows[:shard], rows[shard:]))
        new[...] = old[...] - scale * jnp.concatenate(sides, axis=1)


def add_kernel(left, right, total):
    total[...] = (left[...].astype(jnp.float32) + right[...].astype(jnp.float32)).astype(
        jnp.bfloat16
    )


def updated(kept, given, w_in, w_out, arriving, later):
    halves, blocks, rows, columns = kept.shape
    peers = halves * blocks
    (grads,) = on_chip(
        add_kernel,
        (jax.ShapeDtypeStruct((peers, rows, columns), jnp.bfloat16),),
        (kept.reshape(peers, rows, columns), swapped(given, "core").reshape(peers, rows, columns)),
        kept.size,
    )
    grads = lax.all_to_all(grads, AROUND[:-1], 0, 0)
    grads, arriving = lax.optimization_barrier((grads, arriving))
    for axis in ("z_lo", "z_hi"):
        count = lax.axis_size(axis)
        (copies,) = on_chip(
            sum_and_spread_kernel,
            (jax.ShapeDtypeStruct((count, rows, columns), jnp.bfloat16),),
            (grads,),
            grads.size,
        )
        grads = lax.all_to_all(copies, axis, 0, 0)
        if axis == "z_lo":
            grads, later = lax.optimization_barrier((grads, later))
    peers *= lax.axis_size("core")
    depth = rows // lax.axis_size(Z)
    (copies,) = on_chip(
        sum_and_square_kernel,
        (jax.ShapeDtypeStruct((peers, 2 * depth, columns), jnp.bfloat16),),
        (lax.axis_index(Z)[None], grads),
        grads.size,
        scratch=(pltpu.VMEM((rows, columns), jnp.float32),),
        scalars=1,
    )
    parts = lax.all_to_all(copies, AROUND, 0, 0)
    place = jnp.stack([lax.axis_index(("x_lo", "y")), lax.axis_index("core")])
    shape = jax.ShapeDtypeStruct(w_in.shape, jnp.float32)
    new_in, new_out = on_chip(
        functools.partial(update_kernel, blocks, float(peers * rows * columns)),
        (shape, shape),
        (place, parts, w_in, w_out),
        parts.size,
        scalars=1,
    )
    return new_in, new_out, arriving, later


def local(
    state, increment, diffusivity, land_sea, w_in, w_mid, w_out, obs_col, obs_lev, obs_val, obs_prec
):
    _, cells, features = state.shape
    length = cells + 8
    observed = [numbers[None] for numbers in (obs_col, obs_lev, obs_val, obs_prec)]

    def outs(*shapes):
        return tuple(jax.ShapeDtypeStruct(shape, kind) for shape, kind in shapes)

    columns = 2 * features + w_mid.shape[1]
    width = columns // lax.axis_size("core")
    rows, mine, outer = on_chip(
        first_kernel,
        outs(
            ((w_in.shape[0], columns), jnp.bfloat16),
            ((24, features), jnp.float32),
            ((cells, features), jnp.bfloat16),
        ),
        (state, increment, diffusivity, land_sea, *observed, w_in, w_mid, w_out),
        0,
        fetched=11,
        room=56,
    )
    rows = lax.all_gather(rows, "core", axis=0, tiled=True)
    half = lax.dynamic_slice_in_dim(rows, lax.axis_index("core") * width, width, 1)
    fields = (state, increment, diffusivity)
    half, mine, outer, fields = lax.optimization_barrier((half, mine, outer, fields))
    half = spread(half, Z).reshape(-1, width)
    other = swapped(mine, "x_hi")
    outer = swapped_three_apart(outer)
    packed = outs(((3 * BLOCK + 16, features), jnp.bfloat16))
    (packs,) = on_chip(pack_fields_kernel, packed, fields, 0, fetched=3)
    (own,) = on_chip(pack_edges_kernel, packed, (packs, mine, other), 0)
    near = swapped(own, "core")
    half, near = lax.optimization_barrier((half, near))
    half = spread(half, ("x_lo", "y")).reshape(-1, width)
    far = swapped_between_chips(jnp.concatenate([own, near]))
    far, outer = lax.optimization_barrier((far, outer))
    beyond = swapped(far, "core")
    half, far, beyond = lax.optimization_barrier((half, far, beyond))
    hidden_units = half.shape[0]
    blocks = lax.axis_size(("x_lo", "y"))
    halves = lax.axis_size("x_hi")
    part = ((halves, blocks, hidden_units // blocks, features // halves), jnp.bfloat16)
    narrow = ((cells, features), jnp.float32)
    settled, spreading, ends, kept, given = on_chip(
        functools.partial(whole_kernel, obs_col.shape[0]),
        outs(
            narrow,
            narrow,
            ((8, features), jnp.float32),
            part,
            part,
        ),
        (lax.axis_index("core")[None], state, increment, diffusivity, mine, other, near, far, beyond, outer)
        + (half, swapped(half, "core")),
        40 * cells * hidden_units * (2 * features + hidden_units),
        scratch=(pltpu.VMEM((2, hidden_units, width), jnp.bfloat16),),
        scalars=1,
        direct=9,
        fetched=0,
        place=lambda numbers, rest: [
            rest[0].at[numbers[0][0]],
            rest[0].at[1 - numbers[0][0]],
        ],
    )
    w_in_new, w_out_new, ends, spreading = updated(
        kept, given, w_in, w_out, swapped(ends, "x_hi"), spreading
    )
    far = swapped_between_chips(spreading)
    near = swapped(spreading, "core")
    east = jnp.concatenate([spreading[1:], ends[:1]])
    west = jnp.concatenate([ends[-1:], spreading[:-1]])
    adjoint = settled + (far + near + east + west)
    return adjoint[None], w_in_new, w_out_new


def solution(mesh):
    fine = Mesh(mesh.devices.reshape(FINE_SIZES), FINE_AXES)
    everywhere = TILE + ("x_hi",)
    return jax.shard_map(
        local,
        mesh=fine,
        in_specs=(
            P(TILE, "x_hi", None),
            P(TILE, "x_hi", None),
            P(TILE, "x_hi", None),
            P(TILE, "x_hi"),
            P(TILE, None),
            P(TILE, None),
            P(TILE, None),
            P(everywhere),
            P(everywhere),
            P(everywhere),
            P(everywhere),
        ),
        out_specs=(P(TILE, "x_hi", None), P(TILE, None), P(TILE, None)),
        check_vma=False,
    )
```

```python
import functools

import jax
import jax.numpy as jnp
from jax import lax
from jax.experimental import pallas as pl
from jax.experimental.pallas import tpu as pltpu
from jax.sharding import Mesh
from jax.sharding import PartitionSpec as P

LEARN_RATE = 0.02
EPSILON = 1e-06
CONTRACT_LAST = (((1,), (1,)), ((), ()))
CONTRACT_FIRST = (((0,), (0,)), ((), ()))
FINE_AXES = ("x_lo", "y", "z_hi", "z_lo", "core", "x_hi")
FINE_SIZES = (2, 4, 4, 4, 2, 2)
Z = ("z_hi", "z_lo")
TILE = ("x_lo", "y", "z_hi", "z_lo", "core")
AROUND = ("x_hi", "x_lo", "y", "core")
REACH = 3
BLOCK = 144


def spread(block, axis):
    count = lax.axis_size(axis)
    return lax.all_to_all(jnp.broadcast_to(block[None], (count,) + block.shape), axis, 0, 0)


def swapped(array, axis):
    return lax.ppermute(array, axis, [(0, 1), (1, 0)])


def swapped_between_chips(array):
    pairs = []
    for row in range(1, lax.axis_size(TILE) - 1, 2):
        pairs += [(row, row + 1), (row + 1, row)]
    return lax.ppermute(array, TILE, pairs)


def swapped_three_apart(array):
    count = lax.axis_size(TILE)
    pairs = [(row, row + 3) for row in range(1, count - 3, 2)]
    return lax.ppermute(array, TILE, pairs + [(after, row) for row, after in pairs])


def adjoint_layers(source, hidden_one, hidden_two, weights):
    features = source.shape[1]
    depth = weights.shape[2] - features
    slope_two = 1.0 - jnp.square(hidden_two.astype(jnp.float32))
    back_two = lax.dot_general(
        source, weights[1, :, depth:], CONTRACT_LAST, preferred_element_type=jnp.float32
    )
    back_two = (slope_two * back_two).astype(jnp.bfloat16)
    back_one = lax.dot_general(
        back_two[:, :depth],
        weights[0, :, features:],
        CONTRACT_LAST,
        preferred_element_type=jnp.float32,
    ) + lax.dot_general(
        back_two[:, depth:],
        weights[1, :, :depth],
        CONTRACT_LAST,
        preferred_element_type=jnp.float32,
    )
    slope_one = 1.0 - jnp.square(hidden_one.astype(jnp.float32))
    return (slope_one * back_one).astype(jnp.bfloat16)


def first_kernel(
    state,
    increment,
    diffusivity,
    land_sea,
    col,
    lev,
    val,
    prec,
    w_in,
    w_mid,
    w_out,
    rows,
    edges,
    outer,
):
    features = w_in.shape[1]
    rows[:, :features] = w_in[...].astype(jnp.bfloat16)
    rows[:, features:-features] = w_mid[...]
    rows[:, -features:] = w_out[...].astype(jnp.bfloat16)
    edges[...] = jnp.zeros_like(edges)
    cells = state.shape[1]
    for which, field in enumerate((state, increment, diffusivity)):
        start = 2 * REACH * which
        edges[start : start + REACH] = field[0, :REACH]
        edges[start + REACH : start + 2 * REACH] = field[0, cells - REACH :]
    edges[18:19, :cells] = 0.5 + land_sea[...].astype(jnp.float32)
    count = col.shape[1]
    for row, numbers in enumerate((col, lev, val, prec)):
        edges[19 + row : 20 + row, :count] = numbers[...].astype(jnp.float32)
    outer[...] = (state[0] + increment[0]).astype(jnp.bfloat16)


def ring_gating(mine, other):
    cells = mine.shape[1]
    lane = lax.broadcasted_iota(jnp.int32, (8, cells), 1)
    mine, other = (jnp.broadcast_to(row, (8, cells)) for row in (mine, other))
    other = jnp.where(lane < REACH, other, pltpu.roll(other, 8, 1))
    return jnp.concatenate([mine, other], axis=1)


def ring_field(field, edges, which):
    start = 2 * REACH * which
    return jnp.concatenate(
        [
            field,
            edges[start : start + REACH],
            jnp.zeros((8 - 2 * REACH, field.shape[1]), jnp.float32),
            edges[start + REACH : start + 2 * REACH],
        ]
    )


def pack_fields_kernel(state, increment, diffusivity, pack):
    cells = state.shape[1]
    for which, field in enumerate((state, increment, diffusivity)):
        pack[BLOCK * which : BLOCK * which + cells] = field[0].astype(jnp.bfloat16)


def pack_edges_kernel(fields, mine, other, pack):
    features = fields.shape[1]
    cells = BLOCK - 16
    for which in range(3):
        base, start = BLOCK * which, 2 * REACH * which
        pack[base : base + cells] = fields[base : base + cells]
        edges = [
            other[start : start + REACH],
            jnp.zeros((8 - 2 * REACH, features), jnp.float32),
            other[start + REACH : start + 2 * REACH],
            jnp.zeros((8, features), jnp.float32),
        ]
        pack[base + cells : base + BLOCK] = jnp.concatenate(edges).astype(jnp.bfloat16)
    gating = ring_gating(mine[18:19, :cells], other[18:19, :cells])[:1]
    numbers = mine[21:23, :]
    coarse = numbers.astype(jnp.bfloat16).astype(jnp.float32)
    fine = numbers - coarse
    rest = [gating, mine[19:21, :], coarse, fine, jnp.zeros((16 - 7, features), jnp.float32)]
    pack[3 * BLOCK :] = jnp.concatenate(rest).astype(jnp.bfloat16)


def behind_kernel(far, behind):
    pack = 3 * BLOCK + 16
    behind[:pack] = far[:pack]
    total = far[pack : pack + BLOCK].astype(jnp.float32)
    total = total + far[pack + BLOCK : pack + 2 * BLOCK].astype(jnp.float32)
    behind[pack:] = total.astype(jnp.bfloat16)


def whole_kernel(
    observations,
    core,
    state,
    increment,
    diffusivity,
    mine,
    other,
    near,
    far,
    beyond,
    outer,
    settled_out,
    spreading_out,
    ends_out,
    kept,
    given,
    weights,
):
    cells, features = state.shape[1:]
    depth = weights.shape[2] - features
    length = cells + 8
    pack = 3 * BLOCK + 16
    square = (length, 2 * cells)
    diagonal = lax.broadcasted_iota(jnp.int32, square, 0) == lax.broadcasted_iota(
        jnp.int32, square, 1
    )

    def column(row):
        return jnp.sum(jnp.where(diagonal, row, 0.0), axis=1, keepdims=True)

    def laplace(field, lat):
        return lat + pltpu.roll(field, 1, 0) + pltpu.roll(field, length - 1, 0) - 4.0 * field

    def unpack(ref, start):
        fields = [
            ref[start + BLOCK * i : start + BLOCK * (i + 1), :].astype(jnp.float32)[:length]
            for i in range(3)
        ]
        rest = ref[start + 3 * BLOCK : start + pack, :].astype(jnp.float32)
        return fields + [column(rest[:1])], rest

    def activate(both):
        middle = both.shape[0] // 2
        hidden = jnp.tanh(both[:middle]).astype(jnp.bfloat16).astype(jnp.float32)
        tangent = (1.0 - hidden * hidden) * both[middle:]
        return jnp.concatenate([hidden, tangent]).astype(jnp.bfloat16)

    def networks(rows):
        stacked = jnp.concatenate([row[0] for row in rows] + [row[1] for row in rows])
        stacked = stacked.astype(jnp.bfloat16)
        one = activate(
            lax.dot_general(
                stacked,
                weights[0, :, :features],
                CONTRACT_LAST,
                preferred_element_type=jnp.float32,
            )
        )
        low = activate(jnp.dot(one, weights[0, :, features:], preferred_element_type=jnp.float32))
        high = activate(jnp.dot(one, weights[1, :, :depth], preferred_element_type=jnp.float32))
        out = jnp.dot(
            low, weights[1, :depth, depth:], preferred_element_type=jnp.float32
        ) + jnp.dot(high, weights[1, depth:, depth:], preferred_element_type=jnp.float32)
        saved = (one[:cells], jnp.concatenate([low[:cells], high[:cells]], axis=1), stacked[:cells])
        outs = [out[i * length : (i + 1) * length] for i in range(2 * len(rows))]
        return list(zip(outs[: len(rows)], outs[len(rows) :])), saved

    def observed(final, columns, levels, values, precisions):
        count = columns.shape[1]
        cell_ids = lax.broadcasted_iota(jnp.int32, (length, count), 0).astype(jnp.float32)
        level_ids = lax.broadcasted_iota(jnp.int32, (features, count), 0).astype(jnp.float32)
        pick_cell = (cell_ids == columns).astype(jnp.float32)
        pick_level = (level_ids == levels).astype(jnp.float32)
        at_level = jnp.dot(
            final, pick_level, precision=lax.Precision.HIGHEST, preferred_element_type=jnp.float32
        )
        modelled = jnp.sum(pick_cell * at_level, axis=0, keepdims=True)
        return lax.dot_general(
            pick_cell * (precisions * (modelled - values)),
            pick_level,
            CONTRACT_LAST,
            precision=lax.Precision.HIGHEST,
            preferred_element_type=jnp.float32,
        )

    own = [ring_field(ref[0], other, i) for i, ref in enumerate((state, increment, diffusivity))]
    gate = column(ring_gating(mine[18:19, :cells], other[18:19, :cells])[:1])
    own.append(gate)
    beside, beside_rest = zip(unpack(near, 0), unpack(far, 0))
    second = [unpack(beyond, 0)[0], unpack(far, pack)[0]]
    third = [
        beyond[pack : pack + BLOCK].astype(jnp.float32)[:length],
        jnp.concatenate(
            [outer[...].astype(jnp.float32), jnp.zeros((length - cells, features), jnp.float32)]
        ),
    ]

    def advance(row, lats, moved):
        states, tangents, diffuse, gated = row
        return (
            states + diffuse * laplace(states, lats[0]) + gated * moved[0],
            tangents + diffuse * laplace(tangents, lats[1]) + gated * moved[1],
        )

    def advance_sum(row, middle, lat, moved):
        return middle + row[2] * laplace(middle, lat) + row[3] * (moved[0] + moved[1])

    groups = ((0,), (1, 2), (3, 4))
    all_rows = [own] + list(beside) + second
    moved = []
    first = None
    for group in groups:
        got, saved = networks([all_rows[i] for i in group])
        moved += got
        first = saved if first is None else first
    state_one, increment_one = advance(
        own, [beside[0][i] + beside[1][i] for i in range(2)], moved[0]
    )
    middle_one = state_one + increment_one
    beside_one, beside_middle, second_middle = [], [], []
    for i, (row, next_row, last) in enumerate(zip(beside, second, third)):
        one = advance(row, [own[j] + next_row[j] for j in range(2)], moved[1 + i])
        beside_one.append(one)
        beside_middle.append(one[0] + one[1])
        next_sum = next_row[0] + next_row[1]
        second_middle.append(advance_sum(next_row, next_sum, row[0] + row[1] + last, moved[3 + i]))
    all_rows = [(state_one, increment_one)] + beside_one
    late, moved = None, []
    for group in ((0,), (1, 2)):
        got, saved = networks([all_rows[i] for i in group])
        moved += got
        late = saved if late is None else late
    final = advance_sum(own, middle_one, beside_middle[0] + beside_middle[1], moved[0])
    count = observations
    columns = other[19:20, :count]
    columns = jnp.where(
        columns == 0.0, float(cells), jnp.where(columns == cells - 1.0, length - 1.0, -1.0)
    )
    columns = jnp.concatenate([mine[19:20, :count], columns], axis=1)
    chosen = [
        jnp.concatenate([mine[i : i + 1, :count], other[i : i + 1, :count]], axis=1)
        for i in (20, 21, 22)
    ]
    adjoint = observed(final, columns, *chosen)
    around = jnp.zeros_like(adjoint)
    for row, middle, next_middle, rest, moves in zip(
        beside, beside_middle, second_middle, beside_rest, moved[1:]
    ):
        total = advance_sum(row, middle, middle_one + next_middle, moves)
        around = around + row[2] * observed(
            total,
            rest[1:2, :cells],
            rest[2:3, :cells],
            rest[3:4, :cells] + rest[5:6, :cells],
            rest[4:5, :cells] + rest[6:7, :cells],
        )
    spreading = own[2] * adjoint
    adjoint_one = (adjoint + laplace(spreading, around))[:cells]
    gate = gate[:cells]
    source_late = (gate * adjoint[:cells]).astype(jnp.bfloat16)
    back_late = adjoint_layers(source_late, late[0], late[1], weights)
    adjoint_one = adjoint_one + jnp.dot(
        back_late, weights[0, :, :features], preferred_element_type=jnp.float32
    )
    spreading = own[2][:cells] * adjoint_one
    spreading_out[...] = spreading
    ends_out[...] = jnp.concatenate([spreading[:1], spreading[cells - 7 :]])
    source = (gate * adjoint_one).astype(jnp.bfloat16)
    back_one = adjoint_layers(source, first[0], first[1], weights)
    settled_out[...] = (
        adjoint_one
        - 4.0 * spreading
        + jnp.dot(back_one, weights[0, :, :features], preferred_element_type=jnp.float32)
    )
    first_core = core[0] == 0
    lefts = [jnp.concatenate([back_late, back_one]), jnp.concatenate([late[1], first[1]])]
    rights = [jnp.concatenate([late[2], first[2]]), jnp.concatenate([source_late, source])]
    halves, blocks, rows, width = kept.shape
    for out, which in ((given, 1), (kept, 0)):
        total = lax.dot_general(
            jnp.where(first_core, lefts[which], lefts[1 - which]),
            jnp.where(first_core, rights[which], rights[1 - which]),
            CONTRACT_FIRST,
            preferred_element_type=jnp.float32,
        ).astype(jnp.bfloat16)
        for half in range(halves):
            for block in range(blocks):
                out[half, block] = total[
                    block * rows : (block + 1) * rows, half * width : (half + 1) * width
                ]


def on_chip(kernel, outs, operands, flops, scratch=(), scalars=0, direct=0, fetched=0, place=None, room=32):
    size = sum(array.size * array.dtype.itemsize for array in list(operands) + list(outs))
    by_kernel = fetched > 0 or place is not None
    before = scalars + (direct if by_kernel else len(operands) - scalars)
    count = len(operands) - before
    places = [pltpu.SMEM] * scalars + [pltpu.VMEM] * (before - scalars) + [pl.ANY] * count
    body = kernel
    if by_kernel:
        copies = tuple(
            pltpu.VMEM(array.shape, array.dtype)
            for array in operands[before : before + fetched]
        )
        scratch = copies + (pltpu.SemaphoreType.DMA((count,)),) + tuple(scratch)

        def body(*refs):
            numbers, ready = refs[:scalars], refs[scalars:before]
            sources, refs = refs[before : before + count], refs[before + count :]
            results, refs = refs[: len(outs)], refs[len(outs) :]
            held, done, rest = refs[:fetched], refs[fetched], refs[fetched + 1 :]
            targets = list(held)
            if place is not None:
                targets += place(numbers, rest)
            moves = [
                pltpu.make_async_copy(source, target, done.at[i])
                for i, (source, target) in enumerate(zip(sources, targets))
            ]
            for move in moves:
                move.start()
            for move in moves:
                move.wait()
            kernel(*numbers, *ready, *held, *results, *rest)

    return pl.pallas_call(
        body,
        out_shape=outs,
        in_specs=[pl.BlockSpec(memory_space=place_) for place_ in places],
        out_specs=[pl.BlockSpec(memory_space=pltpu.VMEM)] * len(outs),
        scratch_shapes=scratch,
        compiler_params=pltpu.CompilerParams(vmem_limit_bytes=room * 1024 * 1024),
        cost_estimate=pl.CostEstimate(flops=flops, bytes_accessed=size, transcendentals=0),
    )(*operands)


def sum_and_spread_kernel(parts, copies):
    total = jnp.sum(parts[...].astype(jnp.float32), axis=0).astype(jnp.bfloat16)
    copies[...] = jnp.broadcast_to(total[None], copies.shape)


def sum_and_square_kernel(place, parts, copies, total):
    total[...] = jnp.sum(parts[...].astype(jnp.float32), axis=0)
    depth = copies.shape[1] // 2
    own = total[pl.ds(pl.multiple_of(place[0] * depth, depth), depth), :]
    squares = jnp.sum(total[...] * total[...], axis=0, keepdims=True)
    terms = []
    for _ in range(3):
        terms.append(squares.astype(jnp.bfloat16).astype(jnp.float32))
        squares = squares - terms[-1]
    rest = jnp.zeros((depth - len(terms), squares.shape[1]), jnp.float32)
    both = jnp.concatenate([own] + terms + [rest]).astype(jnp.bfloat16)
    copies[...] = jnp.broadcast_to(both[None], copies.shape)


def update_kernel(blocks, count, place, parts_ref, w_in, w_out, new_in, new_out):
    depth = parts_ref.shape[1] // 2
    shard = w_in.shape[0]
    parts = parts_ref[...].astype(jnp.float32)
    squares = jnp.sum(parts, axis=0)[depth:]
    square_sum = jnp.sum(jnp.sum(squares, axis=0, keepdims=True), axis=1, keepdims=True)
    scale = LEARN_RATE / jnp.sqrt(square_sum / count + EPSILON)
    for which, (old, new) in enumerate(((w_in, new_in), (w_out, new_out))):
        sides = []
        for half in range(2):
            rows = parts_ref[(half * blocks + place[0]) * 2 + which].astype(jnp.float32)[:depth]
            sides.append(jnp.where(place[1] == 0, rows[:shard], rows[shard:]))
        new[...] = old[...] - scale * jnp.concatenate(sides, axis=1)


def add_kernel(left, right, total):
    total[...] = (left[...].astype(jnp.float32) + right[...].astype(jnp.float32)).astype(
        jnp.bfloat16
    )


def updated(kept, given, w_in, w_out, arriving, later):
    halves, blocks, rows, columns = kept.shape
    peers = halves * blocks
    (grads,) = on_chip(
        add_kernel,
        (jax.ShapeDtypeStruct((peers, rows, columns), jnp.bfloat16),),
        (kept.reshape(peers, rows, columns), swapped(given, "core").reshape(peers, rows, columns)),
        kept.size,
    )
    grads = lax.all_to_all(grads, AROUND[:-1], 0, 0)
    grads, arriving = lax.optimization_barrier((grads, arriving))
    for axis in ("z_lo", "z_hi"):
        count = lax.axis_size(axis)
        (copies,) = on_chip(
            sum_and_spread_kernel,
            (jax.ShapeDtypeStruct((count, rows, columns), jnp.bfloat16),),
            (grads,),
            grads.size,
        )
        grads = lax.all_to_all(copies, axis, 0, 0)
        if axis == "z_lo":
            grads, later = lax.optimization_barrier((grads, later))
    peers *= lax.axis_size("core")
    depth = rows // lax.axis_size(Z)
    (copies,) = on_chip(
        sum_and_square_kernel,
        (jax.ShapeDtypeStruct((peers, 2 * depth, columns), jnp.bfloat16),),
        (lax.axis_index(Z)[None], grads),
        grads.size,
        scratch=(pltpu.VMEM((rows, columns), jnp.float32),),
        scalars=1,
    )
    parts = lax.all_to_all(copies, AROUND, 0, 0)
    place = jnp.stack([lax.axis_index(("x_lo", "y")), lax.axis_index("core")])
    shape = jax.ShapeDtypeStruct(w_in.shape, jnp.float32)
    new_in, new_out = on_chip(
        functools.partial(update_kernel, blocks, float(peers * rows * columns)),
        (shape, shape),
        (place, parts, w_in, w_out),
        parts.size,
        scalars=1,
    )
    return new_in, new_out, arriving, later


def local(
    state, increment, diffusivity, land_sea, w_in, w_mid, w_out, obs_col, obs_lev, obs_val, obs_prec
):
    _, cells, features = state.shape
    length = cells + 8
    observed = [numbers[None] for numbers in (obs_col, obs_lev, obs_val, obs_prec)]

    def outs(*shapes):
        return tuple(jax.ShapeDtypeStruct(shape, kind) for shape, kind in shapes)

    columns = 2 * features + w_mid.shape[1]
    width = columns // lax.axis_size("core")
    rows, mine, outer = on_chip(
        first_kernel,
        outs(
            ((w_in.shape[0], columns), jnp.bfloat16),
            ((24, features), jnp.float32),
            ((cells, features), jnp.bfloat16),
        ),
        (state, increment, diffusivity, land_sea, *observed, w_in, w_mid, w_out),
        0,
        fetched=11,
        room=56,
    )
    rows = lax.all_gather(rows, "core", axis=0, tiled=True)
    half = lax.dynamic_slice_in_dim(rows, lax.axis_index("core") * width, width, 1)
    fields = (state, increment, diffusivity)
    half, mine, outer, fields = lax.optimization_barrier((half, mine, outer, fields))
    half = spread(half, Z).reshape(-1, width)
    other = swapped(mine, "x_hi")
    outer = swapped_three_apart(outer)
    packed = outs(((3 * BLOCK + 16, features), jnp.bfloat16))
    (packs,) = on_chip(pack_fields_kernel, packed, fields, 0, fetched=3)
    (own,) = on_chip(pack_edges_kernel, packed, (packs, mine, other), 0)
    near = swapped(own, "core")
    far = swapped_between_chips(jnp.concatenate([own, near]))
    half, near = lax.optimization_barrier((half, near))
    half = spread(half, ("x_lo", "y")).reshape(-1, width)
    far, outer = lax.optimization_barrier((far, outer))
    pack = 3 * BLOCK + 16
    (beyond,) = on_chip(
        behind_kernel, outs(((pack + BLOCK, features), jnp.bfloat16)), (far,), 10**10
    )
    beyond = swapped(beyond, "core")
    half, far, beyond = lax.optimization_barrier((half, far, beyond))
    hidden_units = half.shape[0]
    blocks = lax.axis_size(("x_lo", "y"))
    halves = lax.axis_size("x_hi")
    part = ((halves, blocks, hidden_units // blocks, features // halves), jnp.bfloat16)
    narrow = ((cells, features), jnp.float32)
    settled, spreading, ends, kept, given = on_chip(
        functools.partial(whole_kernel, obs_col.shape[0]),
        outs(
            narrow,
            narrow,
            ((8, features), jnp.float32),
            part,
            part,
        ),
        (lax.axis_index("core")[None], state, increment, diffusivity, mine, other, near, far, beyond, outer)
        + (half, swapped(half, "core")),
        40 * cells * hidden_units * (2 * features + hidden_units),
        scratch=(pltpu.VMEM((2, hidden_units, width), jnp.bfloat16),),
        scalars=1,
        direct=9,
        fetched=0,
        place=lambda numbers, rest: [
            rest[0].at[numbers[0][0]],
            rest[0].at[1 - numbers[0][0]],
        ],
    )
    w_in_new, w_out_new, ends, spreading = updated(
        kept, given, w_in, w_out, swapped(ends, "x_hi"), spreading
    )
    far = swapped_between_chips(spreading)
    near = swapped(spreading, "core")
    east = jnp.concatenate([spreading[1:], ends[:1]])
    west = jnp.concatenate([ends[-1:], spreading[:-1]])
    adjoint = settled + (far + near + east + west)
    return adjoint[None], w_in_new, w_out_new


def solution(mesh):
    fine = Mesh(mesh.devices.reshape(FINE_SIZES), FINE_AXES)
    everywhere = TILE + ("x_hi",)
    return jax.shard_map(
        local,
        mesh=fine,
        in_specs=(
            P(TILE, "x_hi", None),
            P(TILE, "x_hi", None),
            P(TILE, "x_hi", None),
            P(TILE, "x_hi"),
            P(TILE, None),
            P(TILE, None),
            P(TILE, None),
            P(everywhere),
            P(everywhere),
            P(everywhere),
            P(everywhere),
        ),
        out_specs=(P(TILE, "x_hi", None), P(TILE, None), P(TILE, None)),
        check_vma=False,
    )
```

```python
import functools

import jax
import jax.numpy as jnp
from jax import lax
from jax.experimental import pallas as pl
from jax.experimental.pallas import tpu as pltpu
from jax.sharding import Mesh
from jax.sharding import PartitionSpec as P

LEARN_RATE = 0.02
EPSILON = 1e-06
CONTRACT_LAST = (((1,), (1,)), ((), ()))
CONTRACT_FIRST = (((0,), (0,)), ((), ()))
FINE_AXES = ("x_lo", "y", "z_hi", "z_lo", "core", "x_hi")
FINE_SIZES = (2, 4, 4, 4, 2, 2)
Z = ("z_hi", "z_lo")
TILE = ("x_lo", "y", "z_hi", "z_lo", "core")
X = ("x_lo", "x_hi")
AROUND = ("x_hi", "x_lo", "y", "core")
REACH = 3
BLOCK = 144


def spread(block, axis):
    count = lax.axis_size(axis)
    return lax.all_to_all(jnp.broadcast_to(block[None], (count,) + block.shape), axis, 0, 0)


def swapped(array, axis):
    return lax.ppermute(array, axis, [(0, 1), (1, 0)])


def swapped_between_chips(array):
    pairs = []
    for row in range(1, lax.axis_size(TILE) - 1, 2):
        pairs += [(row, row + 1), (row + 1, row)]
    return lax.ppermute(array, TILE, pairs)


def next_along_x(array, step):
    high = lax.axis_size("x_hi")
    places = [low * high + part for part in range(high) for low in range(lax.axis_size("x_lo"))]
    pairs = [(place, places[(x + step) % len(places)]) for x, place in enumerate(places)]
    return lax.ppermute(array, X, pairs)


def swapped_three_apart(array):
    count = lax.axis_size(TILE)
    pairs = [(row, row + 3) for row in range(1, count - 3, 2)]
    return lax.ppermute(array, TILE, pairs + [(after, row) for row, after in pairs])


def adjoint_layers(source, hidden_one, hidden_two, weights):
    features = source.shape[1]
    depth = weights.shape[2] - features
    slope_two = 1.0 - jnp.square(hidden_two.astype(jnp.float32))
    back_two = lax.dot_general(
        source, weights[1, :, depth:], CONTRACT_LAST, preferred_element_type=jnp.float32
    )
    back_two = (slope_two * back_two).astype(jnp.bfloat16)
    back_one = lax.dot_general(
        back_two[:, :depth],
        weights[0, :, features:],
        CONTRACT_LAST,
        preferred_element_type=jnp.float32,
    ) + lax.dot_general(
        back_two[:, depth:],
        weights[1, :, :depth],
        CONTRACT_LAST,
        preferred_element_type=jnp.float32,
    )
    slope_one = 1.0 - jnp.square(hidden_one.astype(jnp.float32))
    return (slope_one * back_one).astype(jnp.bfloat16)


def first_kernel(
    state,
    increment,
    diffusivity,
    land_sea,
    col,
    lev,
    val,
    prec,
    w_in,
    w_mid,
    w_out,
    rows,
    edges,
    outer,
):
    features = w_in.shape[1]
    rows[:, :features] = w_in[...].astype(jnp.bfloat16)
    rows[:, features:-features] = w_mid[...]
    rows[:, -features:] = w_out[...].astype(jnp.bfloat16)
    edges[...] = jnp.zeros_like(edges)
    cells = state.shape[1]
    for which, field in enumerate((state, increment, diffusivity)):
        start = 2 * REACH * which
        edges[start : start + REACH] = field[0, :REACH]
        edges[start + REACH : start + 2 * REACH] = field[0, cells - REACH :]
    edges[18:19, :cells] = 0.5 + land_sea[...].astype(jnp.float32)
    count = col.shape[1]
    for row, numbers in enumerate((col, lev, val, prec)):
        edges[19 + row : 20 + row, :count] = numbers[...].astype(jnp.float32)
    outer[...] = (state[0] + increment[0]).astype(jnp.bfloat16)


def ring_gating(mine, other):
    cells = mine.shape[1]
    lane = lax.broadcasted_iota(jnp.int32, (8, cells), 1)
    mine, other = (jnp.broadcast_to(row, (8, cells)) for row in (mine, other))
    other = jnp.where(lane < REACH, other, pltpu.roll(other, 8, 1))
    return jnp.concatenate([mine, other], axis=1)


def ring_field(field, edges, which):
    start = 2 * REACH * which
    return jnp.concatenate(
        [
            field,
            edges[start : start + REACH],
            jnp.zeros((8 - 2 * REACH, field.shape[1]), jnp.float32),
            edges[start + REACH : start + 2 * REACH],
        ]
    )


def pack_fields_kernel(state, increment, diffusivity, pack):
    cells = state.shape[1]
    for which, field in enumerate((state, increment, diffusivity)):
        pack[BLOCK * which : BLOCK * which + cells] = field[0].astype(jnp.bfloat16)


def pack_edges_kernel(fields, mine, other, pack):
    features = fields.shape[1]
    cells = BLOCK - 16
    for which in range(3):
        base, start = BLOCK * which, 2 * REACH * which
        pack[base : base + cells] = fields[base : base + cells]
        edges = [
            other[start : start + REACH],
            jnp.zeros((8 - 2 * REACH, features), jnp.float32),
            other[start + REACH : start + 2 * REACH],
            jnp.zeros((8, features), jnp.float32),
        ]
        pack[base + cells : base + BLOCK] = jnp.concatenate(edges).astype(jnp.bfloat16)
    gating = ring_gating(mine[18:19, :cells], other[18:19, :cells])[:1]
    numbers = mine[21:23, :]
    coarse = numbers.astype(jnp.bfloat16).astype(jnp.float32)
    fine = numbers - coarse
    rest = [gating, mine[19:21, :], coarse, fine, jnp.zeros((16 - 7, features), jnp.float32)]
    pack[3 * BLOCK :] = jnp.concatenate(rest).astype(jnp.bfloat16)


def behind_kernel(far, behind):
    pack = 3 * BLOCK + 16
    behind[:pack] = far[:pack]
    total = far[pack : pack + BLOCK].astype(jnp.float32)
    total = total + far[pack + BLOCK : pack + 2 * BLOCK].astype(jnp.float32)
    behind[pack:] = total.astype(jnp.bfloat16)


def whole_kernel(
    observations,
    core,
    state,
    increment,
    diffusivity,
    mine,
    other,
    near,
    far,
    beyond,
    outer,
    settled_out,
    spreading_out,
    ends_out,
    kept,
    given,
    weights,
):
    cells, features = state.shape[1:]
    depth = weights.shape[2] - features
    length = cells + 8
    pack = 3 * BLOCK + 16
    square = (length, 2 * cells)
    diagonal = lax.broadcasted_iota(jnp.int32, square, 0) == lax.broadcasted_iota(
        jnp.int32, square, 1
    )

    def column(row):
        return jnp.sum(jnp.where(diagonal, row, 0.0), axis=1, keepdims=True)

    def laplace(field, lat):
        return lat + pltpu.roll(field, 1, 0) + pltpu.roll(field, length - 1, 0) - 4.0 * field

    def unpack(ref, start):
        fields = [
            ref[start + BLOCK * i : start + BLOCK * (i + 1), :].astype(jnp.float32)[:length]
            for i in range(3)
        ]
        rest = ref[start + 3 * BLOCK : start + pack, :].astype(jnp.float32)
        return fields + [column(rest[:1])], rest

    def activate(both):
        middle = both.shape[0] // 2
        hidden = jnp.tanh(both[:middle]).astype(jnp.bfloat16).astype(jnp.float32)
        tangent = (1.0 - hidden * hidden) * both[middle:]
        return jnp.concatenate([hidden, tangent]).astype(jnp.bfloat16)

    def networks(rows):
        stacked = jnp.concatenate([row[0] for row in rows] + [row[1] for row in rows])
        stacked = stacked.astype(jnp.bfloat16)
        one = activate(
            lax.dot_general(
                stacked,
                weights[0, :, :features],
                CONTRACT_LAST,
                preferred_element_type=jnp.float32,
            )
        )
        low = activate(jnp.dot(one, weights[0, :, features:], preferred_element_type=jnp.float32))
        high = activate(jnp.dot(one, weights[1, :, :depth], preferred_element_type=jnp.float32))
        out = jnp.dot(
            low, weights[1, :depth, depth:], preferred_element_type=jnp.float32
        ) + jnp.dot(high, weights[1, depth:, depth:], preferred_element_type=jnp.float32)
        saved = (one[:cells], jnp.concatenate([low[:cells], high[:cells]], axis=1), stacked[:cells])
        outs = [out[i * length : (i + 1) * length] for i in range(2 * len(rows))]
        return list(zip(outs[: len(rows)], outs[len(rows) :])), saved

    def observed(final, columns, levels, values, precisions):
        count = columns.shape[1]
        cell_ids = lax.broadcasted_iota(jnp.int32, (length, count), 0).astype(jnp.float32)
        level_ids = lax.broadcasted_iota(jnp.int32, (features, count), 0).astype(jnp.float32)
        pick_cell = (cell_ids == columns).astype(jnp.float32)
        pick_level = (level_ids == levels).astype(jnp.float32)
        at_level = jnp.dot(
            final, pick_level, precision=lax.Precision.HIGHEST, preferred_element_type=jnp.float32
        )
        modelled = jnp.sum(pick_cell * at_level, axis=0, keepdims=True)
        return lax.dot_general(
            pick_cell * (precisions * (modelled - values)),
            pick_level,
            CONTRACT_LAST,
            precision=lax.Precision.HIGHEST,
            preferred_element_type=jnp.float32,
        )

    own = [ring_field(ref[0], other, i) for i, ref in enumerate((state, increment, diffusivity))]
    gate = column(ring_gating(mine[18:19, :cells], other[18:19, :cells])[:1])
    own.append(gate)
    beside, beside_rest = zip(unpack(near, 0), unpack(far, 0))
    second = [unpack(beyond, 0)[0], unpack(far, pack)[0]]
    third = [
        beyond[pack : pack + BLOCK].astype(jnp.float32)[:length],
        jnp.concatenate(
            [outer[...].astype(jnp.float32), jnp.zeros((length - cells, features), jnp.float32)]
        ),
    ]

    def advance(row, lats, moved):
        states, tangents, diffuse, gated = row
        return (
            states + diffuse * laplace(states, lats[0]) + gated * moved[0],
            tangents + diffuse * laplace(tangents, lats[1]) + gated * moved[1],
        )

    def advance_sum(row, middle, lat, moved):
        return middle + row[2] * laplace(middle, lat) + row[3] * (moved[0] + moved[1])

    groups = ((0,), (1, 2), (3, 4))
    all_rows = [own] + list(beside) + second
    moved = []
    first = None
    for group in groups:
        got, saved = networks([all_rows[i] for i in group])
        moved += got
        first = saved if first is None else first
    state_one, increment_one = advance(
        own, [beside[0][i] + beside[1][i] for i in range(2)], moved[0]
    )
    middle_one = state_one + increment_one
    beside_one, beside_middle, second_middle = [], [], []
    for i, (row, next_row, last) in enumerate(zip(beside, second, third)):
        one = advance(row, [own[j] + next_row[j] for j in range(2)], moved[1 + i])
        beside_one.append(one)
        beside_middle.append(one[0] + one[1])
        next_sum = next_row[0] + next_row[1]
        second_middle.append(advance_sum(next_row, next_sum, row[0] + row[1] + last, moved[3 + i]))
    all_rows = [(state_one, increment_one)] + beside_one
    late, moved = None, []
    for group in ((0,), (1, 2)):
        got, saved = networks([all_rows[i] for i in group])
        moved += got
        late = saved if late is None else late
    final = advance_sum(own, middle_one, beside_middle[0] + beside_middle[1], moved[0])
    count = observations
    columns = other[19:20, :count]
    columns = jnp.where(
        columns == 0.0, float(cells), jnp.where(columns == cells - 1.0, length - 1.0, -1.0)
    )
    columns = jnp.concatenate([mine[19:20, :count], columns], axis=1)
    chosen = [
        jnp.concatenate([mine[i : i + 1, :count], other[i : i + 1, :count]], axis=1)
        for i in (20, 21, 22)
    ]
    adjoint = observed(final, columns, *chosen)
    around = jnp.zeros_like(adjoint)
    for row, middle, next_middle, rest, moves in zip(
        beside, beside_middle, second_middle, beside_rest, moved[1:]
    ):
        total = advance_sum(row, middle, middle_one + next_middle, moves)
        around = around + row[2] * observed(
            total,
            rest[1:2, :cells],
            rest[2:3, :cells],
            rest[3:4, :cells] + rest[5:6, :cells],
            rest[4:5, :cells] + rest[6:7, :cells],
        )
    spreading = own[2] * adjoint
    adjoint_one = (adjoint + laplace(spreading, around))[:cells]
    gate = gate[:cells]
    source_late = (gate * adjoint[:cells]).astype(jnp.bfloat16)
    back_late = adjoint_layers(source_late, late[0], late[1], weights)
    adjoint_one = adjoint_one + jnp.dot(
        back_late, weights[0, :, :features], preferred_element_type=jnp.float32
    )
    spreading = own[2][:cells] * adjoint_one
    spreading_out[...] = spreading
    ends_out[...] = jnp.concatenate([spreading[:1], spreading[cells - 7 :]])
    source = (gate * adjoint_one).astype(jnp.bfloat16)
    back_one = adjoint_layers(source, first[0], first[1], weights)
    settled_out[...] = (
        adjoint_one
        - 4.0 * spreading
        + jnp.dot(back_one, weights[0, :, :features], preferred_element_type=jnp.float32)
    )
    first_core = core[0] == 0
    lefts = [jnp.concatenate([back_late, back_one]), jnp.concatenate([late[1], first[1]])]
    rights = [jnp.concatenate([late[2], first[2]]), jnp.concatenate([source_late, source])]
    halves, blocks, rows, width = kept.shape
    for out, which in ((given, 1), (kept, 0)):
        total = lax.dot_general(
            jnp.where(first_core, lefts[which], lefts[1 - which]),
            jnp.where(first_core, rights[which], rights[1 - which]),
            CONTRACT_FIRST,
            preferred_element_type=jnp.float32,
        ).astype(jnp.bfloat16)
        for half in range(halves):
            for block in range(blocks):
                out[half, block] = total[
                    block * rows : (block + 1) * rows, half * width : (half + 1) * width
                ]


def on_chip(kernel, outs, operands, flops, scratch=(), scalars=0, direct=0, fetched=0, place=None, room=32):
    size = sum(array.size * array.dtype.itemsize for array in list(operands) + list(outs))
    by_kernel = fetched > 0 or place is not None
    before = scalars + (direct if by_kernel else len(operands) - scalars)
    count = len(operands) - before
    places = [pltpu.SMEM] * scalars + [pltpu.VMEM] * (before - scalars) + [pl.ANY] * count
    body = kernel
    if by_kernel:
        copies = tuple(
            pltpu.VMEM(array.shape, array.dtype)
            for array in operands[before : before + fetched]
        )
        scratch = copies + (pltpu.SemaphoreType.DMA((count,)),) + tuple(scratch)

        def body(*refs):
            numbers, ready = refs[:scalars], refs[scalars:before]
            sources, refs = refs[before : before + count], refs[before + count :]
            results, refs = refs[: len(outs)], refs[len(outs) :]
            held, done, rest = refs[:fetched], refs[fetched], refs[fetched + 1 :]
            targets = list(held)
            if place is not None:
                targets += place(numbers, rest)
            moves = [
                pltpu.make_async_copy(source, target, done.at[i])
                for i, (source, target) in enumerate(zip(sources, targets))
            ]
            for move in moves:
                move.start()
            for move in moves:
                move.wait()
            kernel(*numbers, *ready, *held, *results, *rest)

    return pl.pallas_call(
        body,
        out_shape=outs,
        in_specs=[pl.BlockSpec(memory_space=place_) for place_ in places],
        out_specs=[pl.BlockSpec(memory_space=pltpu.VMEM)] * len(outs),
        scratch_shapes=scratch,
        compiler_params=pltpu.CompilerParams(vmem_limit_bytes=room * 1024 * 1024),
        cost_estimate=pl.CostEstimate(flops=flops, bytes_accessed=size, transcendentals=0),
    )(*operands)


def sum_and_spread_kernel(parts, copies):
    total = jnp.sum(parts[...].astype(jnp.float32), axis=0).astype(jnp.bfloat16)
    copies[...] = jnp.broadcast_to(total[None], copies.shape)


def sum_and_square_kernel(place, parts, copies, total):
    total[...] = jnp.sum(parts[...].astype(jnp.float32), axis=0)
    depth = copies.shape[1] // 2
    own = total[pl.ds(pl.multiple_of(place[0] * depth, depth), depth), :]
    squares = jnp.sum(total[...] * total[...], axis=0, keepdims=True)
    terms = []
    for _ in range(3):
        terms.append(squares.astype(jnp.bfloat16).astype(jnp.float32))
        squares = squares - terms[-1]
    rest = jnp.zeros((depth - len(terms), squares.shape[1]), jnp.float32)
    both = jnp.concatenate([own] + terms + [rest]).astype(jnp.bfloat16)
    copies[...] = jnp.broadcast_to(both[None], copies.shape)


def update_kernel(blocks, count, place, parts_ref, w_in, w_out, new_in, new_out):
    depth = parts_ref.shape[1] // 2
    shard = w_in.shape[0]
    parts = parts_ref[...].astype(jnp.float32)
    squares = jnp.sum(parts, axis=0)[depth:]
    square_sum = jnp.sum(jnp.sum(squares, axis=0, keepdims=True), axis=1, keepdims=True)
    scale = LEARN_RATE / jnp.sqrt(square_sum / count + EPSILON)
    for which, (old, new) in enumerate(((w_in, new_in), (w_out, new_out))):
        sides = []
        for half in range(2):
            rows = parts_ref[(half * blocks + place[0]) * 2 + which].astype(jnp.float32)[:depth]
            sides.append(jnp.where(place[1] == 0, rows[:shard], rows[shard:]))
        new[...] = old[...] - scale * jnp.concatenate(sides, axis=1)


def add_kernel(left, right, total):
    total[...] = (left[...].astype(jnp.float32) + right[...].astype(jnp.float32)).astype(
        jnp.bfloat16
    )


def updated(kept, given, w_in, w_out, arriving, later):
    halves, blocks, rows, columns = kept.shape
    peers = halves * blocks
    (grads,) = on_chip(
        add_kernel,
        (jax.ShapeDtypeStruct((peers, rows, columns), jnp.bfloat16),),
        (kept.reshape(peers, rows, columns), swapped(given, "core").reshape(peers, rows, columns)),
        kept.size,
    )
    grads = lax.all_to_all(grads, AROUND[:-1], 0, 0)
    grads, arriving = lax.optimization_barrier((grads, arriving))
    for axis in ("z_lo", "z_hi"):
        count = lax.axis_size(axis)
        (copies,) = on_chip(
            sum_and_spread_kernel,
            (jax.ShapeDtypeStruct((count, rows, columns), jnp.bfloat16),),
            (grads,),
            grads.size,
        )
        grads = lax.all_to_all(copies, axis, 0, 0)
        if axis == "z_lo":
            grads, later = lax.optimization_barrier((grads, later))
    peers *= lax.axis_size("core")
    depth = rows // lax.axis_size(Z)
    (copies,) = on_chip(
        sum_and_square_kernel,
        (jax.ShapeDtypeStruct((peers, 2 * depth, columns), jnp.bfloat16),),
        (lax.axis_index(Z)[None], grads),
        grads.size,
        scratch=(pltpu.VMEM((rows, columns), jnp.float32),),
        scalars=1,
    )
    parts = lax.all_to_all(copies, AROUND, 0, 0)
    place = jnp.stack([lax.axis_index(("x_lo", "y")), lax.axis_index("core")])
    shape = jax.ShapeDtypeStruct(w_in.shape, jnp.float32)
    new_in, new_out = on_chip(
        functools.partial(update_kernel, blocks, float(peers * rows * columns)),
        (shape, shape),
        (place, parts, w_in, w_out),
        parts.size,
        scalars=1,
    )
    return new_in, new_out, arriving, later


def local(
    state, increment, diffusivity, land_sea, w_in, w_mid, w_out, obs_col, obs_lev, obs_val, obs_prec
):
    _, cells, features = state.shape
    length = cells + 8
    observed = [numbers[None] for numbers in (obs_col, obs_lev, obs_val, obs_prec)]

    def outs(*shapes):
        return tuple(jax.ShapeDtypeStruct(shape, kind) for shape, kind in shapes)

    columns = 2 * features + w_mid.shape[1]
    width = columns // lax.axis_size("core")
    rows, mine, outer = on_chip(
        first_kernel,
        outs(
            ((w_in.shape[0], columns), jnp.bfloat16),
            ((24, features), jnp.float32),
            ((cells, features), jnp.bfloat16),
        ),
        (state, increment, diffusivity, land_sea, *observed, w_in, w_mid, w_out),
        0,
        fetched=11,
        room=56,
    )
    rows = lax.all_gather(rows, "core", axis=0, tiled=True)
    half = lax.dynamic_slice_in_dim(rows, lax.axis_index("core") * width, width, 1)
    fields = (state, increment, diffusivity)
    half, mine, outer, fields = lax.optimization_barrier((half, mine, outer, fields))
    half = spread(half, Z).reshape(-1, width)
    other = swapped(mine, "x_hi")
    outer = swapped_three_apart(outer)
    packed = outs(((3 * BLOCK + 16, features), jnp.bfloat16))
    (packs,) = on_chip(pack_fields_kernel, packed, fields, 0, fetched=3)
    other, outer = lax.optimization_barrier((other, outer))
    (own,) = on_chip(pack_edges_kernel, packed, (packs, mine, other), 0)
    near = swapped(own, "core")
    far = swapped_between_chips(jnp.concatenate([own, near]))
    half, near = lax.optimization_barrier((half, near))
    half = spread(half, "y").reshape(-1, width)
    middle = half.shape[0] // 2
    parts = [half, next_along_x(half[:middle], 1), next_along_x(half[middle:], -1)]
    pack = 3 * BLOCK + 16
    (beyond,) = on_chip(
        behind_kernel, outs(((pack + BLOCK, features), jnp.bfloat16)), (far,), far.size
    )
    beyond = swapped(beyond, "core")
    parts[1], far, beyond = lax.optimization_barrier((parts[1], far, beyond))
    hidden_units = 4 * middle
    parts += [swapped(part, "core") for part in parts]
    blocks = lax.axis_size(("x_lo", "y"))
    halves = lax.axis_size("x_hi")
    part = ((halves, blocks, hidden_units // blocks, features // halves), jnp.bfloat16)
    narrow = ((cells, features), jnp.float32)
    settled, spreading, ends, kept, given = on_chip(
        functools.partial(whole_kernel, obs_col.shape[0]),
        outs(
            narrow,
            narrow,
            ((8, features), jnp.float32),
            part,
            part,
        ),
        (jnp.stack([lax.axis_index("core"), lax.axis_index("x_lo")]), state, increment, diffusivity, mine, other, near, far, beyond, outer)
        + tuple(parts),
        40 * cells * hidden_units * (2 * features + hidden_units),
        scratch=(pltpu.VMEM((2, hidden_units, width), jnp.bfloat16),),
        scalars=1,
        direct=9,
        fetched=0,
        place=lambda numbers, rest: [
            rest[0].at[side, pl.ds(pl.multiple_of(start, middle), size)]
            for side in (numbers[0][0], 1 - numbers[0][0])
            for start, size in (
                (numbers[0][1] * 2 * middle, 2 * middle),
                ((1 - numbers[0][1]) * 2 * middle, middle),
                ((1 - numbers[0][1]) * 2 * middle + middle, middle),
            )
        ],
    )
    w_in_new, w_out_new, ends, spreading = updated(
        kept, given, w_in, w_out, swapped(ends, "x_hi"), spreading
    )
    far = swapped_between_chips(spreading)
    near = swapped(spreading, "core")
    east = jnp.concatenate([spreading[1:], ends[:1]])
    west = jnp.concatenate([ends[-1:], spreading[:-1]])
    adjoint = settled + (far + near + east + west)
    return adjoint[None], w_in_new, w_out_new


def solution(mesh):
    fine = Mesh(mesh.devices.reshape(FINE_SIZES), FINE_AXES)
    everywhere = TILE + ("x_hi",)
    return jax.shard_map(
        local,
        mesh=fine,
        in_specs=(
            P(TILE, "x_hi", None),
            P(TILE, "x_hi", None),
            P(TILE, "x_hi", None),
            P(TILE, "x_hi"),
            P(TILE, None),
            P(TILE, None),
            P(TILE, None),
            P(everywhere),
            P(everywhere),
            P(everywhere),
            P(everywhere),
        ),
        out_specs=(P(TILE, "x_hi", None), P(TILE, None), P(TILE, None)),
        check_vma=False,
    )
```

```python
import functools

import jax
import jax.numpy as jnp
from jax import lax
from jax.experimental import pallas as pl
from jax.experimental.pallas import tpu as pltpu
from jax.sharding import Mesh
from jax.sharding import PartitionSpec as P

LEARN_RATE = 0.02
EPSILON = 1e-06
CONTRACT_LAST = (((1,), (1,)), ((), ()))
CONTRACT_FIRST = (((0,), (0,)), ((), ()))
FINE_AXES = ("x_lo", "y", "z_hi", "z_lo", "core", "x_hi")
FINE_SIZES = (2, 4, 4, 4, 2, 2)
Z = ("z_hi", "z_lo")
TILE = ("x_lo", "y", "z_hi", "z_lo", "core")
AROUND = ("x_hi", "x_lo", "y", "core")
REACH = 3
BLOCK = 144


def spread(block, axis):
    count = lax.axis_size(axis)
    return lax.all_to_all(jnp.broadcast_to(block[None], (count,) + block.shape), axis, 0, 0)


def swapped(array, axis):
    return lax.ppermute(array, axis, [(0, 1), (1, 0)])


def swapped_between_chips(array):
    pairs = []
    for row in range(1, lax.axis_size(TILE) - 1, 2):
        pairs += [(row, row + 1), (row + 1, row)]
    return lax.ppermute(array, TILE, pairs)


def swapped_three_apart(array):
    count = lax.axis_size(TILE)
    pairs = [(row, row + 3) for row in range(1, count - 3, 2)]
    return lax.ppermute(array, TILE, pairs + [(after, row) for row, after in pairs])


def adjoint_layers(source, hidden_one, hidden_two, weights):
    features = source.shape[1]
    depth = weights.shape[2] - features
    slope_two = 1.0 - jnp.square(hidden_two.astype(jnp.float32))
    back_two = lax.dot_general(
        source, weights[1, :, depth:], CONTRACT_LAST, preferred_element_type=jnp.float32
    )
    back_two = (slope_two * back_two).astype(jnp.bfloat16)
    back_one = lax.dot_general(
        back_two[:, :depth],
        weights[0, :, features:],
        CONTRACT_LAST,
        preferred_element_type=jnp.float32,
    ) + lax.dot_general(
        back_two[:, depth:],
        weights[1, :, :depth],
        CONTRACT_LAST,
        preferred_element_type=jnp.float32,
    )
    slope_one = 1.0 - jnp.square(hidden_one.astype(jnp.float32))
    return (slope_one * back_one).astype(jnp.bfloat16)


def first_kernel(
    state,
    increment,
    diffusivity,
    land_sea,
    col,
    lev,
    val,
    prec,
    w_in,
    w_mid,
    w_out,
    rows,
    edges,
    outer,
):
    features = w_in.shape[1]
    rows[:, :features] = w_in[...].astype(jnp.bfloat16)
    rows[:, features:-features] = w_mid[...]
    rows[:, -features:] = w_out[...].astype(jnp.bfloat16)
    edges[...] = jnp.zeros_like(edges)
    cells = state.shape[1]
    for which, field in enumerate((state, increment, diffusivity)):
        start = 2 * REACH * which
        edges[start : start + REACH] = field[0, :REACH]
        edges[start + REACH : start + 2 * REACH] = field[0, cells - REACH :]
    edges[18:19, :cells] = 0.5 + land_sea[...].astype(jnp.float32)
    count = col.shape[1]
    for row, numbers in enumerate((col, lev, val, prec)):
        edges[19 + row : 20 + row, :count] = numbers[...].astype(jnp.float32)
    outer[...] = (state[0] + increment[0]).astype(jnp.bfloat16)


def ring_gating(mine, other):
    cells = mine.shape[1]
    lane = lax.broadcasted_iota(jnp.int32, (8, cells), 1)
    mine, other = (jnp.broadcast_to(row, (8, cells)) for row in (mine, other))
    other = jnp.where(lane < REACH, other, pltpu.roll(other, 8, 1))
    return jnp.concatenate([mine, other], axis=1)


def ring_field(field, edges, which):
    start = 2 * REACH * which
    return jnp.concatenate(
        [
            field,
            edges[start : start + REACH],
            jnp.zeros((8 - 2 * REACH, field.shape[1]), jnp.float32),
            edges[start + REACH : start + 2 * REACH],
        ]
    )


def pack_fields_kernel(state, increment, diffusivity, pack):
    cells = state.shape[1]
    for which, field in enumerate((state, increment, diffusivity)):
        pack[BLOCK * which : BLOCK * which + cells] = field[0].astype(jnp.bfloat16)


def pack_edges_kernel(fields, mine, other, pack):
    features = fields.shape[1]
    cells = BLOCK - 16
    for which in range(3):
        base, start = BLOCK * which, 2 * REACH * which
        pack[base : base + cells] = fields[base : base + cells]
        edges = [
            other[start : start + REACH],
            jnp.zeros((8 - 2 * REACH, features), jnp.float32),
            other[start + REACH : start + 2 * REACH],
            jnp.zeros((8, features), jnp.float32),
        ]
        pack[base + cells : base + BLOCK] = jnp.concatenate(edges).astype(jnp.bfloat16)
    gating = ring_gating(mine[18:19, :cells], other[18:19, :cells])[:1]
    numbers = mine[21:23, :]
    coarse = numbers.astype(jnp.bfloat16).astype(jnp.float32)
    fine = numbers - coarse
    rest = [gating, mine[19:21, :], coarse, fine, jnp.zeros((16 - 7, features), jnp.float32)]
    pack[3 * BLOCK :] = jnp.concatenate(rest).astype(jnp.bfloat16)


def whole_kernel(
    observations,
    core,
    state,
    increment,
    diffusivity,
    mine,
    other,
    near,
    far,
    beyond,
    outer,
    settled_out,
    spreading_out,
    ends_out,
    kept,
    given,
    weights,
):
    cells, features = state.shape[1:]
    depth = weights.shape[2] - features
    length = cells + 8
    pack = 3 * BLOCK + 16
    square = (length, 2 * cells)
    diagonal = lax.broadcasted_iota(jnp.int32, square, 0) == lax.broadcasted_iota(
        jnp.int32, square, 1
    )

    def column(row):
        return jnp.sum(jnp.where(diagonal, row, 0.0), axis=1, keepdims=True)

    def laplace(field, lat):
        return lat + pltpu.roll(field, 1, 0) + pltpu.roll(field, length - 1, 0) - 4.0 * field

    def unpack(ref, start):
        fields = [
            ref[start + BLOCK * i : start + BLOCK * (i + 1), :].astype(jnp.float32)[:length]
            for i in range(3)
        ]
        rest = ref[start + 3 * BLOCK : start + pack, :].astype(jnp.float32)
        return fields + [column(rest[:1])], rest

    def activate(both):
        middle = both.shape[0] // 2
        hidden = jnp.tanh(both[:middle]).astype(jnp.bfloat16).astype(jnp.float32)
        tangent = (1.0 - hidden * hidden) * both[middle:]
        return jnp.concatenate([hidden, tangent]).astype(jnp.bfloat16)

    def networks(rows):
        stacked = jnp.concatenate([row[0] for row in rows] + [row[1] for row in rows])
        stacked = stacked.astype(jnp.bfloat16)
        one = activate(
            lax.dot_general(
                stacked,
                weights[0, :, :features],
                CONTRACT_LAST,
                preferred_element_type=jnp.float32,
            )
        )
        low = activate(jnp.dot(one, weights[0, :, features:], preferred_element_type=jnp.float32))
        high = activate(jnp.dot(one, weights[1, :, :depth], preferred_element_type=jnp.float32))
        out = jnp.dot(
            low, weights[1, :depth, depth:], preferred_element_type=jnp.float32
        ) + jnp.dot(high, weights[1, depth:, depth:], preferred_element_type=jnp.float32)
        saved = (one[:cells], jnp.concatenate([low[:cells], high[:cells]], axis=1), stacked[:cells])
        outs = [out[i * length : (i + 1) * length] for i in range(2 * len(rows))]
        return list(zip(outs[: len(rows)], outs[len(rows) :])), saved

    def exactly(left, ones, contract):
        total, ones = 0.0, ones.astype(jnp.bfloat16)
        for _ in range(3):
            term = left.astype(jnp.bfloat16)
            total = total + lax.dot_general(
                term, ones, contract, preferred_element_type=jnp.float32
            )
            left = left - term.astype(jnp.float32)
        return total

    def observed(final, columns, levels, values, precisions):
        count = columns.shape[1]
        cell_ids = lax.broadcasted_iota(jnp.int32, (length, count), 0).astype(jnp.float32)
        level_ids = lax.broadcasted_iota(jnp.int32, (features, count), 0).astype(jnp.float32)
        pick_cell = (cell_ids == columns).astype(jnp.float32)
        pick_level = (level_ids == levels).astype(jnp.float32)
        at_level = exactly(final, pick_level, (((1,), (0,)), ((), ())))
        modelled = jnp.sum(pick_cell * at_level, axis=0, keepdims=True)
        return exactly(pick_cell * (precisions * (modelled - values)), pick_level, CONTRACT_LAST)

    own = [ring_field(ref[0], other, i) for i, ref in enumerate((state, increment, diffusivity))]
    gate = column(ring_gating(mine[18:19, :cells], other[18:19, :cells])[:1])
    own.append(gate)
    beside, beside_rest = zip(unpack(near, 0), unpack(far, 0))
    second = [unpack(beyond, 0)[0], unpack(far, pack)[0]]
    third = [unpack(beyond, pack)[0]]
    third = [
        third[0][0] + third[0][1],
        jnp.concatenate(
            [outer[...].astype(jnp.float32), jnp.zeros((length - cells, features), jnp.float32)]
        ),
    ]

    def advance(row, lats, moved):
        states, tangents, diffuse, gated = row
        return (
            states + diffuse * laplace(states, lats[0]) + gated * moved[0],
            tangents + diffuse * laplace(tangents, lats[1]) + gated * moved[1],
        )

    def advance_sum(row, middle, lat, moved):
        return middle + row[2] * laplace(middle, lat) + row[3] * (moved[0] + moved[1])

    groups = ((0,), (1, 2), (3, 4))
    all_rows = [own] + list(beside) + second
    moved = []
    first = None
    for group in groups:
        got, saved = networks([all_rows[i] for i in group])
        moved += got
        first = saved if first is None else first
    state_one, increment_one = advance(
        own, [beside[0][i] + beside[1][i] for i in range(2)], moved[0]
    )
    middle_one = state_one + increment_one
    beside_one, beside_middle, second_middle = [], [], []
    for i, (row, next_row, last) in enumerate(zip(beside, second, third)):
        one = advance(row, [own[j] + next_row[j] for j in range(2)], moved[1 + i])
        beside_one.append(one)
        beside_middle.append(one[0] + one[1])
        next_sum = next_row[0] + next_row[1]
        second_middle.append(advance_sum(next_row, next_sum, row[0] + row[1] + last, moved[3 + i]))
    all_rows = [(state_one, increment_one)] + beside_one
    late, moved = None, []
    for group in ((0,), (1, 2)):
        got, saved = networks([all_rows[i] for i in group])
        moved += got
        late = saved if late is None else late
    final = advance_sum(own, middle_one, beside_middle[0] + beside_middle[1], moved[0])
    count = observations
    columns = other[19:20, :count]
    columns = jnp.where(
        columns == 0.0, float(cells), jnp.where(columns == cells - 1.0, length - 1.0, -1.0)
    )
    columns = jnp.concatenate([mine[19:20, :count], columns], axis=1)
    chosen = [
        jnp.concatenate([mine[i : i + 1, :count], other[i : i + 1, :count]], axis=1)
        for i in (20, 21, 22)
    ]
    adjoint = observed(final, columns, *chosen)
    around = jnp.zeros_like(adjoint)
    for row, middle, next_middle, rest, moves in zip(
        beside, beside_middle, second_middle, beside_rest, moved[1:]
    ):
        total = advance_sum(row, middle, middle_one + next_middle, moves)
        around = around + row[2] * observed(
            total,
            rest[1:2, :cells],
            rest[2:3, :cells],
            rest[3:4, :cells] + rest[5:6, :cells],
            rest[4:5, :cells] + rest[6:7, :cells],
        )
    spreading = own[2] * adjoint
    adjoint_one = (adjoint + laplace(spreading, around))[:cells]
    gate = gate[:cells]
    source_late = (gate * adjoint[:cells]).astype(jnp.bfloat16)
    back_late = adjoint_layers(source_late, late[0], late[1], weights)
    adjoint_one = adjoint_one + jnp.dot(
        back_late, weights[0, :, :features], preferred_element_type=jnp.float32
    )
    spreading = own[2][:cells] * adjoint_one
    spreading_out[...] = spreading
    ends_out[...] = jnp.concatenate([spreading[:1], spreading[cells - 7 :]])
    source = (gate * adjoint_one).astype(jnp.bfloat16)
    back_one = adjoint_layers(source, first[0], first[1], weights)
    settled_out[...] = (
        adjoint_one
        - 4.0 * spreading
        + jnp.dot(back_one, weights[0, :, :features], preferred_element_type=jnp.float32)
    )
    first_core = core[0] == 0
    lefts = [jnp.concatenate([back_late, back_one]), jnp.concatenate([late[1], first[1]])]
    rights = [jnp.concatenate([late[2], first[2]]), jnp.concatenate([source_late, source])]
    halves, blocks, rows, width = kept.shape
    for out, which in ((given, 1), (kept, 0)):
        total = lax.dot_general(
            jnp.where(first_core, lefts[which], lefts[1 - which]),
            jnp.where(first_core, rights[which], rights[1 - which]),
            CONTRACT_FIRST,
            preferred_element_type=jnp.float32,
        ).astype(jnp.bfloat16)
        for half in range(halves):
            for block in range(blocks):
                out[half, block] = total[
                    block * rows : (block + 1) * rows, half * width : (half + 1) * width
                ]


def on_chip(kernel, outs, operands, flops, scratch=(), scalars=0, direct=0, fetched=0, place=None, room=32):
    size = sum(array.size * array.dtype.itemsize for array in list(operands) + list(outs))
    by_kernel = fetched > 0 or place is not None
    before = scalars + (direct if by_kernel else len(operands) - scalars)
    count = len(operands) - before
    places = [pltpu.SMEM] * scalars + [pltpu.VMEM] * (before - scalars) + [pl.ANY] * count
    body = kernel
    if by_kernel:
        copies = tuple(
            pltpu.VMEM(array.shape, array.dtype)
            for array in operands[before : before + fetched]
        )
        scratch = copies + (pltpu.SemaphoreType.DMA((count,)),) + tuple(scratch)

        def body(*refs):
            numbers, ready = refs[:scalars], refs[scalars:before]
            sources, refs = refs[before : before + count], refs[before + count :]
            results, refs = refs[: len(outs)], refs[len(outs) :]
            held, done, rest = refs[:fetched], refs[fetched], refs[fetched + 1 :]
            targets = list(held)
            if place is not None:
                targets += place(numbers, rest)
            moves = [
                pltpu.make_async_copy(source, target, done.at[i])
                for i, (source, target) in enumerate(zip(sources, targets))
            ]
            for move in moves:
                move.start()
            for move in moves:
                move.wait()
            kernel(*numbers, *ready, *held, *results, *rest)

    return pl.pallas_call(
        body,
        out_shape=outs,
        in_specs=[pl.BlockSpec(memory_space=place_) for place_ in places],
        out_specs=[pl.BlockSpec(memory_space=pltpu.VMEM)] * len(outs),
        scratch_shapes=scratch,
        compiler_params=pltpu.CompilerParams(vmem_limit_bytes=room * 1024 * 1024),
        cost_estimate=pl.CostEstimate(flops=flops, bytes_accessed=size, transcendentals=0),
    )(*operands)


def sum_and_spread_kernel(parts, copies):
    total = jnp.sum(parts[...].astype(jnp.float32), axis=0).astype(jnp.bfloat16)
    copies[...] = jnp.broadcast_to(total[None], copies.shape)


def sum_and_square_kernel(place, parts, copies, total):
    total[...] = jnp.sum(parts[...].astype(jnp.float32), axis=0)
    depth = copies.shape[1] // 2
    own = total[pl.ds(pl.multiple_of(place[0] * depth, depth), depth), :]
    squares = jnp.sum(total[...] * total[...], axis=0, keepdims=True)
    terms = []
    for _ in range(3):
        terms.append(squares.astype(jnp.bfloat16).astype(jnp.float32))
        squares = squares - terms[-1]
    rest = jnp.zeros((depth - len(terms), squares.shape[1]), jnp.float32)
    both = jnp.concatenate([own] + terms + [rest]).astype(jnp.bfloat16)
    copies[...] = jnp.broadcast_to(both[None], copies.shape)


def update_kernel(blocks, count, place, parts_ref, w_in, w_out, new_in, new_out):
    depth = parts_ref.shape[1] // 2
    shard = w_in.shape[0]
    parts = parts_ref[...].astype(jnp.float32)
    squares = jnp.sum(parts, axis=0)[depth:]
    square_sum = jnp.sum(jnp.sum(squares, axis=0, keepdims=True), axis=1, keepdims=True)
    scale = LEARN_RATE / jnp.sqrt(square_sum / count + EPSILON)
    for which, (old, new) in enumerate(((w_in, new_in), (w_out, new_out))):
        sides = []
        for half in range(2):
            rows = parts_ref[(half * blocks + place[0]) * 2 + which].astype(jnp.float32)[:depth]
            sides.append(jnp.where(place[1] == 0, rows[:shard], rows[shard:]))
        new[...] = old[...] - scale * jnp.concatenate(sides, axis=1)


def add_kernel(left, right, total):
    total[...] = (left[...].astype(jnp.float32) + right[...].astype(jnp.float32)).astype(
        jnp.bfloat16
    )


def updated(kept, given, w_in, w_out, soon, later):
    halves, blocks, rows, columns = kept.shape
    peers = halves * blocks
    (grads,) = on_chip(
        add_kernel,
        (jax.ShapeDtypeStruct((peers, rows, columns), jnp.bfloat16),),
        (kept.reshape(peers, rows, columns), swapped(given, "core").reshape(peers, rows, columns)),
        kept.size,
    )
    grads = lax.all_to_all(grads, AROUND[:-1], 0, 0)
    grads, soon = lax.optimization_barrier((grads, soon))
    for axis in ("z_lo", "z_hi"):
        count = lax.axis_size(axis)
        (copies,) = on_chip(
            sum_and_spread_kernel,
            (jax.ShapeDtypeStruct((count, rows, columns), jnp.bfloat16),),
            (grads,),
            grads.size,
        )
        grads = lax.all_to_all(copies, axis, 0, 0)
        if axis == "z_lo":
            grads, later = lax.optimization_barrier((grads, later))
    peers *= lax.axis_size("core")
    depth = rows // lax.axis_size(Z)
    (copies,) = on_chip(
        sum_and_square_kernel,
        (jax.ShapeDtypeStruct((peers, 2 * depth, columns), jnp.bfloat16),),
        (lax.axis_index(Z)[None], grads),
        grads.size,
        scratch=(pltpu.VMEM((rows, columns), jnp.float32),),
        scalars=1,
    )
    parts = lax.all_to_all(copies, AROUND, 0, 0)
    place = jnp.stack([lax.axis_index(("x_lo", "y")), lax.axis_index("core")])
    shape = jax.ShapeDtypeStruct(w_in.shape, jnp.float32)
    new_in, new_out = on_chip(
        functools.partial(update_kernel, blocks, float(peers * rows * columns)),
        (shape, shape),
        (place, parts, w_in, w_out),
        parts.size,
        scalars=1,
    )
    return new_in, new_out, soon, later


def local(
    state, increment, diffusivity, land_sea, w_in, w_mid, w_out, obs_col, obs_lev, obs_val, obs_prec
):
    _, cells, features = state.shape
    length = cells + 8
    observed = [numbers[None] for numbers in (obs_col, obs_lev, obs_val, obs_prec)]

    def outs(*shapes):
        return tuple(jax.ShapeDtypeStruct(shape, kind) for shape, kind in shapes)

    columns = 2 * features + w_mid.shape[1]
    width = columns // lax.axis_size("core")
    rows, mine, outer = on_chip(
        first_kernel,
        outs(
            ((w_in.shape[0], columns), jnp.bfloat16),
            ((24, features), jnp.float32),
            ((cells, features), jnp.bfloat16),
        ),
        (state, increment, diffusivity, land_sea, *observed, w_in, w_mid, w_out),
        0,
        fetched=11,
        room=56,
    )
    rows = lax.all_gather(rows, "core", axis=0, tiled=True)
    half = lax.dynamic_slice_in_dim(rows, lax.axis_index("core") * width, width, 1)
    fields = (state, increment, diffusivity)
    half, mine, outer, fields = lax.optimization_barrier((half, mine, outer, fields))
    half = spread(half, Z).reshape(-1, width)
    other = swapped(mine, "x_hi")
    outer = swapped_three_apart(outer)
    packed = outs(((3 * BLOCK + 16, features), jnp.bfloat16))
    (packs,) = on_chip(pack_fields_kernel, packed, fields, 0, fetched=3)
    (own,) = on_chip(pack_edges_kernel, packed, (packs, mine, other), 0)
    near = swapped(own, "core")
    half, near = lax.optimization_barrier((half, near))
    half = spread(half, ("x_lo", "y")).reshape(-1, width)
    far = swapped_between_chips(jnp.concatenate([own, near]))
    far, outer = lax.optimization_barrier((far, outer))
    beyond = swapped(far, "core")
    half, far, beyond = lax.optimization_barrier((half, far, beyond))
    hidden_units = half.shape[0]
    blocks = lax.axis_size(("x_lo", "y"))
    halves = lax.axis_size("x_hi")
    part = ((halves, blocks, hidden_units // blocks, features // halves), jnp.bfloat16)
    narrow = ((cells, features), jnp.float32)
    settled, spreading, ends, kept, given = on_chip(
        functools.partial(whole_kernel, obs_col.shape[0]),
        outs(
            narrow,
            narrow,
            ((8, features), jnp.float32),
            part,
            part,
        ),
        (lax.axis_index("core")[None], state, increment, diffusivity, mine, other, near, far, beyond, outer)
        + (half, swapped(half, "core")),
        40 * cells * hidden_units * (2 * features + hidden_units),
        scratch=(pltpu.VMEM((2, hidden_units, width), jnp.bfloat16),),
        scalars=1,
        direct=9,
        fetched=0,
        place=lambda numbers, rest: [
            rest[0].at[numbers[0][0]],
            rest[0].at[1 - numbers[0][0]],
        ],
    )
    w_in_new, w_out_new, ends, spreading = updated(
        kept, given, w_in, w_out, ends, spreading
    )
    ends = swapped(ends, "x_hi")
    far = swapped_between_chips(spreading)
    near = swapped(spreading, "core")
    east = jnp.concatenate([spreading[1:], ends[:1]])
    west = jnp.concatenate([ends[-1:], spreading[:-1]])
    adjoint = settled + (far + near + east + west)
    return adjoint[None], w_in_new, w_out_new


def solution(mesh):
    fine = Mesh(mesh.devices.reshape(FINE_SIZES), FINE_AXES)
    everywhere = TILE + ("x_hi",)
    return jax.shard_map(
        local,
        mesh=fine,
        in_specs=(
            P(TILE, "x_hi", None),
            P(TILE, "x_hi", None),
            P(TILE, "x_hi", None),
            P(TILE, "x_hi"),
            P(TILE, None),
            P(TILE, None),
            P(TILE, None),
            P(everywhere),
            P(everywhere),
            P(everywhere),
            P(everywhere),
        ),
        out_specs=(P(TILE, "x_hi", None), P(TILE, None), P(TILE, None)),
        check_vma=False,
    )
```

```python
import functools

import jax
import jax.numpy as jnp
from jax import lax
from jax.experimental import pallas as pl
from jax.experimental.pallas import tpu as pltpu
from jax.sharding import Mesh
from jax.sharding import PartitionSpec as P

LEARN_RATE = 0.02
EPSILON = 1e-06
CONTRACT_LAST = (((1,), (1,)), ((), ()))
CONTRACT_FIRST = (((0,), (0,)), ((), ()))
FINE_AXES = ("x_lo", "y", "z_hi", "z_lo", "core", "x_hi")
FINE_SIZES = (2, 4, 4, 4, 2, 2)
Z = ("z_hi", "z_lo")
TILE = ("x_lo", "y", "z_hi", "z_lo", "core")
AROUND = ("x_hi", "x_lo", "y", "core")
ACROSS = ("x_lo", "y", "core", "x_hi")
REACH = 3
BLOCK = 144


def spread(block, axis):
    count = lax.axis_size(axis)
    return lax.all_to_all(jnp.broadcast_to(block[None], (count,) + block.shape), axis, 0, 0)


def spread_across_x(block):
    sizes = [lax.axis_size(axis) for axis in ACROSS]
    lows, highs, cores = sizes[0], sizes[3], sizes[2]
    groups = []
    for core in range(cores):
        for high in range(highs):
            group = []
            for low in range(lows):
                side = (high + 1) % highs if core == 1 and low == 0 else high
                for y in range(sizes[1]):
                    group.append(((low * sizes[1] + y) * cores + core) * highs + side)
            groups.append(group)
    count = len(groups[0])
    return lax.all_to_all(
        jnp.broadcast_to(block[None], (count,) + block.shape),
        ACROSS,
        0,
        0,
        axis_index_groups=groups,
    )


def swapped(array, axis):
    return lax.ppermute(array, axis, [(0, 1), (1, 0)])


def swapped_between_chips(array):
    pairs = []
    for row in range(1, lax.axis_size(TILE) - 1, 2):
        pairs += [(row, row + 1), (row + 1, row)]
    return lax.ppermute(array, TILE, pairs)


def swapped_three_apart(array):
    count = lax.axis_size(TILE)
    pairs = [(row, row + 3) for row in range(1, count - 3, 2)]
    return lax.ppermute(array, TILE, pairs + [(after, row) for row, after in pairs])


def adjoint_layers(source, hidden_one, hidden_two, weights):
    features = source.shape[1]
    depth = weights.shape[2] - features
    slope_two = 1.0 - jnp.square(hidden_two.astype(jnp.float32))
    back_two = lax.dot_general(
        source, weights[1, :, depth:], CONTRACT_LAST, preferred_element_type=jnp.float32
    )
    back_two = (slope_two * back_two).astype(jnp.bfloat16)
    back_one = lax.dot_general(
        back_two[:, :depth],
        weights[0, :, features:],
        CONTRACT_LAST,
        preferred_element_type=jnp.float32,
    ) + lax.dot_general(
        back_two[:, depth:],
        weights[1, :, :depth],
        CONTRACT_LAST,
        preferred_element_type=jnp.float32,
    )
    slope_one = 1.0 - jnp.square(hidden_one.astype(jnp.float32))
    return (slope_one * back_one).astype(jnp.bfloat16)


def first_kernel(
    state,
    increment,
    diffusivity,
    land_sea,
    col,
    lev,
    val,
    prec,
    w_in,
    w_mid,
    w_out,
    rows,
    edges,
    outer,
):
    features = w_in.shape[1]
    rows[:, :features] = w_in[...].astype(jnp.bfloat16)
    rows[:, features:-features] = w_mid[...]
    rows[:, -features:] = w_out[...].astype(jnp.bfloat16)
    edges[...] = jnp.zeros_like(edges)
    cells = state.shape[1]
    for which, field in enumerate((state, increment, diffusivity)):
        start = 2 * REACH * which
        edges[start : start + REACH] = field[0, :REACH]
        edges[start + REACH : start + 2 * REACH] = field[0, cells - REACH :]
    edges[18:19, :cells] = 0.5 + land_sea[...].astype(jnp.float32)
    count = col.shape[1]
    for row, numbers in enumerate((col, lev, val, prec)):
        edges[19 + row : 20 + row, :count] = numbers[...].astype(jnp.float32)
    outer[...] = (state[0] + increment[0]).astype(jnp.bfloat16)


def ring_gating(mine, other):
    cells = mine.shape[1]
    lane = lax.broadcasted_iota(jnp.int32, (8, cells), 1)
    mine, other = (jnp.broadcast_to(row, (8, cells)) for row in (mine, other))
    other = jnp.where(lane < REACH, other, pltpu.roll(other, 8, 1))
    return jnp.concatenate([mine, other], axis=1)


def ring_field(field, edges, which):
    start = 2 * REACH * which
    return jnp.concatenate(
        [
            field,
            edges[start : start + REACH],
            jnp.zeros((8 - 2 * REACH, field.shape[1]), jnp.float32),
            edges[start + REACH : start + 2 * REACH],
        ]
    )


def pack_fields_kernel(state, increment, diffusivity, pack):
    cells = state.shape[1]
    for which, field in enumerate((state, increment, diffusivity)):
        pack[BLOCK * which : BLOCK * which + cells] = field[0].astype(jnp.bfloat16)


def pack_edges_kernel(fields, mine, other, pack):
    features = fields.shape[1]
    cells = BLOCK - 16
    for which in range(3):
        base, start = BLOCK * which, 2 * REACH * which
        pack[base : base + cells] = fields[base : base + cells]
        edges = [
            other[start : start + REACH],
            jnp.zeros((8 - 2 * REACH, features), jnp.float32),
            other[start + REACH : start + 2 * REACH],
            jnp.zeros((8, features), jnp.float32),
        ]
        pack[base + cells : base + BLOCK] = jnp.concatenate(edges).astype(jnp.bfloat16)
    gating = ring_gating(mine[18:19, :cells], other[18:19, :cells])[:1]
    numbers = mine[21:23, :]
    coarse = numbers.astype(jnp.bfloat16).astype(jnp.float32)
    fine = numbers - coarse
    rest = [gating, mine[19:21, :], coarse, fine, jnp.zeros((16 - 7, features), jnp.float32)]
    pack[3 * BLOCK :] = jnp.concatenate(rest).astype(jnp.bfloat16)


def whole_kernel(
    observations,
    core,
    state,
    increment,
    diffusivity,
    mine,
    other,
    near,
    far,
    beyond,
    outer,
    settled_out,
    spreading_out,
    ends_out,
    kept,
    given,
    weights,
):
    cells, features = state.shape[1:]
    depth = weights.shape[2] - features
    length = cells + 8
    pack = 3 * BLOCK + 16
    square = (length, 2 * cells)
    diagonal = lax.broadcasted_iota(jnp.int32, square, 0) == lax.broadcasted_iota(
        jnp.int32, square, 1
    )

    def column(row):
        return jnp.sum(jnp.where(diagonal, row, 0.0), axis=1, keepdims=True)

    def laplace(field, lat):
        return lat + pltpu.roll(field, 1, 0) + pltpu.roll(field, length - 1, 0) - 4.0 * field

    def unpack(ref, start):
        fields = [
            ref[start + BLOCK * i : start + BLOCK * (i + 1), :].astype(jnp.float32)[:length]
            for i in range(3)
        ]
        rest = ref[start + 3 * BLOCK : start + pack, :].astype(jnp.float32)
        return fields + [column(rest[:1])], rest

    def activate(both):
        middle = both.shape[0] // 2
        hidden = jnp.tanh(both[:middle]).astype(jnp.bfloat16).astype(jnp.float32)
        tangent = (1.0 - hidden * hidden) * both[middle:]
        return jnp.concatenate([hidden, tangent]).astype(jnp.bfloat16)

    def networks(rows):
        stacked = jnp.concatenate([row[0] for row in rows] + [row[1] for row in rows])
        stacked = stacked.astype(jnp.bfloat16)
        one = activate(
            lax.dot_general(
                stacked,
                weights[0, :, :features],
                CONTRACT_LAST,
                preferred_element_type=jnp.float32,
            )
        )
        low = activate(jnp.dot(one, weights[0, :, features:], preferred_element_type=jnp.float32))
        high = activate(jnp.dot(one, weights[1, :, :depth], preferred_element_type=jnp.float32))
        out = jnp.dot(
            low, weights[1, :depth, depth:], preferred_element_type=jnp.float32
        ) + jnp.dot(high, weights[1, depth:, depth:], preferred_element_type=jnp.float32)
        saved = (one[:cells], jnp.concatenate([low[:cells], high[:cells]], axis=1), stacked[:cells])
        outs = [out[i * length : (i + 1) * length] for i in range(2 * len(rows))]
        return list(zip(outs[: len(rows)], outs[len(rows) :])), saved

    def exactly(left, ones, contract):
        total, ones = 0.0, ones.astype(jnp.bfloat16)
        for _ in range(3):
            term = left.astype(jnp.bfloat16)
            total = total + lax.dot_general(
                term, ones, contract, preferred_element_type=jnp.float32
            )
            left = left - term.astype(jnp.float32)
        return total

    def observed(final, columns, levels, values, precisions):
        count = columns.shape[1]
        cell_ids = lax.broadcasted_iota(jnp.int32, (length, count), 0).astype(jnp.float32)
        level_ids = lax.broadcasted_iota(jnp.int32, (features, count), 0).astype(jnp.float32)
        pick_cell = (cell_ids == columns).astype(jnp.float32)
        pick_level = (level_ids == levels).astype(jnp.float32)
        at_level = exactly(final, pick_level, (((1,), (0,)), ((), ())))
        modelled = jnp.sum(pick_cell * at_level, axis=0, keepdims=True)
        return exactly(pick_cell * (precisions * (modelled - values)), pick_level, CONTRACT_LAST)

    own = [ring_field(ref[0], other, i) for i, ref in enumerate((state, increment, diffusivity))]
    gate = column(ring_gating(mine[18:19, :cells], other[18:19, :cells])[:1])
    own.append(gate)
    beside, beside_rest = zip(unpack(near, 0), unpack(far, 0))
    second = [unpack(beyond, 0)[0], unpack(far, pack)[0]]
    third = [unpack(beyond, pack)[0]]
    third = [
        third[0][0] + third[0][1],
        jnp.concatenate(
            [outer[...].astype(jnp.float32), jnp.zeros((length - cells, features), jnp.float32)]
        ),
    ]

    def advance(row, lats, moved):
        states, tangents, diffuse, gated = row
        return (
            states + diffuse * laplace(states, lats[0]) + gated * moved[0],
            tangents + diffuse * laplace(tangents, lats[1]) + gated * moved[1],
        )

    def advance_sum(row, middle, lat, moved):
        return middle + row[2] * laplace(middle, lat) + row[3] * (moved[0] + moved[1])

    groups = ((0,), (1, 2), (3, 4))
    all_rows = [own] + list(beside) + second
    moved = []
    first = None
    for group in groups:
        got, saved = networks([all_rows[i] for i in group])
        moved += got
        first = saved if first is None else first
    state_one, increment_one = advance(
        own, [beside[0][i] + beside[1][i] for i in range(2)], moved[0]
    )
    middle_one = state_one + increment_one
    beside_one, beside_middle, second_middle = [], [], []
    for i, (row, next_row, last) in enumerate(zip(beside, second, third)):
        one = advance(row, [own[j] + next_row[j] for j in range(2)], moved[1 + i])
        beside_one.append(one)
        beside_middle.append(one[0] + one[1])
        next_sum = next_row[0] + next_row[1]
        second_middle.append(advance_sum(next_row, next_sum, row[0] + row[1] + last, moved[3 + i]))
    all_rows = [(state_one, increment_one)] + beside_one
    late, moved = None, []
    for group in ((0,), (1, 2)):
        got, saved = networks([all_rows[i] for i in group])
        moved += got
        late = saved if late is None else late
    final = advance_sum(own, middle_one, beside_middle[0] + beside_middle[1], moved[0])
    count = observations
    columns = other[19:20, :count]
    columns = jnp.where(
        columns == 0.0, float(cells), jnp.where(columns == cells - 1.0, length - 1.0, -1.0)
    )
    columns = jnp.concatenate([mine[19:20, :count], columns], axis=1)
    chosen = [
        jnp.concatenate([mine[i : i + 1, :count], other[i : i + 1, :count]], axis=1)
        for i in (20, 21, 22)
    ]
    adjoint = observed(final, columns, *chosen)
    around = jnp.zeros_like(adjoint)
    for row, middle, next_middle, rest, moves in zip(
        beside, beside_middle, second_middle, beside_rest, moved[1:]
    ):
        total = advance_sum(row, middle, middle_one + next_middle, moves)
        around = around + row[2] * observed(
            total,
            rest[1:2, :cells],
            rest[2:3, :cells],
            rest[3:4, :cells] + rest[5:6, :cells],
            rest[4:5, :cells] + rest[6:7, :cells],
        )
    spreading = own[2] * adjoint
    adjoint_one = (adjoint + laplace(spreading, around))[:cells]
    gate = gate[:cells]
    source_late = (gate * adjoint[:cells]).astype(jnp.bfloat16)
    back_late = adjoint_layers(source_late, late[0], late[1], weights)
    adjoint_one = adjoint_one + jnp.dot(
        back_late, weights[0, :, :features], preferred_element_type=jnp.float32
    )
    spreading = own[2][:cells] * adjoint_one
    spreading_out[...] = spreading
    ends_out[...] = jnp.concatenate([spreading[:1], spreading[cells - 7 :]])
    source = (gate * adjoint_one).astype(jnp.bfloat16)
    back_one = adjoint_layers(source, first[0], first[1], weights)
    settled_out[...] = (
        adjoint_one
        - 4.0 * spreading
        + jnp.dot(back_one, weights[0, :, :features], preferred_element_type=jnp.float32)
    )
    first_core = core[0] == 0
    lefts = [jnp.concatenate([back_late, back_one]), jnp.concatenate([late[1], first[1]])]
    rights = [jnp.concatenate([late[2], first[2]]), jnp.concatenate([source_late, source])]
    halves, blocks, rows, width = kept.shape
    for out, which in ((given, 1), (kept, 0)):
        total = lax.dot_general(
            jnp.where(first_core, lefts[which], lefts[1 - which]),
            jnp.where(first_core, rights[which], rights[1 - which]),
            CONTRACT_FIRST,
            preferred_element_type=jnp.float32,
        ).astype(jnp.bfloat16)
        for half in range(halves):
            for block in range(blocks):
                out[half, block] = total[
                    block * rows : (block + 1) * rows, half * width : (half + 1) * width
                ]


def on_chip(kernel, outs, operands, flops, scratch=(), scalars=0, direct=0, fetched=0, place=None, room=32):
    size = sum(array.size * array.dtype.itemsize for array in list(operands) + list(outs))
    by_kernel = fetched > 0 or place is not None
    before = scalars + (direct if by_kernel else len(operands) - scalars)
    count = len(operands) - before
    places = [pltpu.SMEM] * scalars + [pltpu.VMEM] * (before - scalars) + [pl.ANY] * count
    body = kernel
    if by_kernel:
        copies = tuple(
            pltpu.VMEM(array.shape, array.dtype)
            for array in operands[before : before + fetched]
        )
        scratch = copies + (pltpu.SemaphoreType.DMA((count,)),) + tuple(scratch)

        def body(*refs):
            numbers, ready = refs[:scalars], refs[scalars:before]
            sources, refs = refs[before : before + count], refs[before + count :]
            results, refs = refs[: len(outs)], refs[len(outs) :]
            held, done, rest = refs[:fetched], refs[fetched], refs[fetched + 1 :]
            targets = list(held)
            if place is not None:
                targets += place(numbers, rest)
            moves = [
                pltpu.make_async_copy(source, target, done.at[i])
                for i, (source, target) in enumerate(zip(sources, targets))
            ]
            for move in moves:
                move.start()
            for move in moves:
                move.wait()
            kernel(*numbers, *ready, *held, *results, *rest)

    return pl.pallas_call(
        body,
        out_shape=outs,
        in_specs=[pl.BlockSpec(memory_space=place_) for place_ in places],
        out_specs=[pl.BlockSpec(memory_space=pltpu.VMEM)] * len(outs),
        scratch_shapes=scratch,
        compiler_params=pltpu.CompilerParams(vmem_limit_bytes=room * 1024 * 1024),
        cost_estimate=pl.CostEstimate(flops=flops, bytes_accessed=size, transcendentals=0),
    )(*operands)


def sum_and_spread_kernel(parts, copies):
    total = jnp.sum(parts[...].astype(jnp.float32), axis=0).astype(jnp.bfloat16)
    copies[...] = jnp.broadcast_to(total[None], copies.shape)


def sum_and_square_kernel(place, parts, copies, total):
    total[...] = jnp.sum(parts[...].astype(jnp.float32), axis=0)
    depth = copies.shape[1] // 2
    own = total[pl.ds(pl.multiple_of(place[0] * depth, depth), depth), :]
    squares = jnp.sum(total[...] * total[...], axis=0, keepdims=True)
    terms = []
    for _ in range(3):
        terms.append(squares.astype(jnp.bfloat16).astype(jnp.float32))
        squares = squares - terms[-1]
    rest = jnp.zeros((depth - len(terms), squares.shape[1]), jnp.float32)
    both = jnp.concatenate([own] + terms + [rest]).astype(jnp.bfloat16)
    copies[...] = jnp.broadcast_to(both[None], copies.shape)


def update_kernel(blocks, count, place, parts_ref, w_in, w_out, new_in, new_out):
    depth = parts_ref.shape[1] // 2
    shard = w_in.shape[0]
    parts = parts_ref[...].astype(jnp.float32)
    squares = jnp.sum(parts, axis=0)[depth:]
    square_sum = jnp.sum(jnp.sum(squares, axis=0, keepdims=True), axis=1, keepdims=True)
    scale = LEARN_RATE / jnp.sqrt(square_sum / count + EPSILON)
    for which, (old, new) in enumerate(((w_in, new_in), (w_out, new_out))):
        sides = []
        for half in range(2):
            rows = parts_ref[(half * blocks + place[0]) * 2 + which].astype(jnp.float32)[:depth]
            sides.append(jnp.where(place[1] == 0, rows[:shard], rows[shard:]))
        new[...] = old[...] - scale * jnp.concatenate(sides, axis=1)


def add_kernel(left, right, total):
    total[...] = (left[...].astype(jnp.float32) + right[...].astype(jnp.float32)).astype(
        jnp.bfloat16
    )


def updated(kept, given, w_in, w_out, soon, later):
    halves, blocks, rows, columns = kept.shape
    peers = halves * blocks
    (grads,) = on_chip(
        add_kernel,
        (jax.ShapeDtypeStruct((peers, rows, columns), jnp.bfloat16),),
        (kept.reshape(peers, rows, columns), swapped(given, "core").reshape(peers, rows, columns)),
        kept.size,
    )
    grads = lax.all_to_all(grads, AROUND[:-1], 0, 0)
    grads, soon = lax.optimization_barrier((grads, soon))
    for axis in ("z_lo", "z_hi"):
        count = lax.axis_size(axis)
        (copies,) = on_chip(
            sum_and_spread_kernel,
            (jax.ShapeDtypeStruct((count, rows, columns), jnp.bfloat16),),
            (grads,),
            grads.size,
        )
        grads = lax.all_to_all(copies, axis, 0, 0)
        if axis == "z_lo":
            grads, later = lax.optimization_barrier((grads, later))
    peers *= lax.axis_size("core")
    depth = rows // lax.axis_size(Z)
    (copies,) = on_chip(
        sum_and_square_kernel,
        (jax.ShapeDtypeStruct((peers, 2 * depth, columns), jnp.bfloat16),),
        (lax.axis_index(Z)[None], grads),
        grads.size,
        scratch=(pltpu.VMEM((rows, columns), jnp.float32),),
        scalars=1,
    )
    parts = lax.all_to_all(copies, AROUND, 0, 0)
    place = jnp.stack([lax.axis_index(("x_lo", "y")), lax.axis_index("core")])
    shape = jax.ShapeDtypeStruct(w_in.shape, jnp.float32)
    new_in, new_out = on_chip(
        functools.partial(update_kernel, blocks, float(peers * rows * columns)),
        (shape, shape),
        (place, parts, w_in, w_out),
        parts.size,
        scalars=1,
    )
    return new_in, new_out, soon, later


def local(
    state, increment, diffusivity, land_sea, w_in, w_mid, w_out, obs_col, obs_lev, obs_val, obs_prec
):
    _, cells, features = state.shape
    length = cells + 8
    observed = [numbers[None] for numbers in (obs_col, obs_lev, obs_val, obs_prec)]

    def outs(*shapes):
        return tuple(jax.ShapeDtypeStruct(shape, kind) for shape, kind in shapes)

    columns = 2 * features + w_mid.shape[1]
    width = columns // lax.axis_size("core")
    rows, mine, outer = on_chip(
        first_kernel,
        outs(
            ((w_in.shape[0], columns), jnp.bfloat16),
            ((24, features), jnp.float32),
            ((cells, features), jnp.bfloat16),
        ),
        (state, increment, diffusivity, land_sea, *observed, w_in, w_mid, w_out),
        0,
        fetched=11,
        room=56,
    )
    rows = lax.all_gather(rows, "core", axis=0, tiled=True)
    half = lax.dynamic_slice_in_dim(rows, lax.axis_index("core") * width, width, 1)
    fields = (state, increment, diffusivity)
    half, mine, outer, fields = lax.optimization_barrier((half, mine, outer, fields))
    half = spread(half, Z).reshape(-1, width)
    other = swapped(mine, "x_hi")
    outer = swapped_three_apart(outer)
    packed = outs(((3 * BLOCK + 16, features), jnp.bfloat16))
    (packs,) = on_chip(pack_fields_kernel, packed, fields, 0, fetched=3)
    (own,) = on_chip(pack_edges_kernel, packed, (packs, mine, other), 0)
    near = swapped(own, "core")
    half, near = lax.optimization_barrier((half, near))
    half = spread_across_x(half).reshape(-1, width)
    far = swapped_between_chips(jnp.concatenate([own, near]))
    far, outer = lax.optimization_barrier((far, outer))
    beyond = swapped(far, "core")
    half, far, beyond = lax.optimization_barrier((half, far, beyond))
    hidden_units = half.shape[0]
    blocks = lax.axis_size(("x_lo", "y"))
    halves = lax.axis_size("x_hi")
    part = ((halves, blocks, hidden_units // blocks, features // halves), jnp.bfloat16)
    narrow = ((cells, features), jnp.float32)
    settled, spreading, ends, kept, given = on_chip(
        functools.partial(whole_kernel, obs_col.shape[0]),
        outs(
            narrow,
            narrow,
            ((8, features), jnp.float32),
            part,
            part,
        ),
        (lax.axis_index("core")[None], state, increment, diffusivity, mine, other, near, far, beyond, outer)
        + (half, swapped(half, "core")),
        40 * cells * hidden_units * (2 * features + hidden_units),
        scratch=(pltpu.VMEM((2, hidden_units, width), jnp.bfloat16),),
        scalars=1,
        direct=9,
        fetched=0,
        place=lambda numbers, rest: [
            rest[0].at[numbers[0][0]],
            rest[0].at[1 - numbers[0][0]],
        ],
    )
    w_in_new, w_out_new, ends, spreading = updated(
        kept, given, w_in, w_out, ends, spreading
    )
    ends = swapped(ends, "x_hi")
    far = swapped_between_chips(spreading)
    near = swapped(spreading, "core")
    east = jnp.concatenate([spreading[1:], ends[:1]])
    west = jnp.concatenate([ends[-1:], spreading[:-1]])
    adjoint = settled + (far + near + east + west)
    return adjoint[None], w_in_new, w_out_new


def solution(mesh):
    fine = Mesh(mesh.devices.reshape(FINE_SIZES), FINE_AXES)
    everywhere = TILE + ("x_hi",)
    return jax.shard_map(
        local,
        mesh=fine,
        in_specs=(
            P(TILE, "x_hi", None),
            P(TILE, "x_hi", None),
            P(TILE, "x_hi", None),
            P(TILE, "x_hi"),
            P(TILE, None),
            P(TILE, None),
            P(TILE, None),
            P(everywhere),
            P(everywhere),
            P(everywhere),
            P(everywhere),
        ),
        out_specs=(P(TILE, "x_hi", None), P(TILE, None), P(TILE, None)),
        check_vma=False,
    )
```

```python
import functools

import jax
import jax.numpy as jnp
from jax import lax
from jax.experimental import pallas as pl
from jax.experimental.pallas import tpu as pltpu
from jax.sharding import Mesh
from jax.sharding import PartitionSpec as P

LEARN_RATE = 0.02
EPSILON = 1e-06
CONTRACT_LAST = (((1,), (1,)), ((), ()))
CONTRACT_FIRST = (((0,), (0,)), ((), ()))
FINE_AXES = ("x_lo", "y", "z_hi", "z_lo", "core", "x_hi")
FINE_SIZES = (2, 4, 4, 4, 2, 2)
Z = ("z_hi", "z_lo")
TILE = ("x_lo", "y", "z_hi", "z_lo", "core")
AROUND = ("x_hi", "x_lo", "y", "core")
ACROSS = ("x_lo", "y", "core", "x_hi")
REACH = 3
BLOCK = 144


def spread(block, axis):
    count = lax.axis_size(axis)
    return lax.all_to_all(jnp.broadcast_to(block[None], (count,) + block.shape), axis, 0, 0)


def spread_across_x(block):
    sizes = [lax.axis_size(axis) for axis in ACROSS]
    lows, highs, cores = sizes[0], sizes[3], sizes[2]
    groups = []
    for core in range(cores):
        for high in range(highs):
            group = []
            for low in range(lows):
                side = (high + 1) % highs if core == 1 and low == 0 else high
                for y in range(sizes[1]):
                    group.append(((low * sizes[1] + y) * cores + core) * highs + side)
            groups.append(group)
    count = len(groups[0])
    return lax.all_to_all(
        jnp.broadcast_to(block[None], (count,) + block.shape),
        ACROSS,
        0,
        0,
        axis_index_groups=groups,
    )


def swapped(array, axis):
    return lax.ppermute(array, axis, [(0, 1), (1, 0)])


def swapped_between_chips(array):
    pairs = []
    for row in range(1, lax.axis_size(TILE) - 1, 2):
        pairs += [(row, row + 1), (row + 1, row)]
    return lax.ppermute(array, TILE, pairs)


def swapped_three_apart(array):
    count = lax.axis_size(TILE)
    pairs = [(row, row + 3) for row in range(1, count - 3, 2)]
    return lax.ppermute(array, TILE, pairs + [(after, row) for row, after in pairs])


def adjoint_layers(source, hidden_one, hidden_two, weights):
    features = source.shape[1]
    depth = weights.shape[2] - features
    slope_two = 1.0 - jnp.square(hidden_two.astype(jnp.float32))
    back_two = lax.dot_general(
        source, weights[1, :, depth:], CONTRACT_LAST, preferred_element_type=jnp.float32
    )
    back_two = (slope_two * back_two).astype(jnp.bfloat16)
    back_one = lax.dot_general(
        back_two[:, :depth],
        weights[0, :, features:],
        CONTRACT_LAST,
        preferred_element_type=jnp.float32,
    ) + lax.dot_general(
        back_two[:, depth:],
        weights[1, :, :depth],
        CONTRACT_LAST,
        preferred_element_type=jnp.float32,
    )
    slope_one = 1.0 - jnp.square(hidden_one.astype(jnp.float32))
    return (slope_one * back_one).astype(jnp.bfloat16)


def first_kernel(
    state,
    increment,
    diffusivity,
    land_sea,
    col,
    lev,
    val,
    prec,
    w_in,
    w_mid,
    w_out,
    rows,
    edges,
    outer,
):
    features = w_in.shape[1]
    rows[:, :features] = w_in[...].astype(jnp.bfloat16)
    rows[:, features:-features] = w_mid[...]
    rows[:, -features:] = w_out[...].astype(jnp.bfloat16)
    edges[...] = jnp.zeros_like(edges)
    cells = state.shape[1]
    for which, field in enumerate((state, increment, diffusivity)):
        start = 2 * REACH * which
        edges[start : start + REACH] = field[0, :REACH]
        edges[start + REACH : start + 2 * REACH] = field[0, cells - REACH :]
    edges[18:19, :cells] = 0.5 + land_sea[...].astype(jnp.float32)
    count = col.shape[1]
    for row, numbers in enumerate((col, lev, val, prec)):
        edges[19 + row : 20 + row, :count] = numbers[...].astype(jnp.float32)
    outer[...] = (state[0] + increment[0]).astype(jnp.bfloat16)


def ring_gating(mine, other):
    cells = mine.shape[1]
    lane = lax.broadcasted_iota(jnp.int32, (8, cells), 1)
    mine, other = (jnp.broadcast_to(row, (8, cells)) for row in (mine, other))
    other = jnp.where(lane < REACH, other, pltpu.roll(other, 8, 1))
    return jnp.concatenate([mine, other], axis=1)


def ring_field(field, edges, which):
    start = 2 * REACH * which
    return jnp.concatenate(
        [
            field,
            edges[start : start + REACH],
            jnp.zeros((8 - 2 * REACH, field.shape[1]), jnp.float32),
            edges[start + REACH : start + 2 * REACH],
        ]
    )


def pack_fields_kernel(state, increment, diffusivity, pack):
    cells = state.shape[1]
    for which, field in enumerate((state, increment, diffusivity)):
        pack[BLOCK * which : BLOCK * which + cells] = field[0].astype(jnp.bfloat16)


def pack_edges_kernel(fields, mine, other, pack):
    features = fields.shape[1]
    cells = BLOCK - 16
    for which in range(3):
        base, start = BLOCK * which, 2 * REACH * which
        pack[base : base + cells] = fields[base : base + cells]
        edges = [
            other[start : start + REACH],
            jnp.zeros((8 - 2 * REACH, features), jnp.float32),
            other[start + REACH : start + 2 * REACH],
            jnp.zeros((8, features), jnp.float32),
        ]
        pack[base + cells : base + BLOCK] = jnp.concatenate(edges).astype(jnp.bfloat16)
    gating = ring_gating(mine[18:19, :cells], other[18:19, :cells])[:1]
    numbers = mine[21:23, :]
    coarse = numbers.astype(jnp.bfloat16).astype(jnp.float32)
    fine = numbers - coarse
    rest = [gating, mine[19:21, :], coarse, fine, jnp.zeros((16 - 7, features), jnp.float32)]
    pack[3 * BLOCK :] = jnp.concatenate(rest).astype(jnp.bfloat16)


def behind_kernel(far, behind):
    pack = 3 * BLOCK + 16
    behind[:pack] = far[:pack]
    total = far[pack : pack + BLOCK].astype(jnp.float32)
    total = total + far[pack + BLOCK : pack + 2 * BLOCK].astype(jnp.float32)
    behind[pack:] = total.astype(jnp.bfloat16)


def whole_kernel(
    observations,
    core,
    state,
    increment,
    diffusivity,
    mine,
    other,
    near,
    far,
    beyond,
    outer,
    settled_out,
    spreading_out,
    ends_out,
    kept,
    given,
    weights,
):
    cells, features = state.shape[1:]
    depth = weights.shape[2] - features
    length = cells + 8
    pack = 3 * BLOCK + 16
    square = (length, 2 * cells)
    diagonal = lax.broadcasted_iota(jnp.int32, square, 0) == lax.broadcasted_iota(
        jnp.int32, square, 1
    )

    def column(row):
        return jnp.sum(jnp.where(diagonal, row, 0.0), axis=1, keepdims=True)

    def laplace(field, lat):
        return lat + pltpu.roll(field, 1, 0) + pltpu.roll(field, length - 1, 0) - 4.0 * field

    def unpack(ref, start):
        fields = [
            ref[start + BLOCK * i : start + BLOCK * (i + 1), :].astype(jnp.float32)[:length]
            for i in range(3)
        ]
        rest = ref[start + 3 * BLOCK : start + pack, :].astype(jnp.float32)
        return fields + [column(rest[:1])], rest

    def activate(both):
        middle = both.shape[0] // 2
        hidden = jnp.tanh(both[:middle]).astype(jnp.bfloat16).astype(jnp.float32)
        tangent = (1.0 - hidden * hidden) * both[middle:]
        return jnp.concatenate([hidden, tangent]).astype(jnp.bfloat16)

    def networks(rows):
        stacked = jnp.concatenate([row[0] for row in rows] + [row[1] for row in rows])
        stacked = stacked.astype(jnp.bfloat16)
        one = activate(
            lax.dot_general(
                stacked,
                weights[0, :, :features],
                CONTRACT_LAST,
                preferred_element_type=jnp.float32,
            )
        )
        low = activate(jnp.dot(one, weights[0, :, features:], preferred_element_type=jnp.float32))
        high = activate(jnp.dot(one, weights[1, :, :depth], preferred_element_type=jnp.float32))
        out = jnp.dot(
            low, weights[1, :depth, depth:], preferred_element_type=jnp.float32
        ) + jnp.dot(high, weights[1, depth:, depth:], preferred_element_type=jnp.float32)
        saved = (one[:cells], jnp.concatenate([low[:cells], high[:cells]], axis=1), stacked[:cells])
        outs = [out[i * length : (i + 1) * length] for i in range(2 * len(rows))]
        return list(zip(outs[: len(rows)], outs[len(rows) :])), saved

    def exactly(left, ones, contract):
        total, ones = 0.0, ones.astype(jnp.bfloat16)
        for _ in range(3):
            term = left.astype(jnp.bfloat16)
            total = total + lax.dot_general(
                term, ones, contract, preferred_element_type=jnp.float32
            )
            left = left - term.astype(jnp.float32)
        return total

    def observed(final, columns, levels, values, precisions):
        count = columns.shape[1]
        cell_ids = lax.broadcasted_iota(jnp.int32, (length, count), 0).astype(jnp.float32)
        level_ids = lax.broadcasted_iota(jnp.int32, (features, count), 0).astype(jnp.float32)
        pick_cell = (cell_ids == columns).astype(jnp.float32)
        pick_level = (level_ids == levels).astype(jnp.float32)
        at_level = exactly(final, pick_level, (((1,), (0,)), ((), ())))
        modelled = jnp.sum(pick_cell * at_level, axis=0, keepdims=True)
        return exactly(pick_cell * (precisions * (modelled - values)), pick_level, CONTRACT_LAST)

    own = [ring_field(ref[0], other, i) for i, ref in enumerate((state, increment, diffusivity))]
    gate = column(ring_gating(mine[18:19, :cells], other[18:19, :cells])[:1])
    own.append(gate)
    beside, beside_rest = zip(unpack(near, 0), unpack(far, 0))
    second = [unpack(beyond, 0)[0], unpack(far, pack)[0]]
    third = [
        beyond[pack : pack + BLOCK].astype(jnp.float32)[:length],
        jnp.concatenate(
            [outer[...].astype(jnp.float32), jnp.zeros((length - cells, features), jnp.float32)]
        ),
    ]

    def advance(row, lats, moved):
        states, tangents, diffuse, gated = row
        return (
            states + diffuse * laplace(states, lats[0]) + gated * moved[0],
            tangents + diffuse * laplace(tangents, lats[1]) + gated * moved[1],
        )

    def advance_sum(row, middle, lat, moved):
        return middle + row[2] * laplace(middle, lat) + row[3] * (moved[0] + moved[1])

    groups = ((0,), (1, 2), (3, 4))
    all_rows = [own] + list(beside) + second
    moved = []
    first = None
    for group in groups:
        got, saved = networks([all_rows[i] for i in group])
        moved += got
        first = saved if first is None else first
    state_one, increment_one = advance(
        own, [beside[0][i] + beside[1][i] for i in range(2)], moved[0]
    )
    middle_one = state_one + increment_one
    beside_one, beside_middle, second_middle = [], [], []
    for i, (row, next_row, last) in enumerate(zip(beside, second, third)):
        one = advance(row, [own[j] + next_row[j] for j in range(2)], moved[1 + i])
        beside_one.append(one)
        beside_middle.append(one[0] + one[1])
        next_sum = next_row[0] + next_row[1]
        second_middle.append(advance_sum(next_row, next_sum, row[0] + row[1] + last, moved[3 + i]))
    all_rows = [(state_one, increment_one)] + beside_one
    late, moved = None, []
    for group in ((0,), (1, 2)):
        got, saved = networks([all_rows[i] for i in group])
        moved += got
        late = saved if late is None else late
    final = advance_sum(own, middle_one, beside_middle[0] + beside_middle[1], moved[0])
    count = observations
    columns = other[19:20, :count]
    columns = jnp.where(
        columns == 0.0, float(cells), jnp.where(columns == cells - 1.0, length - 1.0, -1.0)
    )
    columns = jnp.concatenate([mine[19:20, :count], columns], axis=1)
    chosen = [
        jnp.concatenate([mine[i : i + 1, :count], other[i : i + 1, :count]], axis=1)
        for i in (20, 21, 22)
    ]
    adjoint = observed(final, columns, *chosen)
    around = jnp.zeros_like(adjoint)
    for row, middle, next_middle, rest, moves in zip(
        beside, beside_middle, second_middle, beside_rest, moved[1:]
    ):
        total = advance_sum(row, middle, middle_one + next_middle, moves)
        around = around + row[2] * observed(
            total,
            rest[1:2, :cells],
            rest[2:3, :cells],
            rest[3:4, :cells] + rest[5:6, :cells],
            rest[4:5, :cells] + rest[6:7, :cells],
        )
    spreading = own[2] * adjoint
    adjoint_one = (adjoint + laplace(spreading, around))[:cells]
    gate = gate[:cells]
    source_late = (gate * adjoint[:cells]).astype(jnp.bfloat16)
    back_late = adjoint_layers(source_late, late[0], late[1], weights)
    adjoint_one = adjoint_one + jnp.dot(
        back_late, weights[0, :, :features], preferred_element_type=jnp.float32
    )
    spreading = own[2][:cells] * adjoint_one
    spreading_out[...] = spreading
    ends_out[...] = jnp.concatenate([spreading[:1], spreading[cells - 7 :]])
    source = (gate * adjoint_one).astype(jnp.bfloat16)
    back_one = adjoint_layers(source, first[0], first[1], weights)
    settled_out[...] = (
        adjoint_one
        - 4.0 * spreading
        + jnp.dot(back_one, weights[0, :, :features], preferred_element_type=jnp.float32)
    )
    first_core = core[0] == 0
    lefts = [jnp.concatenate([back_late, back_one]), jnp.concatenate([late[1], first[1]])]
    rights = [jnp.concatenate([late[2], first[2]]), jnp.concatenate([source_late, source])]
    halves, blocks, rows, width = kept.shape
    for out, which in ((given, 1), (kept, 0)):
        total = lax.dot_general(
            jnp.where(first_core, lefts[which], lefts[1 - which]),
            jnp.where(first_core, rights[which], rights[1 - which]),
            CONTRACT_FIRST,
            preferred_element_type=jnp.float32,
        ).astype(jnp.bfloat16)
        for half in range(halves):
            for block in range(blocks):
                out[half, block] = total[
                    block * rows : (block + 1) * rows, half * width : (half + 1) * width
                ]


def on_chip(kernel, outs, operands, flops, scratch=(), scalars=0, direct=0, fetched=0, place=None, room=32):
    size = sum(array.size * array.dtype.itemsize for array in list(operands) + list(outs))
    by_kernel = fetched > 0 or place is not None
    before = scalars + (direct if by_kernel else len(operands) - scalars)
    count = len(operands) - before
    places = [pltpu.SMEM] * scalars + [pltpu.VMEM] * (before - scalars) + [pl.ANY] * count
    body = kernel
    if by_kernel:
        copies = tuple(
            pltpu.VMEM(array.shape, array.dtype)
            for array in operands[before : before + fetched]
        )
        scratch = copies + (pltpu.SemaphoreType.DMA((count,)),) + tuple(scratch)

        def body(*refs):
            numbers, ready = refs[:scalars], refs[scalars:before]
            sources, refs = refs[before : before + count], refs[before + count :]
            results, refs = refs[: len(outs)], refs[len(outs) :]
            held, done, rest = refs[:fetched], refs[fetched], refs[fetched + 1 :]
            targets = list(held)
            if place is not None:
                targets += place(numbers, rest)
            moves = [
                pltpu.make_async_copy(source, target, done.at[i])
                for i, (source, target) in enumerate(zip(sources, targets))
            ]
            for move in moves:
                move.start()
            for move in moves:
                move.wait()
            kernel(*numbers, *ready, *held, *results, *rest)

    return pl.pallas_call(
        body,
        out_shape=outs,
        in_specs=[pl.BlockSpec(memory_space=place_) for place_ in places],
        out_specs=[pl.BlockSpec(memory_space=pltpu.VMEM)] * len(outs),
        scratch_shapes=scratch,
        compiler_params=pltpu.CompilerParams(vmem_limit_bytes=room * 1024 * 1024),
        cost_estimate=pl.CostEstimate(flops=flops, bytes_accessed=size, transcendentals=0),
    )(*operands)


def sum_and_spread_kernel(parts, copies):
    total = jnp.sum(parts[...].astype(jnp.float32), axis=0).astype(jnp.bfloat16)
    copies[...] = jnp.broadcast_to(total[None], copies.shape)


def sum_and_square_kernel(place, parts, copies, total):
    total[...] = jnp.sum(parts[...].astype(jnp.float32), axis=0)
    depth = copies.shape[1] // 2
    own = total[pl.ds(pl.multiple_of(place[0] * depth, depth), depth), :]
    squares = jnp.sum(total[...] * total[...], axis=0, keepdims=True)
    terms = []
    for _ in range(3):
        terms.append(squares.astype(jnp.bfloat16).astype(jnp.float32))
        squares = squares - terms[-1]
    rest = jnp.zeros((depth - len(terms), squares.shape[1]), jnp.float32)
    both = jnp.concatenate([own] + terms + [rest]).astype(jnp.bfloat16)
    copies[...] = jnp.broadcast_to(both[None], copies.shape)


def update_kernel(blocks, count, place, parts_ref, w_in, w_out, new_in, new_out):
    depth = parts_ref.shape[1] // 2
    shard = w_in.shape[0]
    parts = parts_ref[...].astype(jnp.float32)
    squares = jnp.sum(parts, axis=0)[depth:]
    square_sum = jnp.sum(jnp.sum(squares, axis=0, keepdims=True), axis=1, keepdims=True)
    scale = LEARN_RATE / jnp.sqrt(square_sum / count + EPSILON)
    for which, (old, new) in enumerate(((w_in, new_in), (w_out, new_out))):
        sides = []
        for half in range(2):
            rows = parts_ref[(half * blocks + place[0]) * 2 + which].astype(jnp.float32)[:depth]
            sides.append(jnp.where(place[1] == 0, rows[:shard], rows[shard:]))
        new[...] = old[...] - scale * jnp.concatenate(sides, axis=1)


def add_kernel(left, right, total):
    total[...] = (left[...].astype(jnp.float32) + right[...].astype(jnp.float32)).astype(
        jnp.bfloat16
    )


def updated(kept, given, w_in, w_out, soon, later):
    halves, blocks, rows, columns = kept.shape
    peers = halves * blocks
    (grads,) = on_chip(
        add_kernel,
        (jax.ShapeDtypeStruct((peers, rows, columns), jnp.bfloat16),),
        (kept.reshape(peers, rows, columns), swapped(given, "core").reshape(peers, rows, columns)),
        kept.size,
    )
    grads = lax.all_to_all(grads, AROUND[:-1], 0, 0)
    grads, soon = lax.optimization_barrier((grads, soon))
    for axis in ("z_lo", "z_hi"):
        count = lax.axis_size(axis)
        (copies,) = on_chip(
            sum_and_spread_kernel,
            (jax.ShapeDtypeStruct((count, rows, columns), jnp.bfloat16),),
            (grads,),
            grads.size,
        )
        grads = lax.all_to_all(copies, axis, 0, 0)
        if axis == "z_lo":
            grads, later = lax.optimization_barrier((grads, later))
    peers *= lax.axis_size("core")
    depth = rows // lax.axis_size(Z)
    (copies,) = on_chip(
        sum_and_square_kernel,
        (jax.ShapeDtypeStruct((peers, 2 * depth, columns), jnp.bfloat16),),
        (lax.axis_index(Z)[None], grads),
        grads.size,
        scratch=(pltpu.VMEM((rows, columns), jnp.float32),),
        scalars=1,
    )
    parts = lax.all_to_all(copies, AROUND, 0, 0)
    place = jnp.stack([lax.axis_index(("x_lo", "y")), lax.axis_index("core")])
    shape = jax.ShapeDtypeStruct(w_in.shape, jnp.float32)
    new_in, new_out = on_chip(
        functools.partial(update_kernel, blocks, float(peers * rows * columns)),
        (shape, shape),
        (place, parts, w_in, w_out),
        parts.size,
        scalars=1,
    )
    return new_in, new_out, soon, later


def local(
    state, increment, diffusivity, land_sea, w_in, w_mid, w_out, obs_col, obs_lev, obs_val, obs_prec
):
    _, cells, features = state.shape
    length = cells + 8
    observed = [numbers[None] for numbers in (obs_col, obs_lev, obs_val, obs_prec)]

    def outs(*shapes):
        return tuple(jax.ShapeDtypeStruct(shape, kind) for shape, kind in shapes)

    columns = 2 * features + w_mid.shape[1]
    width = columns // lax.axis_size("core")
    rows, mine, outer = on_chip(
        first_kernel,
        outs(
            ((w_in.shape[0], columns), jnp.bfloat16),
            ((24, features), jnp.float32),
            ((cells, features), jnp.bfloat16),
        ),
        (state, increment, diffusivity, land_sea, *observed, w_in, w_mid, w_out),
        0,
        fetched=11,
        room=56,
    )
    rows = lax.all_gather(rows, "core", axis=0, tiled=True)
    half = lax.dynamic_slice_in_dim(rows, lax.axis_index("core") * width, width, 1)
    fields = (state, increment, diffusivity)
    half, mine, outer, fields = lax.optimization_barrier((half, mine, outer, fields))
    half = spread(half, Z).reshape(-1, width)
    other = swapped(mine, "x_hi")
    outer = swapped_three_apart(outer)
    packed = outs(((3 * BLOCK + 16, features), jnp.bfloat16))
    (packs,) = on_chip(pack_fields_kernel, packed, fields, 0, fetched=3)
    (own,) = on_chip(pack_edges_kernel, packed, (packs, mine, other), 0)
    near = swapped(own, "core")
    far = swapped_between_chips(jnp.concatenate([own, near]))
    half, near = lax.optimization_barrier((half, near))
    half = spread_across_x(half).reshape(-1, width)
    far, outer = lax.optimization_barrier((far, outer))
    pack = 3 * BLOCK + 16
    (beyond,) = on_chip(
        behind_kernel, outs(((pack + BLOCK, features), jnp.bfloat16)), (far,), 10**10
    )
    beyond = swapped(beyond, "core")
    half, far, beyond = lax.optimization_barrier((half, far, beyond))
    hidden_units = half.shape[0]
    blocks = lax.axis_size(("x_lo", "y"))
    halves = lax.axis_size("x_hi")
    part = ((halves, blocks, hidden_units // blocks, features // halves), jnp.bfloat16)
    narrow = ((cells, features), jnp.float32)
    settled, spreading, ends, kept, given = on_chip(
        functools.partial(whole_kernel, obs_col.shape[0]),
        outs(
            narrow,
            narrow,
            ((8, features), jnp.float32),
            part,
            part,
        ),
        (lax.axis_index("core")[None], state, increment, diffusivity, mine, other, near, far, beyond, outer)
        + (half, swapped(half, "core")),
        40 * cells * hidden_units * (2 * features + hidden_units),
        scratch=(pltpu.VMEM((2, hidden_units, width), jnp.bfloat16),),
        scalars=1,
        direct=9,
        fetched=0,
        place=lambda numbers, rest: [
            rest[0].at[numbers[0][0]],
            rest[0].at[1 - numbers[0][0]],
        ],
    )
    w_in_new, w_out_new, ends, spreading = updated(
        kept, given, w_in, w_out, ends, spreading
    )
    ends = swapped(ends, "x_hi")
    far = swapped_between_chips(spreading)
    near = swapped(spreading, "core")
    east = jnp.concatenate([spreading[1:], ends[:1]])
    west = jnp.concatenate([ends[-1:], spreading[:-1]])
    adjoint = settled + (far + near + east + west)
    return adjoint[None], w_in_new, w_out_new


def solution(mesh):
    fine = Mesh(mesh.devices.reshape(FINE_SIZES), FINE_AXES)
    everywhere = TILE + ("x_hi",)
    return jax.shard_map(
        local,
        mesh=fine,
        in_specs=(
            P(TILE, "x_hi", None),
            P(TILE, "x_hi", None),
            P(TILE, "x_hi", None),
            P(TILE, "x_hi"),
            P(TILE, None),
            P(TILE, None),
            P(TILE, None),
            P(everywhere),
            P(everywhere),
            P(everywhere),
            P(everywhere),
        ),
        out_specs=(P(TILE, "x_hi", None), P(TILE, None), P(TILE, None)),
        check_vma=False,
    )
```
